32 devices in a mesh: dp: 2 (over y), context: 2 (over x), experts: 8 (over z, core).
Axes of the slice: x: 2, y: 2, z: 4, core: 2. Of those that a mesh axis runs over, the one named last changes fastest.
Arguments:
- hidden_in: bfloat16 [2, 4096, 2048], P('dp', ('context', 'experts')), may hold values from -6 to 6
- segments: int32 [2, 4096], P('dp'), may hold values from 0 to 3, as said below
- expert_ids: int32 [2, 4096, 8], P('dp', ('context', 'experts')), may hold values from 0 to 15, all different within a row
- placement_order: int32 [2, 16, 2048], P('dp', ('context', 'experts')), may hold values from 0 to 2047, each once within a row
- out_grad: bfloat16 [2, 4096, 2048], P('dp', ('context', 'experts')), may hold values from -6 to 6
- attention_gain: float32 [2048], replicated, may hold values from 0.5 to 1.5
- query_weight: bfloat16 [2048, 4096], replicated, may hold values from -0.125 to 0.125
- key_matrix: bfloat16 [2048, 512], replicated, may hold values from -0.125 to 0.125
- value_matrix: bfloat16 [2048, 512], replicated, may hold values from -0.125 to 0.125
- query_gain: float32 [128], replicated, may hold values from 0.5 to 1.5
- key_gain: float32 [128], replicated, may hold values from 0.5 to 1.5
- out_weight: bfloat16 [4096, 2048], replicated, may hold values from -0.75 to 0.75
- feedforward_gain: float32 [2048], replicated, may hold values from 0.5 to 1.5
- router_weight: bfloat16 [2048, 16], replicated, may hold values from -0.0625 to 0.0625
- gate_weight: bfloat16 [16, 2048, 768], P('experts', ('dp', 'context')), may hold values from -0.125 to 0.125
- up_weight: bfloat16 [16, 2048, 768], P('experts', ('dp', 'context')), may hold values from -0.125 to 0.125
- down_weight: bfloat16 [16, 768, 2048], P('experts', None, ('dp', 'context')), may hold values from -0.875 to 0.875
Outputs:
- block_out: bfloat16 [2, 4096, 2048], P('dp', ('context', 'experts'))
- input_grad: float32 [2, 4096, 2048], P('dp', ('context', 'experts'))
- attention_gain_grad: float32 [2048], P(('dp', 'context', 'experts'))
- query_weight_grad: float32 [2048, 4096], P(('dp', 'context', 'experts'))
- key_weight_grad: float32 [2048, 512], P(('dp', 'context', 'experts'))
- value_weight_grad: float32 [2048, 512], P(('dp', 'context', 'experts'))
- query_gain_grad: float32 [128], P(('dp', 'context', 'experts'))
- key_gain_grad: float32 [128], P(('dp', 'context', 'experts'))
- out_weight_grad: float32 [4096, 2048], P(('dp', 'context', 'experts'))
- feedforward_gain_grad: float32 [2048], P(('dp', 'context', 'experts'))
- router_weight_grad: float32 [2048, 16], P(('dp', 'context', 'experts'))
- gate_weight_grad: float32 [16, 2048, 768], P('experts', ('dp', 'context'))
- up_weight_grad: float32 [16, 2048, 768], P('experts', ('dp', 'context'))
- down_weight_grad: float32 [16, 768, 2048], P('experts', None, ('dp', 'context'))
The draws below stay inside these ranges and needn't reach their ends.
Inputs may be any that keep to these rules, and one draw needn't show every extreme that they name: `segments`: each row starts at document 0 and rises by one at each of three document starts; document 1 begins within the first 256 positions and ends within the last 256. `placement_order`: each row lists every pair number of its block once. `expert_ids`: A token's 8 experts differ.
All inputs are finite; a program needn't handle non-finite values.
Results may differ from the reference program's by a relative error of at most 0.019.
Values may be sent and summed in bfloat16 or wider, within the bound.
No kernel may reach another device: no remote copies, remote signals or barrier semaphores. Data moves between devices by JAX's collectives and lax.ppermute only.
A program may use at most 320 MiB of HBM per device.

```python
import math
import jax
import jax.numpy as jnp
from jax import lax

MODEL_DIM = 2048
HQ = 32
KEY_HEADS = 4
HEAD_SIZE = 128
FF = 768
TOP = 8
WINDOW = 1024
TOKENS_PER_SHARD = 256
SEQS = 2
SEQUENCE_LENGTH = 4096
EXPERTS = 16
QUERY_PER_KEY = 8
PAIRS = 2048
CAP = 128
WINDOW_BLOCKS = 4
N_CONTEXT = 2
N_EXPERTS = 8


def draw_segments(key, part):
    key = jax.random.fold_in(key, 7)
    row_keys = jax.random.split(key, SEQS)

    def one_row(row_key):
        first_key, second_key, third_key = jax.random.split(row_key, 3)
        start_pos = jax.random.randint(first_key, (), 1, TOKENS_PER_SHARD)
        finish_pos = jax.random.randint(second_key, (), SEQUENCE_LENGTH - TOKENS_PER_SHARD + 1, SEQUENCE_LENGTH - 1)
        middle_pos = jax.random.randint(third_key, (), finish_pos + 1, SEQUENCE_LENGTH)
        places = jnp.arange(SEQUENCE_LENGTH, dtype=jnp.int32)
        return (places >= start_pos).astype(jnp.int32) + (places >= finish_pos).astype(jnp.int32) + (places >= middle_pos).astype(jnp.int32)
    return jax.vmap(one_row)(row_keys)


def level_of(rng, shape, cuts, least, high):
    loudness = 1.0
    for dim, parts in cuts:
        heights = jax.random.uniform(jax.random.fold_in(jax.random.fold_in(rng, 6), dim), (parts,), jnp.float32, least / len(cuts), high / len(cuts))
        loudness = loudness * jnp.repeat(jnp.exp(heights), shape[dim] // parts).reshape((-1,) + (1,) * (len(shape) - 1 - dim))
    return loudness


def distinct(own_key, rows, number_of, top, lift):
    ranking = jax.random.permutation(jax.random.fold_in(own_key, 1), number_of)
    favour = ranking
    for power in range(3):
        favour = favour * favour // number_of
    favour = favour * lift // number_of
    lots = jax.random.randint(jax.random.fold_in(own_key, 2), (rows, number_of), 0, 4096) + favour
    holders = jax.random.permutation(jax.random.fold_in(own_key, 3), rows)[jnp.arange(number_of) % rows]
    lots = jnp.where(jnp.arange(rows)[:, None] == holders[None, :], 1 << 14, lots)
    priority = lots * number_of + jnp.arange(number_of)
    return lax.top_k(priority.astype(jnp.int32), top)[1].astype(jnp.int32)


def gaussian(own_key, dims, width, bound, pieces=(), kind=jnp.bfloat16):
    drawn = width * jax.random.normal(own_key, dims, jnp.float32)
    if pieces:
        drawn = drawn * level_of(own_key, dims, pieces, -0.22, 0.18)
    return jnp.clip(drawn, -bound, bound).astype(kind)


def setup_inputs(seed: int = 0) -> dict:
    streams_of = jax.random.split(jax.random.key(seed), 18)
    hidden_in = gaussian(streams_of[0], (SEQS, SEQUENCE_LENGTH, MODEL_DIM), 1.0, 6.0, ((0, 2), (1, 16)))
    segments = draw_segments(jax.random.fold_in(streams_of[17], 71), 0)
    expert_ids = distinct(streams_of[2], SEQS * SEQUENCE_LENGTH, EXPERTS, TOP, 4096).reshape((SEQS, SEQUENCE_LENGTH, TOP))
    placement_order = jax.vmap(lambda own: jax.random.permutation(own, PAIRS))(jax.random.split(streams_of[3], SEQS * (N_CONTEXT * N_EXPERTS))).reshape((SEQS, N_CONTEXT * N_EXPERTS, PAIRS)).astype(jnp.int32)
    out_grad = gaussian(streams_of[4], (SEQS, SEQUENCE_LENGTH, MODEL_DIM), 1.0, 6.0, ((0, 2), (1, 16)))
    attention_gain = jnp.clip(1.0 + 0.1 * jax.random.normal(streams_of[5], (MODEL_DIM,), jnp.float32), 0.5, 1.5)
    query_weight = gaussian(streams_of[6], (MODEL_DIM, HQ * HEAD_SIZE), MODEL_DIM ** -0.5, 0.125)
    key_matrix = gaussian(streams_of[7], (MODEL_DIM, KEY_HEADS * HEAD_SIZE), MODEL_DIM ** -0.5, 0.125)
    value_matrix = gaussian(streams_of[8], (MODEL_DIM, KEY_HEADS * HEAD_SIZE), MODEL_DIM ** -0.5, 0.125)
    query_gain = jnp.clip(1.0 + 0.1 * jax.random.normal(streams_of[9], (HEAD_SIZE,), jnp.float32), 0.5, 1.5)
    key_gain = jnp.clip(1.0 + 0.1 * jax.random.normal(streams_of[10], (HEAD_SIZE,), jnp.float32), 0.5, 1.5)
    out_weight = gaussian(streams_of[11], (HQ * HEAD_SIZE, MODEL_DIM), (HQ * HEAD_SIZE // 64) ** -0.5, 0.75)
    feedforward_gain = jnp.clip(1.0 + 0.1 * jax.random.normal(streams_of[12], (MODEL_DIM,), jnp.float32), 0.5, 1.5)
    router_weight = gaussian(streams_of[13], (MODEL_DIM, EXPERTS), (4 * MODEL_DIM) ** -0.5, 0.0625)
    gate_weight = gaussian(streams_of[14], (EXPERTS, MODEL_DIM, FF), MODEL_DIM ** -0.5, 0.125, ((0, 8), (1, 4)))
    up_weight = gaussian(streams_of[15], (EXPERTS, MODEL_DIM, FF), MODEL_DIM ** -0.5, 0.125, ((0, 8), (1, 4)))
    down_weight = gaussian(streams_of[16], (EXPERTS, FF, MODEL_DIM), (FF // 16) ** -0.5, 0.875, ((0, 8), (2, 4)))
    return {"hidden_in": hidden_in, "segments": segments, "expert_ids": expert_ids, "placement_order": placement_order, "out_grad": out_grad, "attention_gain": attention_gain, "query_weight": query_weight, "key_matrix": key_matrix, "value_matrix": value_matrix, "query_gain": query_gain, "key_gain": key_gain, "out_weight": out_weight, "feedforward_gain": feedforward_gain, "router_weight": router_weight, "gate_weight": gate_weight, "up_weight": up_weight, "down_weight": down_weight}


norm_eps = 1e-06
rope_base = 1000000.0
masked_score = -1e+30
upper_bound = lax.Precision.HIGHEST

@jax.custom_vjp
def lower_bound(v):
    return lax.optimization_barrier(v.astype(jnp.bfloat16)).astype(jnp.float32)

@jax.custom_vjp
def lower_bound_back(v):
    return v

def low_keep(v):
    return (lower_bound(v), None)

def low_pass(kept, grad):
    return (grad,)

def back_keep(v):
    return (v, None)

def back_low(kept, grad):
    return (lower_bound(grad),)
lower_bound.defvjp(low_keep, low_pass)
lower_bound_back.defvjp(back_keep, back_low)

def rms_scale(values, norm_gain):
    return values * lax.rsqrt(lax.optimization_barrier(jnp.mean(values * values, axis=-1, keepdims=True)) + norm_eps) * norm_gain

def rope_tables(positions, head_width):
    frequencies = jnp.power(rope_base, -jnp.arange(0, head_width, 2).astype(jnp.float32) / head_width)
    angles = positions.astype(jnp.float32)[:, None] * frequencies[None, :]
    return (jnp.cos(angles), jnp.sin(angles))

def rotate(values, cosine, sine_table):
    half_dim = values.shape[-1] // 2
    first_half = values[..., :half_dim]
    second_half = values[..., half_dim:]
    cos_rows = cosine[:, None, :]
    sin_rows = sine_table[:, None, :]
    return jnp.concatenate([first_half * cos_rows - second_half * sin_rows, second_half * cos_rows + first_half * sin_rows], axis=-1)

def attention(query_rows, key_matrix_rows, value_matrix_rows, seg_row):
    window_rows = (WINDOW_BLOCKS + 1) * TOKENS_PER_SHARD
    padded_keys = jnp.concatenate([jnp.zeros((WINDOW_BLOCKS * TOKENS_PER_SHARD, KEY_HEADS, HEAD_SIZE), jnp.float32), key_matrix_rows], 0)
    padded_values = jnp.concatenate([jnp.zeros((WINDOW_BLOCKS * TOKENS_PER_SHARD, KEY_HEADS, HEAD_SIZE), jnp.float32), value_matrix_rows], 0)
    pad_segs = jnp.concatenate([jnp.full((WINDOW_BLOCKS * TOKENS_PER_SHARD,), -1, jnp.int32), seg_row], 0)
    score_scale = 1.0 / math.sqrt(HEAD_SIZE)
    gaps = (WINDOW_BLOCKS * TOKENS_PER_SHARD + jnp.arange(TOKENS_PER_SHARD, dtype=jnp.int32))[:, None] - jnp.arange(window_rows, dtype=jnp.int32)[None, :]

    def one_block(block_index):
        first_row_index = (block_index * TOKENS_PER_SHARD).astype(jnp.int32)
        block_of_queries = lax.dynamic_slice_in_dim(query_rows, first_row_index, TOKENS_PER_SHARD, 0).reshape(TOKENS_PER_SHARD, KEY_HEADS, QUERY_PER_KEY, HEAD_SIZE)
        key_block = lax.dynamic_slice_in_dim(padded_keys, first_row_index, window_rows, 0)
        value_block = lax.dynamic_slice_in_dim(padded_values, first_row_index, window_rows, 0)
        key_segs = lax.dynamic_slice_in_dim(pad_segs, first_row_index, window_rows, 0)
        query_segs = lax.dynamic_slice_in_dim(seg_row, first_row_index, TOKENS_PER_SHARD, 0)
        allowed = (query_segs[:, None] == key_segs[None, :]) & (gaps >= 0) & (gaps < WINDOW)
        scores = jnp.einsum('tngd,snd->ngts', block_of_queries, key_block, precision=upper_bound) * score_scale
        scores = lower_bound_back(scores)
        scores = jnp.where(allowed[None, None], scores, masked_score)
        row_top = lax.optimization_barrier(jnp.max(scores, axis=-1, keepdims=True))
        exp_scores = jnp.exp(scores - row_top)
        probabilities = lower_bound(exp_scores / lax.optimization_barrier(jnp.sum(exp_scores, axis=-1, keepdims=True)))
        head_mix = jnp.einsum('ngts,snd->tngd', probabilities, value_block, precision=upper_bound)
        return head_mix.reshape(TOKENS_PER_SHARD, HQ * HEAD_SIZE)
    blocks_out = lax.map(jax.checkpoint(one_block), jnp.arange(SEQUENCE_LENGTH // TOKENS_PER_SHARD, dtype=jnp.int32))
    return blocks_out.reshape(SEQUENCE_LENGTH, HQ * HEAD_SIZE)

def pick_rows(block_rows, row_index):
    return block_rows[row_index]

def fill_block(send_block, target_block):
    return jnp.zeros((EXPERTS * CAP + 1, MODEL_DIM), jnp.float32).at[target_block].add(send_block)[:-1]

def collect_block(back_block, target_block, kept_block, order_block):
    slot_index = jnp.where(kept_block, target_block, 0)
    seq_vals = jnp.where(kept_block[:, None], back_block[slot_index], 0.0)
    return jnp.zeros((PAIRS, MODEL_DIM), jnp.float32).at[order_block].set(seq_vals)

def experts_part(ffn_in, route_row, order_rows, router_weight, gate_weight, up_weight, down_weight):
    blocks_all = SEQUENCE_LENGTH // TOKENS_PER_SHARD
    logits = lower_bound_back(jnp.dot(ffn_in, router_weight, precision=upper_bound))
    choice_hits = route_row[:, :, None] == jnp.arange(EXPERTS, dtype=jnp.int32)[None, None, :]
    chosen = lax.optimization_barrier(jnp.sum(jnp.where(choice_hits, logits[:, None, :], 0.0), axis=-1))
    gate_probs = jax.nn.softmax(chosen, axis=-1)
    flat_ids = route_row.reshape(blocks_all, PAIRS)
    seq_ids = jnp.take_along_axis(flat_ids, order_rows, 1)
    slot_hits = (seq_ids[:, :, None] == jnp.arange(EXPERTS, dtype=jnp.int32)[None, None, :]).astype(jnp.int32)
    slot_rank = lax.optimization_barrier(jnp.sum((jnp.cumsum(slot_hits, axis=1) - slot_hits) * slot_hits, axis=-1))
    kept_pairs = slot_rank < CAP
    target = jnp.where(kept_pairs, seq_ids * CAP + slot_rank, EXPERTS * CAP)
    rows_in = ffn_in.reshape(blocks_all, TOKENS_PER_SHARD, MODEL_DIM)
    send_rows = jax.vmap(pick_rows)(rows_in, order_rows // TOP)
    outbound = lower_bound_back(jax.vmap(fill_block)(send_rows, target))
    expert_rows = outbound.reshape(blocks_all, EXPERTS, CAP, MODEL_DIM).transpose(1, 0, 2, 3).reshape(EXPERTS, blocks_all * CAP, MODEL_DIM)
    gate_pre = lower_bound_back(jnp.einsum('erd,edf->erf', expert_rows, gate_weight, precision=upper_bound))
    up_pre = lower_bound_back(jnp.einsum('erd,edf->erf', expert_rows, up_weight, precision=upper_bound))
    hidden_units = lower_bound(jax.nn.silu(gate_pre) * up_pre)
    expert_out = lower_bound(lower_bound_back(jnp.einsum('erf,efd->erd', hidden_units, down_weight, precision=upper_bound)))
    returned = expert_out.reshape(EXPERTS, blocks_all, CAP, MODEL_DIM).transpose(1, 0, 2, 3).reshape(blocks_all, EXPERTS * CAP, MODEL_DIM)
    pair_vals = jax.vmap(collect_block)(returned, target, kept_pairs, order_rows).reshape(SEQUENCE_LENGTH, TOP, MODEL_DIM)
    return jnp.einsum('tk,tkd->td', gate_probs, pair_vals, precision=upper_bound)

def layer(hidden, seg_row, route_row, order_rows, weight_set):
    attention_gain, query_weight, key_matrix, value_matrix, query_gain, key_gain, out_weight, feedforward_gain, router_weight, gate_weight, up_weight, down_weight = weight_set
    attention_input = lower_bound(rms_scale(hidden, attention_gain))
    query_pre = lower_bound_back(jnp.dot(attention_input, query_weight, precision=upper_bound)).reshape(SEQUENCE_LENGTH, HQ, HEAD_SIZE)
    key_before_norm = lower_bound_back(jnp.dot(attention_input, key_matrix, precision=upper_bound)).reshape(SEQUENCE_LENGTH, KEY_HEADS, HEAD_SIZE)
    value_matrix_rows = lower_bound(lower_bound_back(jnp.dot(attention_input, value_matrix, precision=upper_bound))).reshape(SEQUENCE_LENGTH, KEY_HEADS, HEAD_SIZE)
    cosine, sine_table = rope_tables(jnp.arange(SEQUENCE_LENGTH, dtype=jnp.int32), HEAD_SIZE)
    query_rows = lower_bound(rotate(rms_scale(query_pre, query_gain), cosine, sine_table))
    key_matrix_rows = lower_bound(rotate(rms_scale(key_before_norm, key_gain), cosine, sine_table))
    attn_mix = lower_bound(lower_bound_back(attention(query_rows, key_matrix_rows, value_matrix_rows, seg_row)))
    middle = hidden + lower_bound_back(jnp.dot(attn_mix, out_weight, precision=upper_bound))
    ffn_in = lower_bound(rms_scale(middle, feedforward_gain))
    return middle + experts_part(ffn_in, route_row, order_rows, router_weight, gate_weight, up_weight, down_weight)

def reference(hidden_in, segments, expert_ids, placement_order, out_grad, attention_gain, query_weight, key_matrix, value_matrix, query_gain, key_gain, out_weight, feedforward_gain, router_weight, gate_weight, up_weight, down_weight):
    weight_set = (attention_gain, query_weight.astype(jnp.float32), key_matrix.astype(jnp.float32), value_matrix.astype(jnp.float32), query_gain, key_gain, out_weight.astype(jnp.float32), feedforward_gain, router_weight.astype(jnp.float32), gate_weight.astype(jnp.float32), up_weight.astype(jnp.float32), down_weight.astype(jnp.float32))

    def one_sequence(totals, seq_items):
        hidden_row, seg_row, route_row, order_rows, cot_row = seq_items

        def forward(hidden, weights_now):
            return layer(hidden, seg_row, route_row, order_rows, weights_now)
        result, pull = jax.vjp(forward, hidden_row.astype(jnp.float32), weight_set)
        row_grad, weight_grads = pull(cot_row.astype(jnp.float32))
        totals = jax.tree.map(jnp.add, totals, weight_grads)
        return (totals, (result.astype(jnp.bfloat16), row_grad))
    zeros_init = jax.tree.map(jnp.zeros_like, weight_set)
    totals, (block_out, input_grad) = lax.scan(one_sequence, zeros_init, (hidden_in, segments, expert_ids, placement_order, out_grad))
    return (block_out, input_grad, totals[0], totals[1], totals[2], totals[3], totals[4], totals[5], totals[6], totals[7], totals[8], totals[9], totals[10], totals[11])
```

```python
import functools, math
import jax, jax.numpy as jnp
from jax import lax
import jax.experimental.pallas as pl
import jax.experimental.pallas.tpu as pltpu
from jax.sharding import PartitionSpec as P

f32=jnp.float32; bf16=jnp.bfloat16
WINDOW=1024
norm_eps=1e-6
masked_score=-1e30
VMEM_BYTES=56*1024*1024
NT=(((1,),(1,)),((),()))
NN=(((1,),(0,)),((),()))

def params(steps=1):
    return pltpu.CompilerParams(dimension_semantics=("arbitrary",)*steps, vmem_limit_bytes=VMEM_BYTES)

def mm(a,b,dims=NN):
    return lax.dot_general(a,b,dims,preferred_element_type=f32)

def heads_kernel(x_ref, w_ref, gain_ref, cos_ref, sin_ref, pre_ref, out_ref):
    head=gain_ref.shape[1]
    pre=mm(x_ref[...], w_ref[...])
    pre_ref[...]=pre
    gain=gain_ref[...]; cos=cos_ref[...]; sin=sin_ref[...]
    for j in range(pre.shape[1]//head):
        u=pre[:, j*head:(j+1)*head]
        n=u*lax.rsqrt(jnp.mean(u*u,-1,keepdims=True)+norm_eps)*gain
        out_ref[:, j*head:(j+1)*head]=(n*cos+pltpu.roll(n,head//2,1)*sin).astype(bf16)

def project_heads(x, w, gain, cos, sin, tile=512):
    rows,depth=x.shape; cols=w.shape[1]; head=gain.shape[0]
    tile=min(tile,cols)
    whole=lambda shape: pl.BlockSpec(shape, lambda i:(0,0))
    return pl.pallas_call(heads_kernel,
        out_shape=(jax.ShapeDtypeStruct((rows,cols),f32),jax.ShapeDtypeStruct((rows,cols),bf16)),
        grid=(cols//tile,),
        in_specs=[whole((rows,depth)),pl.BlockSpec((depth,tile),lambda i:(0,i)),whole((1,head)),whole((rows,head)),whole((rows,head))],
        out_specs=(pl.BlockSpec((rows,tile),lambda i:(0,i)),)*2,
        compiler_params=params(), name="project_heads",
        cost_estimate=pl.CostEstimate(flops=2*rows*depth*cols,bytes_accessed=2*depth*cols+8*rows*cols,transcendentals=0),
    )(x,w,gain[None],cos,sin)

def attend_kernel(scale, blocks, *refs):
    q_ref=refs[0]; k_refs=refs[1:1+blocks]; v_refs=refs[1+blocks:1+2*blocks]
    qseg_ref,kseg_ref,out_ref,inv_ref,bias_ref,vaug_ref=refs[1+2*blocks:]
    rows,head=k_refs[0].shape
    @pl.when(pl.program_id(0)==0)
    def _():
        vaug_ref[...]=jnp.ones_like(vaug_ref)
        lead=lax.broadcasted_iota(jnp.int32,(rows,rows),0)-lax.broadcasted_iota(jnp.int32,(rows,rows),1)
        for b in range(blocks):
            gap=lead+b*rows
            ok=(qseg_ref[...]==kseg_ref[b:b+1,:])&(gap>=0)&(gap<WINDOW)
            bias_ref[b]=jnp.where(ok,0.0,masked_score)
    for b in range(blocks):
        vaug_ref[b,:,:head]=v_refs[b][...]
    lane=lax.broadcasted_iota(jnp.int32,(rows,head),1)
    inv_all=jnp.zeros((rows,head),f32)
    for j in range(q_ref.shape[1]//head):
        q=q_ref[:, j*head:(j+1)*head]
        acc=jnp.zeros((rows,2*head),f32)
        for b in range(blocks):
            s=mm(q,k_refs[b][...],NT)
            p=jnp.exp2(s*scale+bias_ref[b]).astype(bf16)
            acc+=mm(p,vaug_ref[b])
        inv=1.0/acc[:,head:]
        out_ref[:, j*head:(j+1)*head]=(acc[:,:head]*inv).astype(bf16)
        inv_all=jnp.where(lane==j,inv,inv_all)
    inv_ref[...]=inv_all

def attend(q, kvs, qseg, ksegs, kv_heads, head):
    rows,cols=q.shape; blocks=len(kvs); group=cols//kv_heads
    scale=math.log2(math.e)/math.sqrt(head)
    return pl.pallas_call(functools.partial(attend_kernel,scale,blocks),
        out_shape=(jax.ShapeDtypeStruct((rows,cols),bf16),jax.ShapeDtypeStruct((rows,kv_heads*head),f32)),
        grid=(kv_heads,),
        in_specs=[pl.BlockSpec((rows,group),lambda g:(0,g))]
          +[pl.BlockSpec((rows,head),lambda g:(0,g))]*blocks+[pl.BlockSpec((rows,head),lambda g:(0,kv_heads+g))]*blocks
          +[pl.BlockSpec((rows,1),lambda g:(0,0)),pl.BlockSpec((blocks,rows),lambda g:(0,0))],
        out_specs=(pl.BlockSpec((rows,group),lambda g:(0,g)),pl.BlockSpec((rows,head),lambda g:(0,g))),
        scratch_shapes=[pltpu.VMEM((blocks,rows,rows),f32),pltpu.VMEM((blocks,rows,2*head),bf16)],
        compiler_params=params(), name="attend",
        cost_estimate=pl.CostEstimate(flops=6*rows*cols*rows*blocks,bytes_accessed=8*rows*cols,transcendentals=0),
    )(q,*kvs,*kvs,qseg[:,None],ksegs)

def attend_back_kernel(scale, blocks, *refs):
    q_ref=refs[0]; k_refs=refs[1:1+blocks]; v_refs=refs[1+blocks:1+2*blocks]
    (qseg_ref,kseg_ref,grad_ref,mix_ref,inv_ref,pre_ref,gain_ref,cos_ref,sin_ref,
     dpre_ref,dgain_ref,dk_ref,dv_ref,bias_ref,vaug_ref)=refs[1+2*blocks:]
    rows,head=k_refs[0].shape
    soft=scale*math.log(2.0)
    @pl.when(pl.program_id(0)==0)
    def _():
        vaug_ref[...]=jnp.ones_like(vaug_ref)
        lead=lax.broadcasted_iota(jnp.int32,(rows,rows),1)-lax.broadcasted_iota(jnp.int32,(rows,rows),0)
        for b in range(blocks):
            gap=lead+b*rows
            ok=(kseg_ref[:,b:b+1]==qseg_ref[...])&(gap>=0)&(gap<WINDOW)
            bias_ref[b]=jnp.where(ok,0.0,masked_score)
        dgain_ref[...]=jnp.zeros_like(dgain_ref)
    k_turned=[]
    for b in range(blocks):
        vaug_ref[b,:,:head]=v_refs[b][...]
        k_turned.append(k_refs[b][...].T)
    lane=lax.broadcasted_iota(jnp.int32,(rows,head),1)
    gain=gain_ref[...]; cos=cos_ref[...]; sin=sin_ref[...]
    dk_ref[...]=jnp.zeros_like(dk_ref); dv_ref[...]=jnp.zeros_like(dv_ref)
    for j in range(q_ref.shape[1]//head):
        cols=slice(j*head,(j+1)*head)
        q=q_ref[:,cols]
        inv=inv_ref[:,j:j+1]
        grad=grad_ref[:,cols].astype(f32)*inv
        delta=-jnp.sum(grad*mix_ref[:,cols].astype(f32),-1,keepdims=True)
        hi=delta.astype(bf16).astype(f32)
        tail=jnp.where(lane==0,hi,jnp.where(lane==1,delta-hi,0.0)).astype(bf16)
        low=grad.astype(bf16)
        both=jnp.concatenate([low,tail],axis=1)
        turned=jnp.zeros((head,rows),f32)
        for b in range(blocks):
            s=mm(k_refs[b][...],q,NT)
            p=jnp.exp2(s*scale+bias_ref[b])
            d=mm(vaug_ref[b],both,NT)
            ds=(p*d).astype(bf16)
            dk_ref[b]+=mm(ds,q)
            dv_ref[b]+=mm(p.astype(bf16),low)
            turned+=mm(k_turned[b],ds)
        g=turned.T*soft
        g=g*cos+pltpu.roll(g*sin,head//2,1)
        u=pre_ref[:,cols]
        r=lax.rsqrt(jnp.mean(u*u,-1,keepdims=True)+norm_eps)
        n=u*r
        dgain_ref[...]+=jnp.sum(g*n,0,keepdims=True)
        g=g*gain
        dpre_ref[:,cols]=(r*(g-n*jnp.mean(g*n,-1,keepdims=True))).astype(bf16)
    dk_ref[...]*=soft

def attend_back(q, kvs, qseg, ksegs, grad, mix, inv, pre, gain, cos, sin, kv_heads, head, first=0, count=None):
    rows,cols=q.shape; blocks=len(kvs); group=cols//kv_heads
    count=count or kv_heads
    scale=math.log2(math.e)/math.sqrt(head)
    wide=lambda: pl.BlockSpec((rows,group),lambda g:(0,first+g))
    part=lambda: pl.BlockSpec((rows,head),lambda g:(0,first+g))
    whole=lambda *shape: pl.BlockSpec(shape,lambda g:(0,)*len(shape))
    return pl.pallas_call(functools.partial(attend_back_kernel,scale,blocks),
        out_shape=(jax.ShapeDtypeStruct((rows,count*group),bf16),jax.ShapeDtypeStruct((1,head),f32),
                   jax.ShapeDtypeStruct((blocks,rows,count*head),f32),jax.ShapeDtypeStruct((blocks,rows,count*head),f32)),
        grid=(count,),
        in_specs=[wide()]+[part()]*blocks+[pl.BlockSpec((rows,head),lambda g:(0,kv_heads+first+g))]*blocks
          +[whole(1,rows),whole(rows,blocks),wide(),wide(),part(),wide(),whole(1,head),whole(rows,head),whole(rows,head)],
        out_specs=(pl.BlockSpec((rows,group),lambda g:(0,g)),whole(1,head),pl.BlockSpec((blocks,rows,head),lambda g:(0,0,g)),pl.BlockSpec((blocks,rows,head),lambda g:(0,0,g))),
        scratch_shapes=[pltpu.VMEM((blocks,rows,rows),f32),pltpu.VMEM((blocks,rows,2*head),bf16)],
        compiler_params=params(), name="attend_back",
        cost_estimate=pl.CostEstimate(flops=14*rows*count*group*rows*blocks,bytes_accessed=16*rows*cols,transcendentals=0),
    )(q,*kvs,*kvs,qseg[None],ksegs.T,grad,mix,inv,pre,gain[None],cos,sin)

def heads_back_kernel(grad_ref, pre_ref, gain_ref, cos_ref, sin_ref, dpre_ref, dgain_ref):
    head=gain_ref.shape[1]
    total=jnp.zeros((1,head),f32)
    for j in range(pre_ref.shape[1]//head):
        cols=slice(j*head,(j+1)*head)
        g=grad_ref[:,cols]
        g=g*cos_ref[...]+pltpu.roll(g*sin_ref[...],head//2,1)
        u=pre_ref[:,cols]
        r=lax.rsqrt(jnp.mean(u*u,-1,keepdims=True)+norm_eps)
        n=u*r
        total+=jnp.sum(g*n,0,keepdims=True)
        g=g*gain_ref[...]
        dpre_ref[:,cols]=(r*(g-n*jnp.mean(g*n,-1,keepdims=True))).astype(bf16)
    dgain_ref[...]=total

def heads_back(grad, pre, gain, cos, sin):
    rows,cols=grad.shape; head=gain.shape[0]
    return pl.pallas_call(heads_back_kernel,
        out_shape=(jax.ShapeDtypeStruct((rows,cols),bf16),jax.ShapeDtypeStruct((1,head),f32)),
        compiler_params=pltpu.CompilerParams(vmem_limit_bytes=VMEM_BYTES), name="heads_back",
        cost_estimate=pl.CostEstimate(flops=20*rows*cols,bytes_accessed=10*rows*cols,transcendentals=0),
    )(grad,pre,gain[None],cos,sin)

TN=(((0,),(0,)),((),()))

def expert_kernel(capacity, blocks, *refs):
    mine_ref=refs[0]; x_refs=refs[1:1+blocks]; c_refs=refs[1+blocks:1+2*blocks]
    plan_refs=refs[1+2*blocks:1+3*blocks]
    (router_ref,wg_ref,wu_ref,wd_ref,
     rows_ref,pair_ref,hid_ref,dgate_ref,dup_ref,gg_ref)=refs[1+3*blocks:11+3*blocks]
    out_refs=refs[11+3*blocks:11+4*blocks]; back_refs=refs[11+4*blocks:11+5*blocks]
    gates_ref,out_acc,back_acc=refs[11+5*blocks:]
    step=pl.program_id(0); last=pl.num_programs(0)-1
    experts,tokens=plan_refs[0].shape
    @pl.when(step==0)
    def _():
        for b in range(blocks):
            logits=mm(router_ref[...],x_refs[b][...],NT)
            logits=jnp.where(plan_refs[b][...].astype(f32)<UNCHOSEN,logits,masked_score)
            e=jnp.exp(logits-jnp.max(logits,0,keepdims=True))
            gates_ref[b]=e/jnp.sum(e,0,keepdims=True)
    expert=mine_ref[0]+step
    hit=lax.broadcasted_iota(jnp.int32,(experts,tokens),0)==expert
    slot_of=lax.broadcasted_iota(jnp.int32,(capacity,tokens),0)
    picks=[];rows=[];cots=[];weights=[]
    for b in range(blocks):
        slot=jnp.sum(jnp.where(hit,plan_refs[b][...].astype(f32),0.0),0,keepdims=True).astype(jnp.int32)
        gate=jnp.sum(jnp.where(hit,gates_ref[b],0.0),0,keepdims=True)
        on=slot_of==slot
        weights.append(jnp.sum(jnp.where(on,gate,0.0),1,keepdims=True))
        pick=jnp.where(on,1.0,0.0)
        picks.append(pick.astype(bf16))
        rows.append(mm(picks[b],x_refs[b][...]).astype(bf16))
        cots.append(mm(picks[b],c_refs[b][...]))
    rows=jnp.concatenate(rows,0); cots=jnp.concatenate(cots,0); weights=jnp.concatenate(weights,0)
    rows_ref[0]=rows
    gate_pre=mm(rows,wg_ref[0]); up_pre=mm(rows,wu_ref[0])
    sig=jax.nn.sigmoid(gate_pre)
    act=gate_pre*sig
    hidden=(act*up_pre).astype(bf16)
    hid_ref[0]=hidden
    pair=(weights*cots).astype(bf16)
    pair_ref[0]=pair
    hidden_grad=mm(pair,wd_ref[0],NT)
    dgate=(hidden_grad*up_pre*sig*(1.0+gate_pre*(1.0-sig))).astype(bf16)
    dup=(hidden_grad*act).astype(bf16)
    dgate_ref[0]=dgate; dup_ref[0]=dup
    back=(mm(dgate,wg_ref[0],NT)+mm(dup,wu_ref[0],NT)).astype(bf16)
    out=mm(hidden,wd_ref[0])
    gate_grad=jnp.sum(out*cots,1,keepdims=True)
    out=(out*weights).astype(bf16)
    for b in range(blocks):
        part=slice(b*capacity,(b+1)*capacity)
        gg_ref[b]=jnp.sum(jnp.where(picks[b]>0,gate_grad[part],0.0),0,keepdims=True)
        for acc,refs_b,vals in ((back_acc,back_refs,back),(out_acc,out_refs,out)):
            total=mm(picks[b],vals[part],TN)
            @pl.when(step==0)
            def _():
                acc[b]=total
            @pl.when(step==last)
            def _():
                refs_b[b][...]=(acc[b]+total).astype(bf16)

UNCHOSEN=1024.0
def expert_chunk(mine, xs, cs, router, wg, wu, wd, capacity):
    blocks=len(xs); local,width,ff=wg.shape; tokens=xs[0].shape[0]; experts=router.shape[0]
    rows=blocks*capacity
    assert local==2
    once=lambda *shape: pl.BlockSpec(shape,lambda e:(0,)*len(shape),pipeline_mode=pl.Buffered(1))
    per=lambda *shape: pl.BlockSpec((1,)+shape,lambda e:(e,)+(0,)*len(shape))
    fixed=lambda *shape: pl.BlockSpec(shape,lambda e:(0,)*len(shape))
    res=pl.pallas_call(functools.partial(expert_kernel,capacity,blocks),
        out_shape=(jax.ShapeDtypeStruct((local,rows,width),bf16),)*2+(jax.ShapeDtypeStruct((local,rows,ff),bf16),)*3
          +(jax.ShapeDtypeStruct((blocks,local,1,tokens),f32),)+(jax.ShapeDtypeStruct((tokens,width),bf16),)*(2*blocks),
        grid=(local,),
        in_specs=[pl.BlockSpec(memory_space=pltpu.SMEM)]+[once(tokens,width)]*(2*blocks)+[pl.BlockSpec((experts,tokens),lambda e:(tokens//experts,0),pipeline_mode=pl.Buffered(1))]*blocks+[once(experts,width),
            per(width,ff),per(width,ff),per(ff,width)],
        out_specs=(per(rows,width),)*2+(per(rows,ff),)*3+(pl.BlockSpec((blocks,pl.squeezed,1,tokens),lambda e:(0,e,0,0)),)+(fixed(tokens,width),)*(2*blocks),
        scratch_shapes=[pltpu.VMEM((blocks,experts,tokens),f32),pltpu.VMEM((blocks,tokens,width),f32),pltpu.VMEM((blocks,tokens,width),f32)],
        compiler_params=params(), name="expert_chunk",
        cost_estimate=pl.CostEstimate(flops=local*(12*rows*width*ff+8*rows*tokens*width),bytes_accessed=6*local*width*ff,transcendentals=0),
    )(mine,*xs,*cs,*cs,router,wg,wu,wd)
    return res[:5],res[5].reshape(blocks,local,tokens),res[6:6+blocks],res[6+blocks:]

def expert_grads_kernel(chunks, *refs):
    rows=jnp.concatenate([r[0] for r in refs[:chunks]],0)
    pair=jnp.concatenate([r[0] for r in refs[chunks:2*chunks]],0)
    hid=jnp.concatenate([r[0] for r in refs[2*chunks:3*chunks]],0)
    dgate=jnp.concatenate([r[0] for r in refs[3*chunks:4*chunks]],0)
    dup=jnp.concatenate([r[0] for r in refs[4*chunks:5*chunks]],0)
    out_ref=refs[5*chunks]
    ff=hid.shape[1]
    rows=rows.T; pair=pair.T
    out_ref[0,:,:ff]=mm(rows,dgate).astype(bf16)
    out_ref[0,:,ff:2*ff]=mm(rows,dup).astype(bf16)
    out_ref[0,:,2*ff:]=mm(pair,hid).astype(bf16)

def expert_grads(acts, tile=512):
    chunks=len(acts); local,count,width=acts[0][0].shape; ff=acts[0][2].shape[2]
    tall=pl.BlockSpec((1,count,tile),lambda e,i:(e,0,i))
    flat=pl.BlockSpec((1,count,ff),lambda e,i:(e,0,0))
    return pl.pallas_call(functools.partial(expert_grads_kernel,chunks),
        out_shape=jax.ShapeDtypeStruct((local,width,3*ff),bf16),
        grid=(local,width//tile),
        in_specs=[tall]*(2*chunks)+[flat]*(3*chunks),
        out_specs=pl.BlockSpec((1,tile,3*ff),lambda e,i:(e,i,0)),
        compiler_params=params(2), name="expert_grads",
        cost_estimate=pl.CostEstimate(flops=6*local*chunks*count*width*ff,bytes_accessed=6*local*width*ff+4*local*chunks*count*width,transcendentals=0),
    )(*[a[i] for i in range(5) for a in acts])

ALL=("dp","context","experts")


def from_behind(array, axis, by):
    length=lax.axis_size(axis)
    pairs=[(i,i+by) for i in range(length) if 0<=i+by<length]
    return lax.ppermute(array,axis,pairs)


def swap_cores(array):
    return lax.ppermute(array,"experts",[(i,i^1) for i in range(lax.axis_size("experts"))])


def chip_order():
    chips=lax.axis_size("experts")//2
    return list(range(0,chips,2))+list(range(1,chips,2))[::-1]


def next_chip(array):
    order=chip_order(); chips=len(order)
    return lax.ppermute(array,"experts",[(2*order[i]+c,2*order[(i+1)%chips]+c) for i in range(chips) for c in range(2)])


def gather_ring(array):
    lanes=[array]
    for _ in range(len(chip_order())-1):
        lanes.append(next_chip(lanes[-1]))
    return [(lane,swap_cores(lane)) for lane in lanes]


def ring_sources():
    order=chip_order(); chips=len(order)
    me=lax.axis_index("experts")
    spot=jnp.array([order.index(i) for i in range(chips)],jnp.int32)[me//2]
    back=jnp.array(order,jnp.int32)[(spot-jnp.arange(chips))%chips]
    core=me%2
    return jnp.stack([2*back+core,2*back+1-core],1).reshape(-1)


def ring_sum(parts):
    moving=None
    for mine,other in parts[1:]+parts[:1]:
        total=mine.astype(f32)+swap_cores(other).astype(f32)
        if moving is not None:
            total=total+moving.astype(f32)
        moving=next_chip(total.astype(bf16)) if mine is not parts[0][0] else total
    return moving


def sum_everywhere(array):
    for axis in ALL:
        length=lax.axis_size(axis); step=1
        while step<length:
            array=array+lax.ppermute(array,axis,[(i,i^step) for i in range(length)])
            step*=2
    return array


def rms_scale(values, norm_gain):
    return values*lax.rsqrt(jnp.mean(values*values,axis=-1,keepdims=True)+norm_eps)*norm_gain


def rope_rows(positions, head_width):
    frequencies=jnp.power(1000000.0,-jnp.arange(0,head_width,2).astype(f32)/head_width)
    angles=positions.astype(f32)[:,None]*frequencies[None,:]
    cosine,sine=jnp.cos(angles),jnp.sin(angles)
    return jnp.concatenate([cosine,cosine],1),jnp.concatenate([-sine,sine],1)


def slot_plan(ids, order, experts):
    tokens,top=ids.shape
    count=tokens*top
    place=jnp.arange(count,dtype=jnp.int32)
    owner=(order[None,:]//top==jnp.arange(tokens,dtype=jnp.int32)[:,None]).astype(bf16)
    choice=order[:,None]%top==jnp.arange(top,dtype=jnp.int32)[None,:]
    digits=jnp.concatenate([jnp.where(choice,(place//64)[:,None],0),jnp.where(choice,(place%64)[:,None],0)],1).astype(bf16)
    found=mm(owner,digits)
    found=64.0*found[:,:top]+found[:,top:]
    chosen=ids.T[None]==jnp.arange(experts,dtype=jnp.int32)[:,None,None]
    spot=jnp.sum(jnp.where(chosen,found.T[None],0.0),1)
    picked=jnp.any(chosen,1)
    spot=jnp.where(picked,spot,float(count))
    earlier=jnp.sum((spot[:,:,None]<spot[:,None,:]).astype(f32),1)
    return jnp.where(picked,earlier,float(UNCHOSEN))


def own_columns(left):
    tokens,cols=left.shape
    devices=math.prod(lax.axis_size(a) for a in ALL)
    split=left.reshape(tokens,devices//2,2,cols//devices)
    core=lax.axis_index("experts")%2
    keep=lax.dynamic_index_in_dim(split,core,2,False).reshape(tokens,cols//2)
    give=lax.dynamic_index_in_dim(split,1-core,2,False).reshape(tokens,cols//2)
    return jnp.concatenate([keep,swap_cores(give)],0)


def sum_rows(partial):
    dp,context,chips=lax.axis_size("dp"),lax.axis_size("context"),lax.axis_size("experts")//2
    part=lax.psum_scatter(partial,("dp","context"),scatter_dimension=0,tiled=True)
    part=part.reshape(chips,-1,partial.shape[1])
    order=chip_order()
    spot=jnp.array([order.index(i) for i in range(chips)],jnp.int32)[lax.axis_index("experts")//2]
    moving=None
    for step in list(range(1,chips))+[0]:
        dest=jnp.array(order,jnp.int32)[(spot-step)%chips]
        total=lax.dynamic_index_in_dim(part,dest,0,False).astype(f32)
        if moving is not None:
            total=total+moving.astype(f32)
        moving=next_chip(total.astype(bf16)) if step else total
    return moving


def shards(hidden_in, segments, expert_ids, placement_order, out_grad, attention_gain, query_weight, key_matrix, value_matrix,
           query_gain, key_gain, out_weight, feedforward_gain, router_weight, gate_weight, up_weight, down_weight):
    tok_rows,model_width=hidden_in.shape[1:]
    head_dim=query_gain.shape[0]
    kv_width=key_matrix.shape[1]
    kv_heads=kv_width//head_dim
    top_count=expert_ids.shape[2]
    local_experts=gate_weight.shape[0]
    all_experts=local_experts*lax.axis_size("experts")
    capacity=tok_rows*top_count//all_experts
    reach=WINDOW//tok_rows
    seq_axes=("context","experts")
    seq_place=lax.axis_index(seq_axes)
    devices=math.prod(lax.axis_size(a) for a in ALL)
    expert_place=lax.axis_index("experts")

    gate_full=lax.all_gather(gate_weight,("dp","context"),axis=1,tiled=True)
    up_full=lax.all_gather(up_weight,("dp","context"),axis=1,tiled=True)
    down_full=lax.all_gather(down_weight,("dp","context"),axis=2,tiled=True)

    x_rows=hidden_in[0].astype(f32)
    attention_input=rms_scale(x_rows,attention_gain).astype(bf16)
    positions=seq_place*tok_rows+jnp.arange(tok_rows,dtype=jnp.int32)
    cos_rows,sin_rows=rope_rows(positions,head_dim)
    key_pre,key_rows=project_heads(attention_input,key_matrix,key_gain,cos_rows,sin_rows)
    value_rows=mm(attention_input,value_matrix).astype(bf16)
    kvs=[jnp.concatenate([key_rows,value_rows],1)]
    for _ in range(reach):
        kvs.append(from_behind(kvs[-1],seq_axes,1))

    plan=slot_plan(expert_ids[0],placement_order[0,0],all_experts)
    sent=jnp.concatenate([out_grad[0],jnp.pad(plan.astype(bf16),((0,0),(0,model_width-tok_rows)))],0)
    cots=gather_ring(sent)

    query_pre,query_rows=project_heads(attention_input,query_weight,query_gain,cos_rows,sin_rows)
    seg_row=segments[0]
    seg_padded=jnp.concatenate([jnp.full((reach*tok_rows,),-1,jnp.int32),seg_row],0)
    key_segs=lax.dynamic_slice_in_dim(seg_padded,seq_place*tok_rows,(reach+1)*tok_rows,0).reshape(reach+1,tok_rows)[::-1]
    query_segs=key_segs[0]
    attn_mix,inverse=attend(query_rows,kvs,query_segs,key_segs,kv_heads,head_dim)
    middle=x_rows+mm(attn_mix,out_weight)
    ffn_in=rms_scale(middle,feedforward_gain).astype(bf16)
    ffn_blocks=gather_ring(ffn_in)

    router_rows=router_weight.T
    mine=(expert_place*local_experts).astype(jnp.int32)[None]
    acts,gate_parts,out_parts,back_parts=[],[],[],[]
    for xs,cs in zip(ffn_blocks,cots):
        act,gate_part,out_part,back_part=expert_chunk(mine,xs,cs,router_rows,gate_full,up_full,down_full,capacity)
        acts.append(act); gate_parts.append(gate_part); out_parts.append(out_part); back_parts.append(back_part)

    sources=ring_sources()
    gate_rel=jnp.concatenate(gate_parts,0)
    gate_send=jnp.sum(jnp.where((sources[None,:]==jnp.arange(sources.shape[0])[:,None])[:,:,None,None],gate_rel[None],0.0),1)
    gate_grad=lax.all_to_all(gate_send,"experts",0,0,tiled=True).reshape(all_experts,tok_rows).T

    ffn_in_grad=ring_sum(back_parts)
    logits=mm(ffn_in,router_weight)
    chosen=plan.T<UNCHOSEN
    gates=jax.nn.softmax(jnp.where(chosen,logits,masked_score),axis=-1)
    logit_grad=(gates*(gate_grad-jnp.sum(gates*gate_grad,-1,keepdims=True))).astype(bf16)
    ffn_in_grad=ffn_in_grad+mm(logit_grad,router_weight,NT)
    router_grad=mm(ffn_in,logit_grad,TN)
    norm_unused,ffn_pull=jax.vjp(rms_scale,middle,feedforward_gain)
    middle_norm_grad,ffn_gain_grad=ffn_pull(ffn_in_grad)
    middle_grad=out_grad[0].astype(f32)+middle_norm_grad
    branch_grad=middle_grad.astype(bf16)
    mix_grad=mm(branch_grad,out_weight,NT).astype(bf16)

    expert_full=expert_grads(acts)
    expert_rows=lax.psum_scatter(expert_full,("dp","context"),scatter_dimension=1,tiled=True).astype(f32)
    ff=gate_weight.shape[2]
    gate_weight_grad=expert_rows[:,:,:ff]; up_weight_grad=expert_rows[:,:,ff:2*ff]
    down_weight_grad=expert_rows[:,:,2*ff:].transpose(0,2,1)

    block_out=(middle+ring_sum(out_parts)).astype(bf16)

    branch_both=jnp.concatenate([branch_grad,swap_cores(branch_grad)],0)
    out_grad_part=mm(own_columns(attn_mix),branch_both,TN).astype(bf16)
    out_weight_grad=sum_rows(out_grad_part)

    query_pre_grad,query_gain_part,key_parts,value_parts=attend_back(query_rows,kvs,query_segs,key_segs,mix_grad,attn_mix,inverse,query_pre,
        query_gain,cos_rows,sin_rows,kv_heads,head_dim)
    carry=jnp.concatenate([key_parts[reach],value_parts[reach]],1)
    for step in range(reach-1,-1,-1):
        carry=from_behind(carry.astype(bf16),seq_axes,-1).astype(f32)+jnp.concatenate([key_parts[step],value_parts[step]],1)
    value_pre_grad=carry[:,kv_width:].astype(bf16)
    key_pre_grad,key_gain_part=heads_back(carry[:,:kv_width],key_pre,key_gain,cos_rows,sin_rows)

    input_both=own_columns(attention_input)
    query_both=jnp.concatenate([query_pre_grad,swap_cores(query_pre_grad)],0)
    query_weight_grad=sum_rows(mm(input_both,query_both,TN).astype(bf16))
    kv_pre_grad=jnp.concatenate([key_pre_grad,value_pre_grad],1)
    kv_both=jnp.concatenate([kv_pre_grad,swap_cores(kv_pre_grad)],0)
    kv_weight_grad=sum_rows(mm(input_both,kv_both,TN).astype(bf16))

    attn_in_grad=mm(query_pre_grad,query_weight,NT)+mm(key_pre_grad,key_matrix,NT)+mm(value_pre_grad,value_matrix,NT)
    attn_unused,attn_pull=jax.vjp(rms_scale,x_rows,attention_gain)
    x_norm_grad,attn_gain_grad=attn_pull(attn_in_grad)
    input_grad=middle_grad+x_norm_grad

    small=jnp.concatenate([router_grad.reshape(devices,-1),ffn_gain_grad.reshape(devices,-1),attn_gain_grad.reshape(devices,-1),
        query_gain_part.reshape(devices,-1),key_gain_part.reshape(devices,-1)],1)
    small=lax.dynamic_index_in_dim(sum_everywhere(small),lax.axis_index(ALL),0,False)
    rows=model_width//devices; few=head_dim//devices
    router_weight_grad=small[:rows*all_experts].reshape(rows,all_experts)
    rest=small[rows*all_experts:]
    return (block_out[None],input_grad[None],rest[rows:2*rows],query_weight_grad,kv_weight_grad[:,:kv_width],kv_weight_grad[:,kv_width:],
        rest[2*rows:2*rows+few],rest[2*rows+few:],out_weight_grad,rest[:rows],router_weight_grad,gate_weight_grad,up_weight_grad,down_weight_grad)


def solution(mesh):
    tokens=P("dp",("context","experts"),None)
    rows=P(ALL,None); flat=P(ALL)
    tall=P("experts",("dp","context"),None); wide=P("experts",None,("dp","context"))
    in_specs=(tokens,P("dp",None),tokens,tokens,tokens)+(P(),)*9+(tall,tall,wide)
    out_specs=(tokens,tokens,flat,rows,rows,rows,flat,flat,rows,flat,rows,tall,tall,wide)
    return jax.shard_map(shards,mesh=mesh,in_specs=in_specs,out_specs=out_specs,check_vma=False)
```

```python
import functools, math
import jax, jax.numpy as jnp
from jax import lax
import jax.experimental.pallas as pl
import jax.experimental.pallas.tpu as pltpu
from jax.sharding import PartitionSpec as P

f32=jnp.float32; bf16=jnp.bfloat16
WINDOW=1024
norm_eps=1e-6
masked_score=-1e30

def cost(us):
    return pl.CostEstimate(flops=int(us*1.15e9),bytes_accessed=1<<18,transcendentals=0)

VMEM_BYTES=60*1024*1024
NT=(((1,),(1,)),((),()))
NN=(((1,),(0,)),((),()))

def params(steps=1):
    return pltpu.CompilerParams(dimension_semantics=("arbitrary",)*steps, vmem_limit_bytes=VMEM_BYTES)

ANY=pl.BlockSpec(memory_space=pl.ANY)

def mm(a,b,dims=NN):
    return lax.dot_general(a,b,dims,preferred_element_type=f32)

def heads_kernel(count, x_ref, w_ref, gain_ref, cos_ref, sin_ref, *refs):
    pre_ref,out_ref=refs[count:]
    head=gain_ref.shape[1]
    pre=mm(x_ref[...], w_ref[...])
    pre_ref[...]=pre
    gain=gain_ref[...]; cos=cos_ref[...]; sin=sin_ref[...]
    for j in range(pre.shape[1]//head):
        u=pre[:, j*head:(j+1)*head]
        n=u*lax.rsqrt(jnp.mean(u*u,-1,keepdims=True)+norm_eps)*gain
        out_ref[:, j*head:(j+1)*head]=(n*cos+pltpu.roll(n,head//2,1)*sin).astype(bf16)

def project_heads(x, w, gain, cos, sin, tile=512, deps=()):
    rows,depth=x.shape; cols=w.shape[1]; head=gain.shape[0]
    tile=min(tile,cols)
    whole=lambda shape: pl.BlockSpec(shape, lambda i:(0,0))
    return pl.pallas_call(functools.partial(heads_kernel,len(deps)),
        out_shape=(jax.ShapeDtypeStruct((rows,cols),f32),jax.ShapeDtypeStruct((rows,cols),bf16)),
        grid=(cols//tile,),
        in_specs=[whole((rows,depth)),pl.BlockSpec((depth,tile),lambda i:(0,i)),whole((1,head)),whole((rows,head)),whole((rows,head))]+[ANY]*len(deps),
        out_specs=(pl.BlockSpec((rows,tile),lambda i:(0,i)),)*2,
        compiler_params=params(), name="project_heads",
        cost_estimate=cost(13),
    )(x,w,gain[None],cos,sin,*deps)

def attend_kernel(scale, blocks, count, *refs):
    q_ref=refs[0]; k_refs=refs[1:1+blocks]; v_refs=refs[1+blocks:1+2*blocks]
    qseg_ref,kseg_ref=refs[1+2*blocks:3+2*blocks]
    out_ref,inv_ref,bias_ref,vaug_ref=refs[3+2*blocks+count:]
    rows,head=k_refs[0].shape
    @pl.when(pl.program_id(0)==0)
    def _():
        vaug_ref[...]=jnp.ones_like(vaug_ref)
        lead=lax.broadcasted_iota(jnp.int32,(rows,rows),0)-lax.broadcasted_iota(jnp.int32,(rows,rows),1)
        for b in range(blocks):
            gap=lead+b*rows
            ok=(qseg_ref[...]==kseg_ref[b:b+1,:])&(gap>=0)&(gap<WINDOW)
            bias_ref[b]=jnp.where(ok,0.0,masked_score)
    for b in range(blocks):
        vaug_ref[b,:,:head]=v_refs[b][...]
    lane=lax.broadcasted_iota(jnp.int32,(rows,head),1)
    inv_all=jnp.zeros((rows,head),f32)
    for j in range(q_ref.shape[1]//head):
        q=q_ref[:, j*head:(j+1)*head]
        acc=jnp.zeros((rows,2*head),f32)
        for b in range(blocks):
            s=mm(q,k_refs[b][...],NT)
            p=jnp.exp2(s*scale+bias_ref[b]).astype(bf16)
            acc+=mm(p,vaug_ref[b])
        inv=1.0/acc[:,head:]
        out_ref[:, j*head:(j+1)*head]=(acc[:,:head]*inv).astype(bf16)
        inv_all=jnp.where(lane==j,inv,inv_all)
    inv_ref[...]=inv_all

def attend(q, kvs, qseg, ksegs, kv_heads, head, deps=()):
    rows,cols=q.shape; blocks=len(kvs); group=cols//kv_heads
    scale=math.log2(math.e)/math.sqrt(head)
    return pl.pallas_call(functools.partial(attend_kernel,scale,blocks,len(deps)),
        out_shape=(jax.ShapeDtypeStruct((rows,cols),bf16),jax.ShapeDtypeStruct((rows,kv_heads*head),f32)),
        grid=(kv_heads,),
        in_specs=[pl.BlockSpec((rows,group),lambda g:(0,g))]
          +[pl.BlockSpec((rows,head),lambda g:(0,g))]*blocks+[pl.BlockSpec((rows,head),lambda g:(0,kv_heads+g))]*blocks
          +[pl.BlockSpec((rows,1),lambda g:(0,0)),pl.BlockSpec((blocks,rows),lambda g:(0,0))]+[ANY]*len(deps),
        out_specs=(pl.BlockSpec((rows,group),lambda g:(0,g)),pl.BlockSpec((rows,head),lambda g:(0,g))),
        scratch_shapes=[pltpu.VMEM((blocks,rows,rows),f32),pltpu.VMEM((blocks,rows,2*head),bf16)],
        compiler_params=params(), name="attend",
        cost_estimate=cost(16),
    )(q,*kvs,*kvs,qseg[:,None],ksegs,*deps)

def attend_back_kernel(scale, blocks, count, *refs):
    q_ref=refs[0]; k_refs=refs[1:1+blocks]; v_refs=refs[1+blocks:1+2*blocks]
    qseg_ref,kseg_ref,grad_ref,mix_ref,inv_ref,pre_ref,gain_ref,cos_ref,sin_ref=refs[1+2*blocks:10+2*blocks]
    dpre_ref,dgain_ref,dk_ref,dv_ref,bias_ref,vaug_ref=refs[10+2*blocks+count:]
    rows,head=k_refs[0].shape
    soft=scale*math.log(2.0)
    @pl.when(pl.program_id(0)==0)
    def _():
        vaug_ref[...]=jnp.ones_like(vaug_ref)
        lead=lax.broadcasted_iota(jnp.int32,(rows,rows),1)-lax.broadcasted_iota(jnp.int32,(rows,rows),0)
        for b in range(blocks):
            gap=lead+b*rows
            ok=(kseg_ref[:,b:b+1]==qseg_ref[...])&(gap>=0)&(gap<WINDOW)
            bias_ref[b]=jnp.where(ok,0.0,masked_score)
        dgain_ref[...]=jnp.zeros_like(dgain_ref)
    k_turned=[]
    for b in range(blocks):
        vaug_ref[b,:,:head]=v_refs[b][...]
        k_turned.append(k_refs[b][...].T)
    lane=lax.broadcasted_iota(jnp.int32,(rows,head),1)
    gain=gain_ref[...]; cos=cos_ref[...]; sin=sin_ref[...]
    dk_ref[...]=jnp.zeros_like(dk_ref); dv_ref[...]=jnp.zeros_like(dv_ref)
    for j in range(q_ref.shape[1]//head):
        cols=slice(j*head,(j+1)*head)
        q=q_ref[:,cols]
        inv=inv_ref[:,j:j+1]
        grad=grad_ref[:,cols].astype(f32)*inv
        delta=-jnp.sum(grad*mix_ref[:,cols].astype(f32),-1,keepdims=True)
        hi=delta.astype(bf16).astype(f32)
        tail=jnp.where(lane==0,hi,jnp.where(lane==1,delta-hi,0.0)).astype(bf16)
        low=grad.astype(bf16)
        both=jnp.concatenate([low,tail],axis=1)
        turned=jnp.zeros((head,rows),f32)
        for b in range(blocks):
            s=mm(k_refs[b][...],q,NT)
            p=jnp.exp2(s*scale+bias_ref[b])
            d=mm(vaug_ref[b],both,NT)
            ds=(p*d).astype(bf16)
            dk_ref[b]+=mm(ds,q)
            dv_ref[b]+=mm(p.astype(bf16),low)
            turned+=mm(k_turned[b],ds)
        g=turned.T*soft
        g=g*cos+pltpu.roll(g*sin,head//2,1)
        u=pre_ref[:,cols]
        r=lax.rsqrt(jnp.mean(u*u,-1,keepdims=True)+norm_eps)
        n=u*r
        dgain_ref[...]+=jnp.sum(g*n,0,keepdims=True)
        g=g*gain
        dpre_ref[:,cols]=(r*(g-n*jnp.mean(g*n,-1,keepdims=True))).astype(bf16)
    dk_ref[...]*=soft

def attend_back(q, kvs, qseg, ksegs, grad, mix, inv, pre, gain, cos, sin, kv_heads, head, first=0, count=None, deps=()):
    rows,cols=q.shape; blocks=len(kvs); group=cols//kv_heads
    count=count or kv_heads
    scale=math.log2(math.e)/math.sqrt(head)
    wide=lambda: pl.BlockSpec((rows,group),lambda g:(0,first+g))
    part=lambda: pl.BlockSpec((rows,head),lambda g:(0,first+g))
    whole=lambda *shape: pl.BlockSpec(shape,lambda g:(0,)*len(shape))
    return pl.pallas_call(functools.partial(attend_back_kernel,scale,blocks,len(deps)),
        out_shape=(jax.ShapeDtypeStruct((rows,count*group),bf16),jax.ShapeDtypeStruct((1,head),f32),
                   jax.ShapeDtypeStruct((blocks,rows,count*head),f32),jax.ShapeDtypeStruct((blocks,rows,count*head),f32)),
        grid=(count,),
        in_specs=[wide()]+[part()]*blocks+[pl.BlockSpec((rows,head),lambda g:(0,kv_heads+first+g))]*blocks
          +[whole(1,rows),whole(rows,blocks),wide(),wide(),part(),wide(),whole(1,head),whole(rows,head),whole(rows,head)]+[ANY]*len(deps),
        out_specs=(pl.BlockSpec((rows,group),lambda g:(0,g)),whole(1,head),pl.BlockSpec((blocks,rows,head),lambda g:(0,0,g)),pl.BlockSpec((blocks,rows,head),lambda g:(0,0,g))),
        scratch_shapes=[pltpu.VMEM((blocks,rows,rows),f32),pltpu.VMEM((blocks,rows,2*head),bf16)],
        compiler_params=params(), name="attend_back",
        cost_estimate=cost(6+11*count),
    )(q,*kvs,*kvs,qseg[None],ksegs.T,grad,mix,inv,pre,gain[None],cos,sin,*deps)

def heads_back_kernel(count, grad_ref, pre_ref, gain_ref, cos_ref, sin_ref, *refs):
    dpre_ref,dgain_ref=refs[count:]
    head=gain_ref.shape[1]
    total=jnp.zeros((1,head),f32)
    for j in range(pre_ref.shape[1]//head):
        cols=slice(j*head,(j+1)*head)
        g=grad_ref[:,cols]
        g=g*cos_ref[...]+pltpu.roll(g*sin_ref[...],head//2,1)
        u=pre_ref[:,cols]
        r=lax.rsqrt(jnp.mean(u*u,-1,keepdims=True)+norm_eps)
        n=u*r
        total+=jnp.sum(g*n,0,keepdims=True)
        g=g*gain_ref[...]
        dpre_ref[:,cols]=(r*(g-n*jnp.mean(g*n,-1,keepdims=True))).astype(bf16)
    dgain_ref[...]=total

def heads_back(grad, pre, gain, cos, sin, deps=()):
    rows,cols=grad.shape; head=gain.shape[0]
    full=lambda *a: pl.BlockSpec(a,lambda i:(0,0))
    return pl.pallas_call(functools.partial(heads_back_kernel,len(deps)),
        out_shape=(jax.ShapeDtypeStruct((rows,cols),bf16),jax.ShapeDtypeStruct((1,head),f32)),
        grid=(1,),
        in_specs=[full(rows,cols)]*2+[full(1,head),full(rows,head),full(rows,head)]+[ANY]*len(deps),
        out_specs=(full(rows,cols),full(1,head)),
        compiler_params=params(), name="heads_back", cost_estimate=cost(3),
    )(grad,pre,gain[None],cos,sin,*deps)

def key_value_kernel(count, x_ref, in_gain_ref, wk_ref, wv_ref, gain_ref, cos_ref, sin_ref, *refs):
    norm_ref,pre_ref,kv_ref=refs[count:]
    head=gain_ref.shape[1]; width=wk_ref.shape[1]
    x=x_ref[...].astype(f32)
    norm=(x*lax.rsqrt(jnp.mean(x*x,-1,keepdims=True)+norm_eps)*in_gain_ref[...]).astype(bf16)
    norm_ref[...]=norm
    pre=mm(norm,wk_ref[...])
    pre_ref[...]=pre
    gain=gain_ref[...]; cos=cos_ref[...]; sin=sin_ref[...]
    for j in range(width//head):
        u=pre[:, j*head:(j+1)*head]
        n=u*lax.rsqrt(jnp.mean(u*u,-1,keepdims=True)+norm_eps)*gain
        kv_ref[:, j*head:(j+1)*head]=(n*cos+pltpu.roll(n,head//2,1)*sin).astype(bf16)
    kv_ref[:,width:]=mm(norm,wv_ref[...]).astype(bf16)

def key_value(x, in_gain, wk, wv, gain, cos, sin, deps=()):
    rows,depth=x.shape; width=wk.shape[1]; head=gain.shape[0]
    full=lambda a: pl.BlockSpec(a,lambda i:(0,0))
    return pl.pallas_call(functools.partial(key_value_kernel,len(deps)),
        out_shape=(jax.ShapeDtypeStruct((rows,depth),bf16),jax.ShapeDtypeStruct((rows,width),f32),jax.ShapeDtypeStruct((rows,2*width),bf16)),
        grid=(1,),
        in_specs=[full((rows,depth)),full((1,depth)),full((depth,width)),full((depth,width)),full((1,head)),full((rows,head)),full((rows,head))]+[ANY]*len(deps),
        out_specs=(full((rows,depth)),full((rows,width)),full((rows,2*width))),
        compiler_params=params(), name="key_value",
        cost_estimate=cost(5),
    )(x,in_gain[None],wk,wv,gain[None],cos,sin,*deps)

def out_kernel(count, mix_ref, w_ref, x_ref, gain_ref, plan_ref, *refs):
    middle_ref,sent_ref=refs[count:]
    i=pl.program_id(0); tile=w_ref.shape[1]
    rows=mix_ref.shape[0]
    for t in range(middle_ref.shape[1]//tile):
        @pl.when(i==t)
        def _():
            cols=slice(t*tile,(t+1)*tile)
            middle_ref[:,cols]=x_ref[:,cols].astype(f32)+mm(mix_ref[...],w_ref[...])
    @pl.when(i==pl.num_programs(0)-1)
    def _():
        v=middle_ref[...]
        sent_ref[:rows]=(v*lax.rsqrt(jnp.mean(v*v,-1,keepdims=True)+norm_eps)*gain_ref[...]).astype(bf16)
        sent_ref[rows:]=jnp.zeros((sent_ref.shape[0]-rows,sent_ref.shape[1]),bf16)
        sent_ref[rows:,:plan_ref.shape[1]]=plan_ref[...]

def project_out(mix, w, x, gain, plan, tile=512, deps=()):
    rows,depth=mix.shape; width=w.shape[1]; experts=plan.shape[0]
    full=lambda *a: pl.BlockSpec(a,lambda i:(0,0))
    return pl.pallas_call(functools.partial(out_kernel,len(deps)),
        out_shape=(jax.ShapeDtypeStruct((rows,width),f32),jax.ShapeDtypeStruct((rows+experts,width),bf16)),
        grid=(width//tile,),
        in_specs=[full(rows,depth),pl.BlockSpec((depth,tile),lambda i:(0,i)),full(rows,width),full(1,width),full(experts,rows)]+[ANY]*len(deps),
        out_specs=(full(rows,width),full(rows+experts,width)),
        compiler_params=params(), name="project_out", cost_estimate=cost(10),
    )(mix,w,x,gain[None],plan,*deps)

def turned_kernel(count, x_ref, w_ref, *refs):
    refs[count][...]=mm(x_ref[...],w_ref[...],NT).astype(refs[count].dtype)

def times_turned(x, w, dtype, tile=512, deps=()):
    rows,depth=x.shape; cols=w.shape[0]
    tile=min(tile,cols)
    return pl.pallas_call(functools.partial(turned_kernel,len(deps)),
        out_shape=jax.ShapeDtypeStruct((rows,cols),dtype),
        grid=(cols//tile,),
        in_specs=[pl.BlockSpec((rows,depth),lambda i:(0,0)),pl.BlockSpec((tile,depth),lambda i:(i,0))]+[ANY]*len(deps),
        out_specs=pl.BlockSpec((rows,tile),lambda i:(0,i)),
        compiler_params=params(), name="times_turned", cost_estimate=cost(11),
    )(x,w,*deps)


def hold(value, *deps):
    return pl.pallas_call(lambda *refs: None,
        out_shape=jax.ShapeDtypeStruct(value.shape,value.dtype),
        in_specs=[ANY]*(1+len(deps)), out_specs=ANY, input_output_aliases={0:0},
        name="hold", cost_estimate=cost(0.1),
    )(value,*deps)

TN=(((0,),(0,)),((),()))
UNCHOSEN=1024.0

def pack_kernel(count, gate_ref, up_ref, down_ref, *refs):
    out_ref=refs[count]
    ff=gate_ref.shape[1]
    out_ref[:,:ff]=gate_ref[...]
    out_ref[:,ff:2*ff]=up_ref[...]
    out_ref[:,2*ff:]=down_ref[...].T

def pack_weights(gate, up, down, which, deps=()):
    rows,ff=gate.shape[1:]
    return pl.pallas_call(functools.partial(pack_kernel,len(deps)),
        out_shape=jax.ShapeDtypeStruct((rows,3*ff),bf16),
        grid=(1,),
        in_specs=[pl.BlockSpec((pl.squeezed,rows,ff),lambda i:(which,0,0))]*2+[pl.BlockSpec((pl.squeezed,ff,rows),lambda i:(which,0,0))]+[ANY]*len(deps),
        out_specs=pl.BlockSpec((rows,3*ff),lambda i:(0,0)),
        compiler_params=params(), name="pack_weights",
        cost_estimate=cost(3),
    )(gate,up,down,*deps)

def expert_kernel(capacity, blocks, chained, pieces, count, *refs):
    mine_ref,place_ref=refs[:2]; refs=refs[2:]
    x_refs,c_refs,plan_refs=refs[:blocks],refs[blocks:2*blocks],refs[2*blocks:3*blocks]; refs=refs[3*blocks:]
    prev_out=prev_back=(None,)*blocks
    if chained:
        prev_out,prev_back=refs[:blocks],refs[blocks:2*blocks]; refs=refs[2*blocks:]
    router_ref=refs[0]; weight_refs=refs[1:1+pieces]; refs=refs[1+pieces+count:]
    rows_ref,pair_ref,hid_ref,dgate_ref,dup_ref=refs[:5]; refs=refs[5:]
    out_refs,back_refs=refs[:blocks],refs[blocks:2*blocks]
    kept_ref,sems=refs[2*blocks:]
    experts,tokens=plan_refs[0].shape
    ff=hid_ref.shape[1]
    copies=[[] for _ in range(3)]
    for i in range(3):
        for j,piece in enumerate(weight_refs):
            tall=piece.shape[0]
            spot=pl.ds(pl.multiple_of(place_ref[j],tall),tall)
            copies[i].append(pltpu.make_async_copy(piece.at[:,i*ff:(i+1)*ff],kept_ref.at[i,spot],sems.at[i,j]))
            copies[i][-1].start()
    def ready(i):
        for copy in copies[i]:
            copy.wait()
    hit=lax.broadcasted_iota(jnp.int32,(experts,tokens),0)==mine_ref[0]
    slot_of=lax.broadcasted_iota(jnp.int32,(capacity,tokens),0)
    picks=[];rows=[];cots=[];weights=[]
    for b in range(blocks):
        plan=plan_refs[b][...].astype(f32)
        logits=mm(router_ref[...],x_refs[b][...],NT)
        logits=jnp.where(plan<UNCHOSEN,logits,masked_score)
        e=jnp.exp(logits-jnp.max(logits,0,keepdims=True))
        gates=e/jnp.sum(e,0,keepdims=True)
        slot=jnp.sum(jnp.where(hit,plan,0.0),0,keepdims=True).astype(jnp.int32)
        gate=jnp.sum(jnp.where(hit,gates,0.0),0,keepdims=True)
        on=slot_of==slot
        weights.append(jnp.sum(jnp.where(on,gate,0.0),1,keepdims=True))
        picks.append(jnp.where(on,1.0,0.0).astype(bf16))
        rows.append(mm(picks[b],x_refs[b][...]).astype(bf16))
        cots.append(mm(picks[b],c_refs[b][...]))
    rows=jnp.concatenate(rows,0); cots=jnp.concatenate(cots,0); weights=jnp.concatenate(weights,0)
    rows_ref[...]=rows
    pair=(weights*cots).astype(bf16)
    pair_ref[...]=pair
    ready(0)
    gate_pre=mm(rows,kept_ref[0])
    ready(1)
    up_pre=mm(rows,kept_ref[1])
    sig=jax.nn.sigmoid(gate_pre)
    act=gate_pre*sig
    hidden=(act*up_pre).astype(bf16)
    hid_ref[...]=hidden
    ready(2)
    hidden_grad=mm(pair,kept_ref[2])
    dgate=(hidden_grad*up_pre*sig*(1.0+gate_pre*(1.0-sig))).astype(bf16)
    dup=(hidden_grad*act).astype(bf16)
    dgate_ref[...]=dgate; dup_ref[...]=dup
    back=(mm(dgate,kept_ref[0],NT)+mm(dup,kept_ref[1],NT)).astype(bf16)
    out=mm(hidden,kept_ref[2],NT)
    gate_grad=jnp.sum(out*cots,1,keepdims=True)
    out=(out*weights).astype(bf16)
    for b in range(blocks):
        part=slice(b*capacity,(b+1)*capacity)
        for prev,ref,vals in ((prev_back[b],back_refs[b],back),(prev_out[b],out_refs[b],out)):
            total=mm(picks[b],vals[part],TN)
            if chained:
                total+=prev[:tokens].astype(f32)
            ref[:tokens]=total.astype(bf16)
        grad=jnp.sum(jnp.where(picks[b]>0,gate_grad[part],0.0),0,keepdims=True)
        grad=jnp.where(hit,grad,0.0)
        high=grad.astype(bf16).astype(f32)
        back_refs[b][tokens:]=jnp.zeros((experts,back_refs[b].shape[1]),bf16)
        for i,digit in enumerate((high,grad-high)):
            spot=slice(i*tokens,(i+1)*tokens)
            if chained:
                digit+=prev_back[b][tokens:,spot].astype(f32)
            back_refs[b][tokens:,spot]=digit.astype(bf16)

def expert_chunk(mine, xs, cs, router, pieces, places, capacity, prev=None, deps=()):
    blocks=len(xs); tokens,width=cs[0].shape; ff=pieces[0].shape[1]//3; experts=router.shape[0]
    rows=blocks*capacity
    full=lambda *shape: pl.BlockSpec(shape,lambda i:(0,)*len(shape))
    once=lambda *shape: pl.BlockSpec(shape,lambda i:(0,)*len(shape),pipeline_mode=pl.Buffered(1))
    partial=[jax.ShapeDtypeStruct((tokens,width),bf16)]*blocks
    res=pl.pallas_call(functools.partial(expert_kernel,capacity,blocks,prev is not None,len(pieces),len(deps)),
        out_shape=[jax.ShapeDtypeStruct((rows,width),bf16)]*2+[jax.ShapeDtypeStruct((rows,ff),bf16)]*3
          +partial+[jax.ShapeDtypeStruct((tokens+experts,width),bf16)]*blocks,
        grid=(1,),
        in_specs=[pl.BlockSpec(memory_space=pltpu.SMEM)]*2+[once(tokens,width)]*(2*blocks)
          +[pl.BlockSpec((experts,tokens),lambda i:(tokens//experts,0),pipeline_mode=pl.Buffered(1))]*blocks
          +([once(tokens,width)]*blocks+[once(tokens+experts,width)]*blocks if prev else [])+[once(experts,width)]+[ANY]*(len(pieces)+len(deps)),
        out_specs=[once(rows,width)]*2+[once(rows,ff)]*3+[once(tokens,width)]*blocks+[once(tokens+experts,width)]*blocks,
        scratch_shapes=[pltpu.VMEM((3,width,ff),bf16),pltpu.SemaphoreType.DMA((3,len(pieces)))],
        compiler_params=params(), name="expert_chunk",
        cost_estimate=cost(4+4.7*blocks),
    )(mine,places,*xs,*cs,*xs,*(tuple(prev[0])+tuple(prev[1]) if prev else ()),router,*pieces,*deps)
    return res[:5],res[5:5+blocks],res[5+blocks:]

def expert_grads_kernel(chunks, count, *refs):
    join=lambda i: jnp.concatenate([r[...] for r in refs[i*chunks:(i+1)*chunks]],0)
    rows,pair,hid,dgate,dup=[join(i) for i in range(5)]
    out_ref=refs[5*chunks+count]
    ff=hid.shape[1]
    rows=rows.T; pair=pair.T
    out_ref[:,:ff]=mm(rows,dgate).astype(bf16)
    out_ref[:,ff:2*ff]=mm(rows,dup).astype(bf16)
    out_ref[:,2*ff:]=mm(pair,hid).astype(bf16)

def expert_grads(acts, tile=512, deps=()):
    chunks=len(acts); width=acts[0][0].shape[1]; ff=acts[0][2].shape[1]
    count=sum(a[0].shape[0] for a in acts)
    tall=[pl.BlockSpec((a[0].shape[0],tile),lambda i:(0,i)) for a in acts]
    flat=[pl.BlockSpec((a[0].shape[0],ff),lambda i:(0,0)) for a in acts]
    return pl.pallas_call(functools.partial(expert_grads_kernel,chunks,len(deps)),
        out_shape=jax.ShapeDtypeStruct((width,3*ff),bf16),
        grid=(width//tile,),
        in_specs=tall*2+flat*3+[ANY]*len(deps),
        out_specs=pl.BlockSpec((tile,3*ff),lambda i:(i,0)),
        compiler_params=params(), name="expert_grads",
        cost_estimate=cost(16),
    )(*[a[i] for i in range(5) for a in acts],*deps)


def pooled_kernel(rows, parts, count, *refs):
    core_ref=refs[0]; left=jnp.concatenate([refs[1][...],refs[2][...]],0)
    rights=refs[3:3+2*parts]; out_ref,turned_ref=refs[3+2*parts+count:]
    turned_ref[...]=left.T.reshape(turned_ref.shape)
    pairs=turned_ref.shape[0]//2
    kept=jnp.concatenate([turned_ref[2*i+core_ref[0]] for i in range(pairs)],0)
    start=0
    for p in range(parts):
        right=jnp.concatenate([rights[p][...],rights[parts+p][...]],0)
        out_ref[:,start:start+right.shape[1]]=mm(kept,right).astype(bf16)
        start+=right.shape[1]

def pooled_grad(core, left, left_other, rights, rights_other, rows, tile=512, deps=()):
    tokens,depth=left.shape; parts=len(rights); cols=sum(r.shape[1] for r in rights)
    tile=max(min(tile,depth),2*rows)
    full=[pl.BlockSpec(r.shape,lambda i:(0,0)) for r in rights]
    return pl.pallas_call(functools.partial(pooled_kernel,rows,parts,len(deps)),
        out_shape=jax.ShapeDtypeStruct((depth//2,cols),bf16),
        grid=(depth//tile,),
        in_specs=[pl.BlockSpec(memory_space=pltpu.SMEM)]+[pl.BlockSpec((tokens,tile),lambda i:(0,i))]*2+full*2+[ANY]*len(deps),
        out_specs=pl.BlockSpec((tile//2,cols),lambda i:(i,0)),
        scratch_shapes=[pltpu.VMEM((tile//rows,rows,2*tokens),bf16)],
        compiler_params=params(), name="pooled_grad", cost_estimate=cost(9*depth*cols/8e6),
    )(core,left,left_other,*rights,*rights_other,*deps)

ALL=("dp","context","experts")


def by_chips(array, step):
    axes=("context","experts")
    length=lax.axis_size(axes)
    return lax.ppermute(array,axes,[(i,i+2*step) for i in range(length) if 0<=i+2*step<length])


def after(value, *others):
    return lax.optimization_barrier((value,)+others)[0]


def swap_cores(array):
    return lax.ppermute(array,"experts",[(i,i^1) for i in range(lax.axis_size("experts"))])


def chip_order():
    chips=lax.axis_size("experts")//2
    return list(range(0,chips,2))+list(range(1,chips,2))[::-1]


def next_chip(array):
    order=chip_order(); chips=len(order)
    return lax.ppermute(array,"experts",[(2*order[i]+c,2*order[(i+1)%chips]+c) for i in range(chips) for c in range(2)])


def gather_ring(array):
    lanes=[array]
    for _ in range(len(chip_order())-1):
        lanes.append(next_chip(lanes[-1]))
    return [(lane,swap_cores(lane)) for lane in lanes]


def ring_step(part, moving=None, holds=()):
    mine,other=part
    if moving is not None:
        other=hold(other,moving,*holds)
    total=mine.astype(f32)+swap_cores(other).astype(f32)
    return total if moving is None else total+moving.astype(f32)


def sum_everywhere(array):
    for axis in ALL:
        length=lax.axis_size(axis); step=1
        while step<length:
            array=array+lax.ppermute(array,axis,[(i,i^step) for i in range(length)])
            step*=2
    return array


def rms_scale(values, norm_gain):
    return values*lax.rsqrt(jnp.mean(values*values,axis=-1,keepdims=True)+norm_eps)*norm_gain


def rope_rows(positions, head_width):
    frequencies=jnp.power(1000000.0,-jnp.arange(0,head_width,2).astype(f32)/head_width)
    angles=positions.astype(f32)[:,None]*frequencies[None,:]
    cosine,sine=jnp.cos(angles),jnp.sin(angles)
    return jnp.concatenate([cosine,cosine],1),jnp.concatenate([-sine,sine],1)


def slot_plan(ids, order, experts):
    tokens,top=ids.shape
    count=tokens*top
    place=jnp.arange(count,dtype=jnp.int32)
    owner=(order[None,:]//top==jnp.arange(tokens,dtype=jnp.int32)[:,None]).astype(bf16)
    choice=order[:,None]%top==jnp.arange(top,dtype=jnp.int32)[None,:]
    digits=jnp.concatenate([jnp.where(choice,(place//64)[:,None],0),jnp.where(choice,(place%64)[:,None],0)],1).astype(bf16)
    found=mm(owner,digits)
    found=64.0*found[:,:top]+found[:,top:]
    chosen=ids.T[None]==jnp.arange(experts,dtype=jnp.int32)[:,None,None]
    spot=jnp.sum(jnp.where(chosen,found.T[None],0.0),1)
    picked=jnp.any(chosen,1)
    spot=jnp.where(picked,spot,float(count))
    earlier=jnp.sum((spot[:,:,None]<spot[:,None,:]).astype(f32),1)
    return jnp.where(picked,earlier,float(UNCHOSEN))


def chip_spot():
    order=chip_order()
    return jnp.array([order.index(i) for i in range(len(order))],jnp.int32)[lax.axis_index("experts")//2]


def ring_rows(parts, holds=()):
    order=chip_order(); chips=len(order); spot=chip_spot()
    moving=[]
    for step in list(range(1,chips))+[0]:
        total=lax.dynamic_index_in_dim(parts,jnp.array(order,jnp.int32)[(spot-step)%chips],1,False).astype(f32)
        if moving:
            total=total+moving[-1].astype(f32)
        if step==0:
            return total,moving
        total=total.astype(bf16)
        if len(holds)>=len(moving)>0:
            total=hold(total,holds[len(moving)-1])
        moving.append(next_chip(total))


def sum_rows(partial, ring_first, holds=()):
    cols=partial.shape[1]
    square=lax.axis_size("dp")*lax.axis_size("context"); chips=lax.axis_size("experts")//2
    if ring_first:
        part,moving=ring_rows(partial.reshape(square,chips,-1,cols),holds)
        part=part.astype(bf16).reshape(-1,cols)
        return lax.psum_scatter(part,("dp","context"),scatter_dimension=0,tiled=True).astype(f32),moving
    part=lax.psum_scatter(partial,("dp","context"),scatter_dimension=0,tiled=True)
    total,moving=ring_rows(part.reshape(1,chips,-1,cols))
    return total.reshape(-1,cols),part


def shards(hidden_in, segments, expert_ids, placement_order, out_grad, attention_gain, query_weight, key_matrix, value_matrix,
           query_gain, key_gain, out_weight, feedforward_gain, router_weight, gate_weight, up_weight, down_weight):
    tok_rows,model_width=hidden_in.shape[1:]
    head_dim=query_gain.shape[0]
    kv_width=key_matrix.shape[1]
    kv_heads=kv_width//head_dim
    top_count=expert_ids.shape[2]
    local_experts=gate_weight.shape[0]
    all_experts=local_experts*lax.axis_size("experts")
    capacity=tok_rows*top_count//all_experts
    reach=WINDOW//tok_rows
    seq_axes=("context","experts")
    seq_place=lax.axis_index(seq_axes)
    devices=math.prod(lax.axis_size(a) for a in ALL)
    expert_place=lax.axis_index("experts")

    before=()
    packed=[pack_weights(gate_weight,up_weight,down_weight,0)]
    cots=gather_ring(out_grad[0])

    positions=seq_place*tok_rows+jnp.arange(tok_rows,dtype=jnp.int32)
    cos_rows,sin_rows=rope_rows(positions,head_dim)
    attention_input,key_pre,kv=key_value(hidden_in[0],attention_gain,key_matrix,value_matrix,key_gain,cos_rows,sin_rows,deps=(packed[0],))
    for expert in range(1,local_experts):
        packed.append(pack_weights(gate_weight,up_weight,down_weight,expert,deps=(kv,packed[-1])))
    weights=[lax.all_gather(p,("dp","context"),axis=0,tiled=True) for p in packed]
    pieces=[([w],jnp.zeros((1,),jnp.int32)) for w in weights]
    plan=slot_plan(expert_ids[0],placement_order[0,0],all_experts)

    lower=expert_place%2==0
    lane=[kv]
    query_pre,query_rows=project_heads(attention_input,query_weight,query_gain,cos_rows,sin_rows,deps=(packed[-1],))
    for step in range(reach//2):
        lane.append(by_chips(hold(lane[-1],query_rows) if step==1 else lane[-1],1))
    kvs=[kv]
    for near,far in zip(lane[:-1],lane[1:]):
        kvs+=[swap_cores(jnp.where(lower,near,far)),far]
    seg_row=segments[0]
    seg_padded=jnp.concatenate([jnp.full((reach*tok_rows,),-1,jnp.int32),seg_row],0)
    key_segs=lax.dynamic_slice_in_dim(seg_padded,seq_place*tok_rows,(reach+1)*tok_rows,0).reshape(reach+1,tok_rows)[::-1]
    query_segs=key_segs[0]
    attn_mix,inverse=attend(query_rows,kvs,query_segs,key_segs,kv_heads,head_dim,deps=(cots[1][0],))
    middle,sent=project_out(attn_mix,out_weight,hidden_in[0],feedforward_gain,plan.astype(bf16),deps=(cots[2][0],))
    sent=hold(sent,cots[3][0])
    router_rows=router_weight.T
    chips=len(cots)
    steps=list(range(chips))
    ffn_blocks=[(sent,swap_cores(sent))]
    acts=[[] for _ in range(local_experts)]
    out_parts=[{} for _ in range(local_experts)]; back_parts=[{} for _ in range(local_experts)]
    expert_full=[None]*local_experts
    before=(middle,)
    def run(expert, some, *deps):
        nonlocal before
        blocks=[(2*s+i) for s in some for i in range(2)]
        xs=[ffn_blocks[s][i] for s in some for i in range(2)]
        cs=[cots[s][i] for s in some for i in range(2)]
        known=([out_parts[expert-1][k] for k in blocks],[back_parts[expert-1][k] for k in blocks]) if expert else None
        which=(expert_place*local_experts+expert).astype(jnp.int32)[None]
        act,outs,backs=expert_chunk(which,xs,cs,router_rows,*pieces[expert][:2],capacity,known,deps=before+deps)
        acts[expert].append(act)
        out_parts[expert].update(zip(blocks,outs)); back_parts[expert].update(zip(blocks,backs))
        before=(act[4],)
    def grads(expert, *deps):
        nonlocal before
        expert_full[expert]=expert_grads(acts[expert],deps=before+deps)
        before=(expert_full[expert],)
    def part(parts, s):
        return parts[-1][2*s],parts[-1][2*s+1]
    coming=next_chip(sent)
    for s in steps:
        run(0,[s],)
        if s+1<chips:
            coming=hold(coming,*before)
            ffn_blocks.append((coming,swap_cores(coming)))
            if s+2<chips:
                coming=next_chip(coming)
    for expert in range(1,local_experts-1):
        grads(expert-1)
        run(expert,steps[:chips//2]); run(expert,steps[chips//2:])
    last=local_experts-1
    grads(last-1)
    run(last,steps[1:2])
    total=ring_step(part(back_parts,1)).astype(bf16)
    moving=next_chip(total)
    for s in steps[2:]:
        run(last,[s],total)
        if s==2:
            run(last,steps[:1])
        total=ring_step(part(back_parts,s),moving,before).astype(bf16)
        moving=next_chip(total)
    grads(last,total)
    moving=hold(moving,*before)
    back_total=ring_step(part(back_parts,0),moving)
    ffn_in_grad=back_total[:tok_rows]
    gate_grad=(back_total[tok_rows:,:tok_rows]+back_total[tok_rows:,tok_rows:2*tok_rows]).T

    ffn_in=sent[:tok_rows]
    logits=mm(ffn_in,router_weight)
    chosen=plan.T<UNCHOSEN
    gates=jax.nn.softmax(jnp.where(chosen,logits,masked_score),axis=-1)
    logit_grad=(gates*(gate_grad-jnp.sum(gates*gate_grad,-1,keepdims=True))).astype(bf16)
    ffn_in_grad=ffn_in_grad+mm(logit_grad,router_weight,NT)
    router_grad=mm(ffn_in,logit_grad,TN)
    norm_unused,ffn_pull=jax.vjp(rms_scale,middle,feedforward_gain)
    middle_norm_grad,ffn_gain_grad=ffn_pull(ffn_in_grad)
    middle_grad=out_grad[0].astype(f32)+middle_norm_grad
    branch_grad=middle_grad.astype(bf16)
    mix_grad=times_turned(branch_grad,out_weight,bf16,deps=before)

    ff=gate_weight.shape[2]
    expert_low=[lax.psum_scatter(a,("dp","context"),scatter_dimension=0,tiled=True) for a in expert_full]
    expert_rows=[r.astype(f32) for r in expert_low]
    gate_weight_grad=jnp.stack([r[:,:ff] for r in expert_rows]); up_weight_grad=jnp.stack([r[:,ff:2*ff] for r in expert_rows])
    down_weight_grad=jnp.stack([r[:,2*ff:].T for r in expert_rows])

    core=expert_place%2
    core_ref=core.astype(jnp.int32)[None]
    out_part=pooled_grad(core_ref,attn_mix,swap_cores(attn_mix),[branch_grad],[swap_cores(branch_grad)],out_weight.shape[0]//devices,deps=(mix_grad,))
    out_weight_grad,out_low=sum_rows(out_part,False)

    halves=2 if kv_heads%2==0 else 1
    count=kv_heads//halves
    query_parts,gain_parts,key_grads,value_grads=[],[],[],[]
    before=(out_part,expert_low[0])
    for half in range(halves):
        query_part,gain_part,key_parts,value_parts=attend_back(query_rows,kvs,query_segs,key_segs,mix_grad,attn_mix,inverse,query_pre,
            query_gain,cos_rows,sin_rows,kv_heads,head_dim,half*count,count,deps=before)
        query_parts.append(query_part); gain_parts.append(gain_part)
        key_grads.append(key_parts); value_grads.append(value_parts)
        before=(query_part,)
    query_both=[swap_cores(q) for q in query_parts]
    input_other=swap_cores(attention_input)
    query_sum=pooled_grad(core_ref,attention_input,input_other,query_parts,query_both,model_width//devices,deps=before)
    query_weight_grad,_=sum_rows(query_sum,False)

    window=[jnp.concatenate([k[d] for k in key_grads]+[v[d] for v in value_grads],1) for d in range(reach+1)]
    lanes=window[::2]
    for d in range(1,reach,2):
        moved=swap_cores(window[d].astype(bf16)).astype(f32)
        lanes[d//2]+=jnp.where(lower,moved,0.0)
        lanes[d//2+1]+=jnp.where(lower,0.0,moved)
    carry=lanes[-1]
    for own in lanes[-2::-1]:
        carry=by_chips(carry.astype(bf16),-1).astype(f32)+own
    query_pre_grad=jnp.concatenate(query_parts,1)
    query_gain_part=sum(gain_parts)
    value_pre_grad=carry[:,kv_width:].astype(bf16)

    attn_in_part=times_turned(query_pre_grad,query_weight,f32,deps=(query_sum,))
    key_pre_grad,key_gain_part=heads_back(carry[:,:kv_width],key_pre,key_gain,cos_rows,sin_rows,deps=(attn_in_part,))
    attn_in_grad=attn_in_part+mm(key_pre_grad,key_matrix,NT)+mm(value_pre_grad,value_matrix,NT)
    attn_unused,attn_pull=jax.vjp(rms_scale,hidden_in[0].astype(f32),attention_gain)
    x_norm_grad,attn_gain_grad=attn_pull(attn_in_grad)
    input_grad=middle_grad+x_norm_grad

    small=jnp.concatenate([g.reshape(devices,-1) for g in (router_grad,ffn_gain_grad,attn_gain_grad,query_gain_part,key_gain_part)],1)
    pairs=small.reshape(devices//2,2,-1)
    small=lax.dynamic_index_in_dim(pairs,core,1,False)+swap_cores(lax.dynamic_index_in_dim(pairs,1-core,1,False))
    kv_pre_grad=jnp.concatenate([key_pre_grad,value_pre_grad],1)
    kv_part=pooled_grad(core_ref,attention_input,input_other,[kv_pre_grad],[swap_cores(kv_pre_grad)],model_width//devices,
        deps=(attn_in_part,expert_low[-1])).reshape(devices//2,-1,2*kv_width)
    extra=-(-small.shape[1]//(16*2*kv_width))*16
    small=jnp.pad(small.astype(bf16),((0,0),(0,extra*2*kv_width-small.shape[1]))).reshape(devices//2,extra,2*kv_width)
    kv_rows,_=sum_rows(jnp.concatenate([kv_part,small],1).reshape(-1,2*kv_width),False)
    rows=model_width//devices; few=head_dim//devices
    kv_weight_grad=kv_rows[:rows]
    small=kv_rows[rows:].reshape(-1)
    router_weight_grad=small[:rows*all_experts].reshape(rows,all_experts)
    rest=small[rows*all_experts:]

    total=hold(ring_step(part(out_parts,1)).astype(bf16),kv_part)
    for s in steps[2:]:
        total=ring_step(part(out_parts,s),next_chip(total)).astype(bf16)
    block_out=(middle+ring_step(part(out_parts,0),next_chip(total))).astype(bf16)
    return (block_out[None],input_grad[None],rest[rows:2*rows],query_weight_grad,kv_weight_grad[:,:kv_width],kv_weight_grad[:,kv_width:],
        rest[2*rows:2*rows+few],rest[2*rows+few:2*rows+2*few],out_weight_grad,rest[:rows],router_weight_grad,gate_weight_grad,up_weight_grad,
        down_weight_grad)


def solution(mesh):
    tokens=P("dp",("context","experts"),None)
    rows=P(ALL,None); flat=P(ALL)
    tall=P("experts",("dp","context"),None); wide=P("experts",None,("dp","context"))
    in_specs=(tokens,P("dp",None),tokens,tokens,tokens)+(P(),)*9+(tall,tall,wide)
    out_specs=(tokens,tokens,flat,rows,rows,rows,flat,flat,rows,flat,rows,tall,tall,wide)
    return jax.shard_map(shards,mesh=mesh,in_specs=in_specs,out_specs=out_specs,check_vma=False)
```

```python
import functools, math
import jax, jax.numpy as jnp
from jax import lax
import jax.experimental.pallas as pl
import jax.experimental.pallas.tpu as pltpu
from jax.sharding import PartitionSpec as P

f32=jnp.float32; bf16=jnp.bfloat16
WINDOW=1024
norm_eps=1e-6
masked_score=-1e30

def cost(us):
    return pl.CostEstimate(flops=int(us*1.15e9),bytes_accessed=1<<18,transcendentals=0)

VMEM_BYTES=60*1024*1024
NT=(((1,),(1,)),((),()))
NN=(((1,),(0,)),((),()))

def params(steps=1):
    return pltpu.CompilerParams(dimension_semantics=("arbitrary",)*steps, vmem_limit_bytes=VMEM_BYTES)

ANY=pl.BlockSpec(memory_space=pl.ANY)

def mm(a,b,dims=NN):
    return lax.dot_general(a,b,dims,preferred_element_type=f32)

def heads_kernel(count, x_ref, w_ref, gain_ref, cos_ref, sin_ref, *refs):
    pre_ref,out_ref=refs[count:]
    head=gain_ref.shape[1]
    pre=mm(x_ref[...], w_ref[...])
    pre_ref[...]=pre
    gain=gain_ref[...]; cos=cos_ref[...]; sin=sin_ref[...]
    for j in range(pre.shape[1]//head):
        u=pre[:, j*head:(j+1)*head]
        n=u*lax.rsqrt(jnp.mean(u*u,-1,keepdims=True)+norm_eps)*gain
        out_ref[:, j*head:(j+1)*head]=(n*cos+pltpu.roll(n,head//2,1)*sin).astype(bf16)

def project_heads(x, w, gain, cos, sin, tile=512, deps=()):
    rows,depth=x.shape; cols=w.shape[1]; head=gain.shape[0]
    tile=min(tile,cols)
    whole=lambda shape: pl.BlockSpec(shape, lambda i:(0,0))
    return pl.pallas_call(functools.partial(heads_kernel,len(deps)),
        out_shape=(jax.ShapeDtypeStruct((rows,cols),f32),jax.ShapeDtypeStruct((rows,cols),bf16)),
        grid=(cols//tile,),
        in_specs=[whole((rows,depth)),pl.BlockSpec((depth,tile),lambda i:(0,i)),whole((1,head)),whole((rows,head)),whole((rows,head))]+[ANY]*len(deps),
        out_specs=(pl.BlockSpec((rows,tile),lambda i:(0,i)),)*2,
        compiler_params=params(), name="project_heads",
        cost_estimate=cost(13),
    )(x,w,gain[None],cos,sin,*deps)

def attend_kernel(scale, blocks, count, *refs):
    q_ref=refs[0]; k_refs=refs[1:1+blocks]; v_refs=refs[1+blocks:1+2*blocks]
    qseg_ref,kseg_ref=refs[1+2*blocks:3+2*blocks]
    out_ref,inv_ref,bias_ref,vaug_ref=refs[3+2*blocks+count:]
    rows,head=k_refs[0].shape
    @pl.when(pl.program_id(0)==0)
    def _():
        vaug_ref[...]=jnp.ones_like(vaug_ref)
        lead=lax.broadcasted_iota(jnp.int32,(rows,rows),0)-lax.broadcasted_iota(jnp.int32,(rows,rows),1)
        for b in range(blocks):
            gap=lead+b*rows
            ok=(qseg_ref[...]==kseg_ref[b:b+1,:])&(gap>=0)&(gap<WINDOW)
            bias_ref[b]=jnp.where(ok,0.0,masked_score)
    for b in range(blocks):
        vaug_ref[b,:,:head]=v_refs[b][...]
    lane=lax.broadcasted_iota(jnp.int32,(rows,head),1)
    inv_all=jnp.zeros((rows,head),f32)
    for j in range(q_ref.shape[1]//head):
        q=q_ref[:, j*head:(j+1)*head]
        acc=jnp.zeros((rows,2*head),f32)
        for b in range(blocks):
            s=mm(q,k_refs[b][...],NT)
            p=jnp.exp2(s*scale+bias_ref[b]).astype(bf16)
            acc+=mm(p,vaug_ref[b])
        inv=1.0/acc[:,head:]
        out_ref[:, j*head:(j+1)*head]=(acc[:,:head]*inv).astype(bf16)
        inv_all=jnp.where(lane==j,inv,inv_all)
    inv_ref[...]=inv_all

def attend(q, kvs, qseg, ksegs, kv_heads, head, deps=()):
    rows,cols=q.shape; blocks=len(kvs); group=cols//kv_heads
    scale=math.log2(math.e)/math.sqrt(head)
    return pl.pallas_call(functools.partial(attend_kernel,scale,blocks,len(deps)),
        out_shape=(jax.ShapeDtypeStruct((rows,cols),bf16),jax.ShapeDtypeStruct((rows,kv_heads*head),f32)),
        grid=(kv_heads,),
        in_specs=[pl.BlockSpec((rows,group),lambda g:(0,g))]
          +[pl.BlockSpec((rows,head),lambda g:(0,g))]*blocks+[pl.BlockSpec((rows,head),lambda g:(0,kv_heads+g))]*blocks
          +[pl.BlockSpec((rows,1),lambda g:(0,0)),pl.BlockSpec((blocks,rows),lambda g:(0,0))]+[ANY]*len(deps),
        out_specs=(pl.BlockSpec((rows,group),lambda g:(0,g)),pl.BlockSpec((rows,head),lambda g:(0,g))),
        scratch_shapes=[pltpu.VMEM((blocks,rows,rows),f32),pltpu.VMEM((blocks,rows,2*head),bf16)],
        compiler_params=params(), name="attend",
        cost_estimate=cost(16),
    )(q,*kvs,*kvs,qseg[:,None],ksegs,*deps)

def attend_back_kernel(scale, blocks, count, *refs):
    q_ref=refs[0]; k_refs=refs[1:1+blocks]; v_refs=refs[1+blocks:1+2*blocks]
    qseg_ref,kseg_ref,grad_ref,mix_ref,inv_ref,pre_ref,gain_ref,cos_ref,sin_ref=refs[1+2*blocks:10+2*blocks]
    dpre_ref,dgain_ref,dk_ref,dv_ref,bias_ref,vaug_ref=refs[10+2*blocks+count:]
    rows,head=k_refs[0].shape
    soft=scale*math.log(2.0)
    @pl.when(pl.program_id(0)==0)
    def _():
        vaug_ref[...]=jnp.ones_like(vaug_ref)
        lead=lax.broadcasted_iota(jnp.int32,(rows,rows),1)-lax.broadcasted_iota(jnp.int32,(rows,rows),0)
        for b in range(blocks):
            gap=lead+b*rows
            ok=(kseg_ref[:,b:b+1]==qseg_ref[...])&(gap>=0)&(gap<WINDOW)
            bias_ref[b]=jnp.where(ok,0.0,masked_score)
        dgain_ref[...]=jnp.zeros_like(dgain_ref)
    k_turned=[]
    for b in range(blocks):
        vaug_ref[b,:,:head]=v_refs[b][...]
        k_turned.append(k_refs[b][...].T)
    lane=lax.broadcasted_iota(jnp.int32,(rows,head),1)
    gain=gain_ref[...]; cos=cos_ref[...]; sin=sin_ref[...]
    dk_ref[...]=jnp.zeros_like(dk_ref); dv_ref[...]=jnp.zeros_like(dv_ref)
    for j in range(q_ref.shape[1]//head):
        cols=slice(j*head,(j+1)*head)
        q=q_ref[:,cols]
        inv=inv_ref[:,j:j+1]
        grad=grad_ref[:,cols].astype(f32)*inv
        delta=-jnp.sum(grad*mix_ref[:,cols].astype(f32),-1,keepdims=True)
        hi=delta.astype(bf16).astype(f32)
        tail=jnp.where(lane==0,hi,jnp.where(lane==1,delta-hi,0.0)).astype(bf16)
        low=grad.astype(bf16)
        both=jnp.concatenate([low,tail],axis=1)
        turned=jnp.zeros((head,rows),f32)
        for b in range(blocks):
            s=mm(k_refs[b][...],q,NT)
            p=jnp.exp2(s*scale+bias_ref[b])
            d=mm(vaug_ref[b],both,NT)
            ds=(p*d).astype(bf16)
            dk_ref[b]+=mm(ds,q)
            dv_ref[b]+=mm(p.astype(bf16),low)
            turned+=mm(k_turned[b],ds)
        g=turned.T*soft
        g=g*cos+pltpu.roll(g*sin,head//2,1)
        u=pre_ref[:,cols]
        r=lax.rsqrt(jnp.mean(u*u,-1,keepdims=True)+norm_eps)
        n=u*r
        dgain_ref[...]+=jnp.sum(g*n,0,keepdims=True)
        g=g*gain
        dpre_ref[:,cols]=(r*(g-n*jnp.mean(g*n,-1,keepdims=True))).astype(bf16)
    dk_ref[...]*=soft

def attend_back(q, kvs, qseg, ksegs, grad, mix, inv, pre, gain, cos, sin, kv_heads, head, first=0, count=None, deps=()):
    rows,cols=q.shape; blocks=len(kvs); group=cols//kv_heads
    count=count or kv_heads
    scale=math.log2(math.e)/math.sqrt(head)
    wide=lambda: pl.BlockSpec((rows,group),lambda g:(0,first+g))
    part=lambda: pl.BlockSpec((rows,head),lambda g:(0,first+g))
    whole=lambda *shape: pl.BlockSpec(shape,lambda g:(0,)*len(shape))
    return pl.pallas_call(functools.partial(attend_back_kernel,scale,blocks,len(deps)),
        out_shape=(jax.ShapeDtypeStruct((rows,count*group),bf16),jax.ShapeDtypeStruct((1,head),f32),
                   jax.ShapeDtypeStruct((blocks,rows,count*head),f32),jax.ShapeDtypeStruct((blocks,rows,count*head),f32)),
        grid=(count,),
        in_specs=[wide()]+[part()]*blocks+[pl.BlockSpec((rows,head),lambda g:(0,kv_heads+first+g))]*blocks
          +[whole(1,rows),whole(rows,blocks),wide(),wide(),part(),wide(),whole(1,head),whole(rows,head),whole(rows,head)]+[ANY]*len(deps),
        out_specs=(pl.BlockSpec((rows,group),lambda g:(0,g)),whole(1,head),pl.BlockSpec((blocks,rows,head),lambda g:(0,0,g)),pl.BlockSpec((blocks,rows,head),lambda g:(0,0,g))),
        scratch_shapes=[pltpu.VMEM((blocks,rows,rows),f32),pltpu.VMEM((blocks,rows,2*head),bf16)],
        compiler_params=params(), name="attend_back",
        cost_estimate=cost(6+11*count),
    )(q,*kvs,*kvs,qseg[None],ksegs.T,grad,mix,inv,pre,gain[None],cos,sin,*deps)

def heads_back_kernel(count, grad_ref, pre_ref, gain_ref, cos_ref, sin_ref, *refs):
    dpre_ref,dgain_ref=refs[count:]
    head=gain_ref.shape[1]
    total=jnp.zeros((1,head),f32)
    for j in range(pre_ref.shape[1]//head):
        cols=slice(j*head,(j+1)*head)
        g=grad_ref[:,cols]
        g=g*cos_ref[...]+pltpu.roll(g*sin_ref[...],head//2,1)
        u=pre_ref[:,cols]
        r=lax.rsqrt(jnp.mean(u*u,-1,keepdims=True)+norm_eps)
        n=u*r
        total+=jnp.sum(g*n,0,keepdims=True)
        g=g*gain_ref[...]
        dpre_ref[:,cols]=(r*(g-n*jnp.mean(g*n,-1,keepdims=True))).astype(bf16)
    dgain_ref[...]=total

def heads_back(grad, pre, gain, cos, sin, deps=()):
    rows,cols=grad.shape; head=gain.shape[0]
    full=lambda *a: pl.BlockSpec(a,lambda i:(0,0))
    return pl.pallas_call(functools.partial(heads_back_kernel,len(deps)),
        out_shape=(jax.ShapeDtypeStruct((rows,cols),bf16),jax.ShapeDtypeStruct((1,head),f32)),
        grid=(1,),
        in_specs=[full(rows,cols)]*2+[full(1,head),full(rows,head),full(rows,head)]+[ANY]*len(deps),
        out_specs=(full(rows,cols),full(1,head)),
        compiler_params=params(), name="heads_back", cost_estimate=cost(3),
    )(grad,pre,gain[None],cos,sin,*deps)

def key_value_kernel(count, x_ref, in_gain_ref, wk_ref, wv_ref, gain_ref, cos_ref, sin_ref, *refs):
    norm_ref,pre_ref,kv_ref=refs[count:]
    head=gain_ref.shape[1]; width=wk_ref.shape[1]
    x=x_ref[...].astype(f32)
    norm=(x*lax.rsqrt(jnp.mean(x*x,-1,keepdims=True)+norm_eps)*in_gain_ref[...]).astype(bf16)
    norm_ref[...]=norm
    pre=mm(norm,wk_ref[...])
    pre_ref[...]=pre
    gain=gain_ref[...]; cos=cos_ref[...]; sin=sin_ref[...]
    for j in range(width//head):
        u=pre[:, j*head:(j+1)*head]
        n=u*lax.rsqrt(jnp.mean(u*u,-1,keepdims=True)+norm_eps)*gain
        kv_ref[:, j*head:(j+1)*head]=(n*cos+pltpu.roll(n,head//2,1)*sin).astype(bf16)
    kv_ref[:,width:]=mm(norm,wv_ref[...]).astype(bf16)

def key_value(x, in_gain, wk, wv, gain, cos, sin, deps=()):
    rows,depth=x.shape; width=wk.shape[1]; head=gain.shape[0]
    full=lambda a: pl.BlockSpec(a,lambda i:(0,0))
    return pl.pallas_call(functools.partial(key_value_kernel,len(deps)),
        out_shape=(jax.ShapeDtypeStruct((rows,depth),bf16),jax.ShapeDtypeStruct((rows,width),f32),jax.ShapeDtypeStruct((rows,2*width),bf16)),
        grid=(1,),
        in_specs=[full((rows,depth)),full((1,depth)),full((depth,width)),full((depth,width)),full((1,head)),full((rows,head)),full((rows,head))]+[ANY]*len(deps),
        out_specs=(full((rows,depth)),full((rows,width)),full((rows,2*width))),
        compiler_params=params(), name="key_value",
        cost_estimate=cost(5),
    )(x,in_gain[None],wk,wv,gain[None],cos,sin,*deps)

def out_kernel(count, mix_ref, w_ref, x_ref, gain_ref, plan_ref, *refs):
    middle_ref,sent_ref=refs[count:]
    i=pl.program_id(0); tile=w_ref.shape[1]
    rows=mix_ref.shape[0]
    for t in range(middle_ref.shape[1]//tile):
        @pl.when(i==t)
        def _():
            cols=slice(t*tile,(t+1)*tile)
            middle_ref[:,cols]=x_ref[:,cols].astype(f32)+mm(mix_ref[...],w_ref[...])
    @pl.when(i==pl.num_programs(0)-1)
    def _():
        v=middle_ref[...]
        sent_ref[:rows]=(v*lax.rsqrt(jnp.mean(v*v,-1,keepdims=True)+norm_eps)*gain_ref[...]).astype(bf16)
        sent_ref[rows:]=jnp.zeros((sent_ref.shape[0]-rows,sent_ref.shape[1]),bf16)
        sent_ref[rows:,:plan_ref.shape[1]]=plan_ref[...]

def project_out(mix, w, x, gain, plan, tile=512, deps=()):
    rows,depth=mix.shape; width=w.shape[1]; experts=plan.shape[0]
    full=lambda *a: pl.BlockSpec(a,lambda i:(0,0))
    return pl.pallas_call(functools.partial(out_kernel,len(deps)),
        out_shape=(jax.ShapeDtypeStruct((rows,width),f32),jax.ShapeDtypeStruct((rows+experts,width),bf16)),
        grid=(width//tile,),
        in_specs=[full(rows,depth),pl.BlockSpec((depth,tile),lambda i:(0,i)),full(rows,width),full(1,width),full(experts,rows)]+[ANY]*len(deps),
        out_specs=(full(rows,width),full(rows+experts,width)),
        compiler_params=params(), name="project_out", cost_estimate=cost(10),
    )(mix,w,x,gain[None],plan,*deps)

def turned_kernel(parts, count, *refs):
    w_ref=refs[parts]; out_ref=refs[parts+1+count]
    start=0; total=None
    for x_ref in refs[:parts]:
        stop=start+x_ref.shape[1]
        term=mm(x_ref[...],w_ref[:,start:stop],NT)
        total=term if total is None else total+term
        start=stop
    out_ref[...]=total.astype(out_ref.dtype)

def times_turned(xs, w, dtype, tile=512, deps=()):
    rows=xs[0].shape[0]; cols,depth=w.shape
    tile=min(tile,cols)
    return pl.pallas_call(functools.partial(turned_kernel,len(xs),len(deps)),
        out_shape=jax.ShapeDtypeStruct((rows,cols),dtype),
        grid=(cols//tile,),
        in_specs=[pl.BlockSpec(x.shape,lambda i:(0,0)) for x in xs]+[pl.BlockSpec((tile,depth),lambda i:(i,0))]+[ANY]*len(deps),
        out_specs=pl.BlockSpec((rows,tile),lambda i:(0,i)),
        compiler_params=params(), name="times_turned", cost_estimate=cost(11),
    )(*xs,w,*deps)

def hold(value, *deps):
    return pl.pallas_call(lambda *refs: None,
        out_shape=jax.ShapeDtypeStruct(value.shape,value.dtype),
        in_specs=[ANY]*(1+len(deps)), out_specs=ANY, input_output_aliases={0:0},
        name="hold", cost_estimate=cost(0.1),
    )(value,*deps)

TN=(((0,),(0,)),((),()))
UNCHOSEN=1024.0

def pack_kernel(count, gate_ref, up_ref, down_ref, *refs):
    out_ref=refs[count]
    ff=gate_ref.shape[1]
    out_ref[:,:ff]=gate_ref[...]
    out_ref[:,ff:2*ff]=up_ref[...]
    out_ref[:,2*ff:]=down_ref[...].T

def pack_weights(gate, up, down, which, deps=()):
    rows,ff=gate.shape[1:]
    return pl.pallas_call(functools.partial(pack_kernel,len(deps)),
        out_shape=jax.ShapeDtypeStruct((rows,3*ff),bf16),
        grid=(1,),
        in_specs=[pl.BlockSpec((pl.squeezed,rows,ff),lambda i:(which,0,0))]*2+[pl.BlockSpec((pl.squeezed,ff,rows),lambda i:(which,0,0))]+[ANY]*len(deps),
        out_specs=pl.BlockSpec((rows,3*ff),lambda i:(0,0)),
        compiler_params=params(), name="pack_weights",
        cost_estimate=cost(3),
    )(gate,up,down,*deps)

def expert_kernel(capacity, blocks, chained, pieces, count, *refs):
    mine_ref,place_ref=refs[:2]; refs=refs[2:]
    x_refs,c_refs,plan_refs=refs[:blocks],refs[blocks:2*blocks],refs[2*blocks:3*blocks]; refs=refs[3*blocks:]
    prev_out=prev_back=(None,)*blocks
    if chained:
        prev_out,prev_back=refs[:blocks],refs[blocks:2*blocks]; refs=refs[2*blocks:]
    router_ref=refs[0]; weight_refs=refs[1:1+pieces]; refs=refs[1+pieces+count:]
    rows_ref,pair_ref,hid_ref,dgate_ref,dup_ref=refs[:5]; refs=refs[5:]
    out_refs,back_refs=refs[:blocks],refs[blocks:2*blocks]
    kept_ref,sems=refs[2*blocks:]
    experts,tokens=plan_refs[0].shape
    ff=hid_ref.shape[1]
    copies=[[] for _ in range(3)]
    for i in range(3):
        for j,piece in enumerate(weight_refs):
            tall=piece.shape[0]
            spot=pl.ds(pl.multiple_of(place_ref[j],tall),tall)
            copies[i].append(pltpu.make_async_copy(piece.at[:,i*ff:(i+1)*ff],kept_ref.at[i,spot],sems.at[i,j]))
            copies[i][-1].start()
    def ready(i):
        for copy in copies[i]:
            copy.wait()
    hit=lax.broadcasted_iota(jnp.int32,(experts,tokens),0)==mine_ref[0]
    slot_of=lax.broadcasted_iota(jnp.int32,(capacity,tokens),0)
    picks=[];rows=[];cots=[];weights=[]
    for b in range(blocks):
        plan=plan_refs[b][...].astype(f32)
        logits=mm(router_ref[...],x_refs[b][...],NT)
        logits=jnp.where(plan<UNCHOSEN,logits,masked_score)
        e=jnp.exp(logits-jnp.max(logits,0,keepdims=True))
        gates=e/jnp.sum(e,0,keepdims=True)
        slot=jnp.sum(jnp.where(hit,plan,0.0),0,keepdims=True).astype(jnp.int32)
        gate=jnp.sum(jnp.where(hit,gates,0.0),0,keepdims=True)
        on=slot_of==slot
        weights.append(jnp.sum(jnp.where(on,gate,0.0),1,keepdims=True))
        picks.append(jnp.where(on,1.0,0.0).astype(bf16))
        rows.append(mm(picks[b],x_refs[b][...]).astype(bf16))
        cots.append(mm(picks[b],c_refs[b][...]))
    rows=jnp.concatenate(rows,0); cots=jnp.concatenate(cots,0); weights=jnp.concatenate(weights,0)
    rows_ref[...]=rows
    pair=(weights*cots).astype(bf16)
    pair_ref[...]=pair
    ready(0)
    gate_pre=mm(rows,kept_ref[0])
    ready(1)
    up_pre=mm(rows,kept_ref[1])
    sig=jax.nn.sigmoid(gate_pre)
    act=gate_pre*sig
    hidden=(act*up_pre).astype(bf16)
    hid_ref[...]=hidden
    ready(2)
    hidden_grad=mm(pair,kept_ref[2])
    dgate=(hidden_grad*up_pre*sig*(1.0+gate_pre*(1.0-sig))).astype(bf16)
    dup=(hidden_grad*act).astype(bf16)
    dgate_ref[...]=dgate; dup_ref[...]=dup
    back=(mm(dgate,kept_ref[0],NT)+mm(dup,kept_ref[1],NT)).astype(bf16)
    out=mm(hidden,kept_ref[2],NT)
    gate_grad=jnp.sum(out*cots,1,keepdims=True)
    out=(out*weights).astype(bf16)
    for b in range(blocks):
        part=slice(b*capacity,(b+1)*capacity)
        for prev,ref,vals in ((prev_back[b],back_refs[b],back),(prev_out[b],out_refs[b],out)):
            total=mm(picks[b],vals[part],TN)
            if chained:
                total+=prev[:tokens].astype(f32)
            ref[:tokens]=total.astype(bf16)
        grad=jnp.sum(jnp.where(picks[b]>0,gate_grad[part],0.0),0,keepdims=True)
        grad=jnp.where(hit,grad,0.0)
        high=grad.astype(bf16).astype(f32)
        back_refs[b][tokens:]=jnp.zeros((experts,back_refs[b].shape[1]),bf16)
        for i,digit in enumerate((high,grad-high)):
            spot=slice(i*tokens,(i+1)*tokens)
            if chained:
                digit+=prev_back[b][tokens:,spot].astype(f32)
            back_refs[b][tokens:,spot]=digit.astype(bf16)

def expert_chunk(mine, xs, cs, router, pieces, places, capacity, prev=None, deps=()):
    blocks=len(xs); tokens,width=cs[0].shape; ff=pieces[0].shape[1]//3; experts=router.shape[0]
    rows=blocks*capacity
    full=lambda *shape: pl.BlockSpec(shape,lambda i:(0,)*len(shape))
    once=lambda *shape: pl.BlockSpec(shape,lambda i:(0,)*len(shape),pipeline_mode=pl.Buffered(1))
    partial=[jax.ShapeDtypeStruct((tokens,width),bf16)]*blocks
    res=pl.pallas_call(functools.partial(expert_kernel,capacity,blocks,prev is not None,len(pieces),len(deps)),
        out_shape=[jax.ShapeDtypeStruct((rows,width),bf16)]*2+[jax.ShapeDtypeStruct((rows,ff),bf16)]*3
          +partial+[jax.ShapeDtypeStruct((tokens+experts,width),bf16)]*blocks,
        grid=(1,),
        in_specs=[pl.BlockSpec(memory_space=pltpu.SMEM)]*2+[once(tokens,width)]*(2*blocks)
          +[pl.BlockSpec((experts,tokens),lambda i:(tokens//experts,0),pipeline_mode=pl.Buffered(1))]*blocks
          +([once(tokens,width)]*blocks+[once(tokens+experts,width)]*blocks if prev else [])+[once(experts,width)]+[ANY]*(len(pieces)+len(deps)),
        out_specs=[once(rows,width)]*2+[once(rows,ff)]*3+[once(tokens,width)]*blocks+[once(tokens+experts,width)]*blocks,
        scratch_shapes=[pltpu.VMEM((3,width,ff),bf16),pltpu.SemaphoreType.DMA((3,len(pieces)))],
        compiler_params=params(), name="expert_chunk",
        cost_estimate=cost(4+4.7*blocks),
    )(mine,places,*xs,*cs,*xs,*(tuple(prev[0])+tuple(prev[1]) if prev else ()),router,*pieces,*deps)
    return res[:5],res[5:5+blocks],res[5+blocks:]

def expert_grads_kernel(chunks, count, *refs):
    join=lambda i: jnp.concatenate([r[...] for r in refs[i*chunks:(i+1)*chunks]],0)
    rows,pair,hid,dgate,dup=[join(i) for i in range(5)]
    out_ref=refs[5*chunks+count]
    ff=hid.shape[1]
    rows=rows.T; pair=pair.T
    out_ref[:,:ff]=mm(rows,dgate).astype(bf16)
    out_ref[:,ff:2*ff]=mm(rows,dup).astype(bf16)
    out_ref[:,2*ff:]=mm(pair,hid).astype(bf16)

def expert_grads(acts, tile=512, deps=()):
    chunks=len(acts); width=acts[0][0].shape[1]; ff=acts[0][2].shape[1]
    count=sum(a[0].shape[0] for a in acts)
    tall=[pl.BlockSpec((a[0].shape[0],tile),lambda i:(0,i)) for a in acts]
    flat=[pl.BlockSpec((a[0].shape[0],ff),lambda i:(0,0)) for a in acts]
    return pl.pallas_call(functools.partial(expert_grads_kernel,chunks,len(deps)),
        out_shape=jax.ShapeDtypeStruct((width,3*ff),bf16),
        grid=(width//tile,),
        in_specs=tall*2+flat*3+[ANY]*len(deps),
        out_specs=pl.BlockSpec((tile,3*ff),lambda i:(i,0)),
        compiler_params=params(), name="expert_grads",
        cost_estimate=cost(16),
    )(*[a[i] for i in range(5) for a in acts],*deps)


def pooled_kernel(rows, parts, count, *refs):
    core_ref=refs[0]; left=jnp.concatenate([refs[1][...],refs[2][...]],0)
    rights=refs[3:3+2*parts]; out_ref,turned_ref=refs[3+2*parts+count:]
    turned_ref[...]=left.T.reshape(turned_ref.shape)
    pairs=turned_ref.shape[0]//2
    kept=jnp.concatenate([turned_ref[2*i+core_ref[0]] for i in range(pairs)],0)
    start=0
    for p in range(parts):
        right=jnp.concatenate([rights[p][...],rights[parts+p][...]],0)
        out_ref[:,start:start+right.shape[1]]=mm(kept,right).astype(bf16)
        start+=right.shape[1]

def pooled_grad(core, left, left_other, rights, rights_other, rows, tile=512, deps=()):
    tokens,depth=left.shape; parts=len(rights); cols=sum(r.shape[1] for r in rights)
    tile=max(min(tile,depth),2*rows)
    full=[pl.BlockSpec(r.shape,lambda i:(0,0)) for r in rights]
    return pl.pallas_call(functools.partial(pooled_kernel,rows,parts,len(deps)),
        out_shape=jax.ShapeDtypeStruct((depth//2,cols),bf16),
        grid=(depth//tile,),
        in_specs=[pl.BlockSpec(memory_space=pltpu.SMEM)]+[pl.BlockSpec((tokens,tile),lambda i:(0,i))]*2+full*2+[ANY]*len(deps),
        out_specs=pl.BlockSpec((tile//2,cols),lambda i:(i,0)),
        scratch_shapes=[pltpu.VMEM((tile//rows,rows,2*tokens),bf16)],
        compiler_params=params(), name="pooled_grad", cost_estimate=cost(9*depth*cols/8e6),
    )(core,left,left_other,*rights,*rights_other,*deps)


def rows_back_kernel(count, mine_ref, other_ref, moving_ref, middle_ref, gain_ref, sent_ref, router_ref, cot_ref, *refs):
    grad_ref,branch_ref,router_grad_ref,gain_grad_ref=refs[count:]
    tokens=middle_ref.shape[0]
    total=mine_ref[...].astype(f32)+other_ref[...].astype(f32)+moving_ref[...].astype(f32)
    gate_grad=total[tokens:,:tokens]+total[tokens:,tokens:2*tokens]
    rows=sent_ref[:tokens]; router=router_ref[...]
    logits=mm(router,rows,NT)
    logits=jnp.where(sent_ref[tokens:,:tokens].astype(f32)<UNCHOSEN,logits,masked_score)
    e=jnp.exp(logits-jnp.max(logits,0,keepdims=True))
    gates=e/jnp.sum(e,0,keepdims=True)
    logit_grad=(gates*(gate_grad-jnp.sum(gates*gate_grad,0,keepdims=True))).astype(bf16)
    router_grad_ref[...]=mm(logit_grad,rows)
    grad=total[:tokens]+mm(logit_grad,router,TN)
    v=middle_ref[...]
    r=lax.rsqrt(jnp.mean(v*v,-1,keepdims=True)+norm_eps)
    n=v*r
    gain_grad_ref[...]=jnp.sum(grad*n,0,keepdims=True)
    g=grad*gain_ref[...]
    out=cot_ref[...].astype(f32)+r*(g-n*jnp.mean(g*n,-1,keepdims=True))
    grad_ref[...]=out
    branch_ref[...]=out.astype(bf16)

def rows_back(mine, other, moving, middle, gain, sent, router, cot, deps=()):
    tokens,width=middle.shape; experts=router.shape[0]
    full=lambda *a: pl.BlockSpec(a,lambda i:(0,0))
    tall=full(tokens+experts,width); flat=full(tokens,width)
    return pl.pallas_call(functools.partial(rows_back_kernel,len(deps)),
        out_shape=(jax.ShapeDtypeStruct((tokens,width),f32),jax.ShapeDtypeStruct((tokens,width),bf16),
                   jax.ShapeDtypeStruct((experts,width),f32),jax.ShapeDtypeStruct((1,width),f32)),
        grid=(1,),
        in_specs=[tall,tall,tall,flat,full(1,width),tall,full(experts,width),flat]+[ANY]*len(deps),
        out_specs=(flat,flat,full(experts,width),full(1,width)),
        compiler_params=params(), name="rows_back", cost_estimate=cost(6),
    )(mine,other,moving,middle,gain[None],sent,router,cot,*deps)

ALL=("dp","context","experts")


def by_chips(array, step):
    axes=("context","experts")
    length=lax.axis_size(axes)
    return lax.ppermute(array,axes,[(i,i+2*step) for i in range(length) if 0<=i+2*step<length])


def after(value, *others):
    return lax.optimization_barrier((value,)+others)[0]


def swap_cores(array):
    return lax.ppermute(array,"experts",[(i,i^1) for i in range(lax.axis_size("experts"))])


def chip_order():
    chips=lax.axis_size("experts")//2
    return list(range(0,chips,2))+list(range(1,chips,2))[::-1]


def next_chip(array):
    order=chip_order(); chips=len(order)
    return lax.ppermute(array,"experts",[(2*order[i]+c,2*order[(i+1)%chips]+c) for i in range(chips) for c in range(2)])


def gather_ring(array):
    lanes=[array]
    for _ in range(len(chip_order())-1):
        lanes.append(next_chip(lanes[-1]))
    return [(lane,swap_cores(lane)) for lane in lanes]


def ring_step(part, moving=None, holds=()):
    mine,other=part
    if moving is not None:
        other=hold(other,moving,*holds)
    total=mine.astype(f32)+swap_cores(other).astype(f32)
    return total if moving is None else total+moving.astype(f32)


def sum_everywhere(array):
    for axis in ALL:
        length=lax.axis_size(axis); step=1
        while step<length:
            array=array+lax.ppermute(array,axis,[(i,i^step) for i in range(length)])
            step*=2
    return array


def rms_scale(values, norm_gain):
    return values*lax.rsqrt(jnp.mean(values*values,axis=-1,keepdims=True)+norm_eps)*norm_gain


def rope_rows(positions, head_width):
    frequencies=jnp.power(1000000.0,-jnp.arange(0,head_width,2).astype(f32)/head_width)
    angles=positions.astype(f32)[:,None]*frequencies[None,:]
    cosine,sine=jnp.cos(angles),jnp.sin(angles)
    return jnp.concatenate([cosine,cosine],1),jnp.concatenate([-sine,sine],1)


def slot_plan(ids, order, experts):
    tokens,top=ids.shape
    count=tokens*top
    place=jnp.arange(count,dtype=jnp.int32)
    owner=(order[None,:]//top==jnp.arange(tokens,dtype=jnp.int32)[:,None]).astype(bf16)
    choice=order[:,None]%top==jnp.arange(top,dtype=jnp.int32)[None,:]
    digits=jnp.concatenate([jnp.where(choice,(place//64)[:,None],0),jnp.where(choice,(place%64)[:,None],0)],1).astype(bf16)
    found=mm(owner,digits)
    found=64.0*found[:,:top]+found[:,top:]
    chosen=ids.T[None]==jnp.arange(experts,dtype=jnp.int32)[:,None,None]
    spot=jnp.sum(jnp.where(chosen,found.T[None],0.0),1)
    picked=jnp.any(chosen,1)
    spot=jnp.where(picked,spot,float(count))
    earlier=jnp.sum((spot[:,:,None]<spot[:,None,:]).astype(f32),1)
    return jnp.where(picked,earlier,float(UNCHOSEN))


def chip_spot():
    order=chip_order()
    return jnp.array([order.index(i) for i in range(len(order))],jnp.int32)[lax.axis_index("experts")//2]


def ring_rows(parts, holds=()):
    order=chip_order(); chips=len(order); spot=chip_spot()
    moving=[]
    for step in list(range(1,chips))+[0]:
        total=lax.dynamic_index_in_dim(parts,jnp.array(order,jnp.int32)[(spot-step)%chips],1,False).astype(f32)
        if moving:
            total=total+moving[-1].astype(f32)
        if step==0:
            return total,moving
        total=total.astype(bf16)
        if len(holds)>=len(moving)>0:
            total=hold(total,holds[len(moving)-1])
        moving.append(next_chip(total))


def sum_rows(partial, ring_first, *holds):
    cols=partial.shape[1]
    square=lax.axis_size("dp")*lax.axis_size("context"); chips=lax.axis_size("experts")//2
    if ring_first:
        part,moving=ring_rows(partial.reshape(square,chips,-1,cols))
        part=hold(part.astype(bf16).reshape(-1,cols),*holds)
        return lax.psum_scatter(part,("dp","context"),scatter_dimension=0,tiled=True).astype(f32),moving
    part=lax.psum_scatter(partial,("dp","context"),scatter_dimension=0,tiled=True)
    total,moving=ring_rows(part.reshape(1,chips,-1,cols))
    return total.reshape(-1,cols),part


def shards(hidden_in, segments, expert_ids, placement_order, out_grad, attention_gain, query_weight, key_matrix, value_matrix,
           query_gain, key_gain, out_weight, feedforward_gain, router_weight, gate_weight, up_weight, down_weight):
    tok_rows,model_width=hidden_in.shape[1:]
    head_dim=query_gain.shape[0]
    kv_width=key_matrix.shape[1]
    kv_heads=kv_width//head_dim
    top_count=expert_ids.shape[2]
    local_experts=gate_weight.shape[0]
    all_experts=local_experts*lax.axis_size("experts")
    capacity=tok_rows*top_count//all_experts
    reach=WINDOW//tok_rows
    seq_axes=("context","experts")
    seq_place=lax.axis_index(seq_axes)
    devices=math.prod(lax.axis_size(a) for a in ALL)
    expert_place=lax.axis_index("experts")

    before=()
    packed=[pack_weights(gate_weight,up_weight,down_weight,0)]
    cot_lanes=[out_grad[0],next_chip(out_grad[0])]

    positions=seq_place*tok_rows+jnp.arange(tok_rows,dtype=jnp.int32)
    cos_rows,sin_rows=rope_rows(positions,head_dim)
    attention_input,key_pre,kv=key_value(hidden_in[0],attention_gain,key_matrix,value_matrix,key_gain,cos_rows,sin_rows,deps=(packed[0],))
    for expert in range(1,local_experts):
        packed.append(pack_weights(gate_weight,up_weight,down_weight,expert,deps=(kv,packed[-1])))
    weights=[lax.all_gather(p,("dp","context"),axis=0,tiled=True) for p in packed]
    pieces=[([w],jnp.zeros((1,),jnp.int32)) for w in weights]
    plan=slot_plan(expert_ids[0],placement_order[0,0],all_experts)

    lower=expert_place%2==0
    lane=[kv]
    query_pre,query_rows=project_heads(attention_input,query_weight,query_gain,cos_rows,sin_rows,deps=(packed[-1],))
    for step in range(reach//2):
        lane.append(by_chips(hold(lane[-1],query_rows) if step==1 else lane[-1],1))
    cot_lanes[1]=hold(cot_lanes[1],lane[-1])
    for _ in range(len(chip_order())-2):
        cot_lanes.append(next_chip(cot_lanes[-1]))
    cots=[(c,swap_cores(c)) for c in cot_lanes]
    kvs=[lane[0]]
    for near,far in zip(lane[:-1],lane[1:]):
        kvs+=[swap_cores(jnp.where(lower,near,far)),far]
    seg_row=segments[0]
    seg_padded=jnp.concatenate([jnp.full((reach*tok_rows,),-1,jnp.int32),seg_row],0)
    key_segs=lax.dynamic_slice_in_dim(seg_padded,seq_place*tok_rows,(reach+1)*tok_rows,0).reshape(reach+1,tok_rows)[::-1]
    query_segs=key_segs[0]
    attn_mix,inverse=attend(query_rows,kvs,query_segs,key_segs,kv_heads,head_dim)
    middle,sent=project_out(attn_mix,out_weight,hidden_in[0],feedforward_gain,plan.astype(bf16),deps=(cots[2][0],))
    sent=hold(sent,cots[3][0])
    router_rows=router_weight.T
    chips=len(cots)
    steps=list(range(chips))
    ffn_blocks=[(sent,swap_cores(sent))]
    acts=[[] for _ in range(local_experts)]
    out_parts=[{} for _ in range(local_experts)]; back_parts=[{} for _ in range(local_experts)]
    expert_full=[None]*local_experts
    before=(middle,)
    def run(expert, some, *deps):
        nonlocal before
        blocks=[(2*s+i) for s in some for i in range(2)]
        xs=[ffn_blocks[s][i] for s in some for i in range(2)]
        cs=[cots[s][i] for s in some for i in range(2)]
        known=([out_parts[expert-1][k] for k in blocks],[back_parts[expert-1][k] for k in blocks]) if expert else None
        which=(expert_place*local_experts+expert).astype(jnp.int32)[None]
        act,outs,backs=expert_chunk(which,xs,cs,router_rows,*pieces[expert][:2],capacity,known,deps=before+deps)
        acts[expert].append(act)
        out_parts[expert].update(zip(blocks,outs)); back_parts[expert].update(zip(blocks,backs))
        before=(act[4],)
    def grads(expert, *deps):
        nonlocal before
        expert_full[expert]=expert_grads(acts[expert],deps=before+deps)
        before=(expert_full[expert],)
    def part(parts, s):
        return parts[-1][2*s],parts[-1][2*s+1]
    coming=next_chip(sent)
    for s in steps:
        run(0,[s],)
        if s+1<chips:
            coming=hold(coming,*before)
            ffn_blocks.append((coming,swap_cores(coming)))
            if s+2<chips:
                coming=next_chip(coming)
    for expert in range(1,local_experts-1):
        grads(expert-1)
        run(expert,steps[:chips//2]); run(expert,steps[chips//2:])
    last=local_experts-1
    grads(last-1)
    run(last,steps[1:2])
    total=ring_step(part(back_parts,1)).astype(bf16)
    moving=next_chip(total)
    for s in steps[2:]:
        run(last,[s],total)
        if s==2:
            run(last,steps[:1])
        total=ring_step(part(back_parts,s),moving,before).astype(bf16)
        moving=next_chip(total)
    grads(last,total)
    moving=hold(moving,*before)
    mine,other=part(back_parts,0)
    middle_grad,branch_grad,router_grad,ffn_gain_grad=rows_back(mine,swap_cores(other),moving,middle,feedforward_gain,sent,router_rows,out_grad[0])
    router_grad=router_grad.T
    mix_grad=times_turned([branch_grad],out_weight,bf16,deps=before)

    ff=gate_weight.shape[2]
    expert_low=[lax.psum_scatter(a,("dp","context"),scatter_dimension=0,tiled=True) for a in expert_full]
    expert_rows=[r.astype(f32) for r in expert_low]
    gate_weight_grad=jnp.stack([r[:,:ff] for r in expert_rows]); up_weight_grad=jnp.stack([r[:,ff:2*ff] for r in expert_rows])
    down_weight_grad=jnp.stack([r[:,2*ff:].T for r in expert_rows])

    core=expert_place%2
    core_ref=core.astype(jnp.int32)[None]
    out_part=pooled_grad(core_ref,attn_mix,swap_cores(attn_mix),[branch_grad],[swap_cores(branch_grad)],out_weight.shape[0]//devices,deps=(mix_grad,))
    out_low=lax.psum_scatter(out_part,("dp","context"),scatter_dimension=0,tiled=True)

    halves=2 if kv_heads%2==0 else 1
    count=kv_heads//halves
    query_parts,gain_parts,key_grads,value_grads=[],[],[],[]
    before=(out_part,expert_low[0])
    total=hold(ring_step(part(out_parts,1)).astype(bf16),out_part)
    for half in range(halves):
        query_part,gain_part,key_parts,value_parts=attend_back(query_rows,kvs,query_segs,key_segs,mix_grad,attn_mix,inverse,query_pre,
            query_gain,cos_rows,sin_rows,kv_heads,head_dim,half*count,count,deps=before)
        query_parts.append(query_part); gain_parts.append(gain_part)
        key_grads.append(key_parts); value_grads.append(value_parts)
        before=(query_part,)
        if half+2<chips:
            moving=hold(next_chip(total),query_part)
            total=ring_step(part(out_parts,half+2),moving).astype(bf16)
            before+=(total,)
    query_both=[swap_cores(q) for q in query_parts]
    input_other=swap_cores(attention_input)
    query_sum=pooled_grad(core_ref,attention_input,input_other,query_parts,query_both,model_width//devices,deps=before+(expert_low[-1],))
    query_weight_grad,query_low=sum_rows(query_sum,False)

    window=[jnp.concatenate([k[d] for k in key_grads]+[v[d] for v in value_grads],1) for d in range(reach+1)]
    lanes=window[::2]
    for d in range(1,reach,2):
        moved=swap_cores(window[d].astype(bf16)).astype(f32)
        lanes[d//2]+=jnp.where(lower,moved,0.0)
        lanes[d//2+1]+=jnp.where(lower,0.0,moved)
    attn_in_part=times_turned(query_parts,query_weight,f32,deps=(query_sum,))
    carry=lanes[-1].astype(bf16)
    for own,kernel in zip(lanes[-2::-1],(query_sum,attn_in_part)):
        carry=hold(by_chips(carry,-1),kernel).astype(f32)+own
        carry=carry.astype(bf16) if own is not lanes[0] else carry
    query_gain_part=sum(gain_parts)
    value_pre_grad=carry[:,kv_width:].astype(bf16)

    key_pre_grad,key_gain_part=heads_back(carry[:,:kv_width],key_pre,key_gain,cos_rows,sin_rows,deps=(attn_in_part,))
    attn_in_grad=attn_in_part+mm(key_pre_grad,key_matrix,NT)+mm(value_pre_grad,value_matrix,NT)
    attn_unused,attn_pull=jax.vjp(rms_scale,hidden_in[0].astype(f32),attention_gain)
    x_norm_grad,attn_gain_grad=attn_pull(attn_in_grad)
    input_grad=middle_grad+x_norm_grad

    small=jnp.concatenate([g.reshape(devices,-1) for g in (router_grad,ffn_gain_grad,attn_gain_grad,query_gain_part,key_gain_part)],1)
    pairs=small.reshape(devices//2,2,-1)
    small=lax.dynamic_index_in_dim(pairs,core,1,False)+swap_cores(lax.dynamic_index_in_dim(pairs,1-core,1,False))
    kv_pre_grad=jnp.concatenate([key_pre_grad,value_pre_grad],1)
    kv_part=pooled_grad(core_ref,attention_input,input_other,[kv_pre_grad],[swap_cores(kv_pre_grad)],model_width//devices,
        deps=(attn_in_part,expert_low[-1],out_low)).reshape(devices//2,-1,2*kv_width)
    extra=-(-small.shape[1]//(16*2*kv_width))*16
    small=jnp.pad(small.astype(bf16),((0,0),(0,extra*2*kv_width-small.shape[1]))).reshape(devices//2,extra,2*kv_width)
    out_weight_grad,out_sent=ring_rows(out_low.reshape(1,chips,-1,out_low.shape[1]))
    out_weight_grad=out_weight_grad.reshape(-1,out_low.shape[1])
    total=hold(total,carry)
    for s in steps[2+halves:]:
        total=ring_step(part(out_parts,s),next_chip(total)).astype(bf16)
    last_out=next_chip(total)
    block_out=(middle+ring_step(part(out_parts,0),last_out)).astype(bf16)
    kv_rows,_=sum_rows(jnp.concatenate([kv_part,small],1).reshape(-1,2*kv_width),True,query_low,out_sent[-1],last_out)
    rows=model_width//devices; few=head_dim//devices
    kv_weight_grad=kv_rows[:rows]
    small=kv_rows[rows:].reshape(-1)
    router_weight_grad=small[:rows*all_experts].reshape(rows,all_experts)
    rest=small[rows*all_experts:]

    return (block_out[None],input_grad[None],rest[rows:2*rows],query_weight_grad,kv_weight_grad[:,:kv_width],kv_weight_grad[:,kv_width:],
        rest[2*rows:2*rows+few],rest[2*rows+few:2*rows+2*few],out_weight_grad,rest[:rows],router_weight_grad,gate_weight_grad,up_weight_grad,
        down_weight_grad)


def solution(mesh):
    tokens=P("dp",("context","experts"),None)
    rows=P(ALL,None); flat=P(ALL)
    tall=P("experts",("dp","context"),None); wide=P("experts",None,("dp","context"))
    in_specs=(tokens,P("dp",None),tokens,tokens,tokens)+(P(),)*9+(tall,tall,wide)
    out_specs=(tokens,tokens,flat,rows,rows,rows,flat,flat,rows,flat,rows,tall,tall,wide)
    return jax.shard_map(shards,mesh=mesh,in_specs=in_specs,out_specs=out_specs,check_vma=False)
```

```python
import functools, math
import jax, jax.numpy as jnp
from jax import lax
import jax.experimental.pallas as pl
import jax.experimental.pallas.tpu as pltpu
from jax.sharding import PartitionSpec as P

f32=jnp.float32; bf16=jnp.bfloat16
WINDOW=1024
norm_eps=1e-6
masked_score=-1e30

def cost(us):
    return pl.CostEstimate(flops=int(us*1.15e9),bytes_accessed=1<<18,transcendentals=0)

VMEM_BYTES=60*1024*1024
NT=(((1,),(1,)),((),()))
NN=(((1,),(0,)),((),()))

def params(steps=1):
    return pltpu.CompilerParams(dimension_semantics=("arbitrary",)*steps, vmem_limit_bytes=VMEM_BYTES)

ANY=pl.BlockSpec(memory_space=pl.ANY)

def mm(a,b,dims=NN):
    return lax.dot_general(a,b,dims,preferred_element_type=f32)

def heads_kernel(count, x_ref, w_ref, gain_ref, cos_ref, sin_ref, *refs):
    pre_ref,out_ref=refs[count:]
    head=gain_ref.shape[1]
    pre=mm(x_ref[...], w_ref[...])
    pre_ref[...]=pre
    gain=gain_ref[...]; cos=cos_ref[...]; sin=sin_ref[...]
    for j in range(pre.shape[1]//head):
        u=pre[:, j*head:(j+1)*head]
        n=u*lax.rsqrt(jnp.mean(u*u,-1,keepdims=True)+norm_eps)*gain
        out_ref[:, j*head:(j+1)*head]=(n*cos+pltpu.roll(n,head//2,1)*sin).astype(bf16)

def project_heads(x, w, gain, cos, sin, tile=512, deps=()):
    rows,depth=x.shape; cols=w.shape[1]; head=gain.shape[0]
    tile=min(tile,cols)
    whole=lambda shape: pl.BlockSpec(shape, lambda i:(0,0))
    return pl.pallas_call(functools.partial(heads_kernel,len(deps)),
        out_shape=(jax.ShapeDtypeStruct((rows,cols),f32),jax.ShapeDtypeStruct((rows,cols),bf16)),
        grid=(cols//tile,),
        in_specs=[whole((rows,depth)),pl.BlockSpec((depth,tile),lambda i:(0,i)),whole((1,head)),whole((rows,head)),whole((rows,head))]+[ANY]*len(deps),
        out_specs=(pl.BlockSpec((rows,tile),lambda i:(0,i)),)*2,
        compiler_params=params(), name="project_heads",
        cost_estimate=cost(13),
    )(x,w,gain[None],cos,sin,*deps)

def attend_kernel(scale, blocks, count, *refs):
    q_ref=refs[0]; k_refs=refs[1:1+blocks]; v_refs=refs[1+blocks:1+2*blocks]
    qseg_ref,kseg_ref=refs[1+2*blocks:3+2*blocks]
    out_ref,inv_ref,bias_ref,vaug_ref=refs[3+2*blocks+count:]
    rows,head=k_refs[0].shape
    @pl.when(pl.program_id(0)==0)
    def _():
        vaug_ref[...]=jnp.ones_like(vaug_ref)
        lead=lax.broadcasted_iota(jnp.int32,(rows,rows),0)-lax.broadcasted_iota(jnp.int32,(rows,rows),1)
        for b in range(blocks):
            gap=lead+b*rows
            ok=(qseg_ref[...]==kseg_ref[b:b+1,:])&(gap>=0)&(gap<WINDOW)
            bias_ref[b]=jnp.where(ok,0.0,masked_score)
    for b in range(blocks):
        vaug_ref[b,:,:head]=v_refs[b][...]
    lane=lax.broadcasted_iota(jnp.int32,(rows,head),1)
    inv_all=jnp.zeros((rows,head),f32)
    for j in range(q_ref.shape[1]//head):
        q=q_ref[:, j*head:(j+1)*head]
        acc=jnp.zeros((rows,2*head),f32)
        for b in range(blocks):
            s=mm(q,k_refs[b][...],NT)
            p=jnp.exp2(s*scale+bias_ref[b]).astype(bf16)
            acc+=mm(p,vaug_ref[b])
        inv=1.0/acc[:,head:]
        out_ref[:, j*head:(j+1)*head]=(acc[:,:head]*inv).astype(bf16)
        inv_all=jnp.where(lane==j,inv,inv_all)
    inv_ref[...]=inv_all

def attend(q, kvs, qseg, ksegs, kv_heads, head, deps=()):
    rows,cols=q.shape; blocks=len(kvs); group=cols//kv_heads
    scale=math.log2(math.e)/math.sqrt(head)
    return pl.pallas_call(functools.partial(attend_kernel,scale,blocks,len(deps)),
        out_shape=(jax.ShapeDtypeStruct((rows,cols),bf16),jax.ShapeDtypeStruct((rows,kv_heads*head),f32)),
        grid=(kv_heads,),
        in_specs=[pl.BlockSpec((rows,group),lambda g:(0,g))]
          +[pl.BlockSpec((rows,head),lambda g:(0,g))]*blocks+[pl.BlockSpec((rows,head),lambda g:(0,kv_heads+g))]*blocks
          +[pl.BlockSpec((rows,1),lambda g:(0,0)),pl.BlockSpec((blocks,rows),lambda g:(0,0))]+[ANY]*len(deps),
        out_specs=(pl.BlockSpec((rows,group),lambda g:(0,g)),pl.BlockSpec((rows,head),lambda g:(0,g))),
        scratch_shapes=[pltpu.VMEM((blocks,rows,rows),f32),pltpu.VMEM((blocks,rows,2*head),bf16)],
        compiler_params=params(), name="attend",
        cost_estimate=cost(16),
    )(q,*kvs,*kvs,qseg[:,None],ksegs,*deps)

def attend_back_kernel(scale, blocks, count, *refs):
    q_ref=refs[0]; k_refs=refs[1:1+blocks]; v_refs=refs[1+blocks:1+2*blocks]
    qseg_ref,kseg_ref,grad_ref,mix_ref,inv_ref,pre_ref,gain_ref,cos_ref,sin_ref=refs[1+2*blocks:10+2*blocks]
    dpre_ref,dgain_ref,key_ref,value_ref,bias_ref,vaug_ref,dk_ref,dv_ref=refs[10+2*blocks+count:]
    rows,head=k_refs[0].shape
    soft=scale*math.log(2.0)
    @pl.when(pl.program_id(0)==0)
    def _():
        vaug_ref[...]=jnp.ones_like(vaug_ref)
        lead=lax.broadcasted_iota(jnp.int32,(rows,rows),1)-lax.broadcasted_iota(jnp.int32,(rows,rows),0)
        for b in range(blocks):
            gap=lead+b*rows
            ok=(kseg_ref[:,b:b+1]==qseg_ref[...])&(gap>=0)&(gap<WINDOW)
            bias_ref[b]=jnp.where(ok,0.0,masked_score)
        dgain_ref[...]=jnp.zeros_like(dgain_ref)
    k_turned=[]
    for b in range(blocks):
        vaug_ref[b,:,:head]=v_refs[b][...]
        k_turned.append(k_refs[b][...].T)
    lane=lax.broadcasted_iota(jnp.int32,(rows,head),1)
    gain=gain_ref[...]; cos=cos_ref[...]; sin=sin_ref[...]
    dk_ref[...]=jnp.zeros_like(dk_ref); dv_ref[...]=jnp.zeros_like(dv_ref)
    for j in range(q_ref.shape[1]//head):
        cols=slice(j*head,(j+1)*head)
        q=q_ref[:,cols]
        inv=inv_ref[:,j:j+1]
        grad=grad_ref[:,cols].astype(f32)*inv
        delta=-jnp.sum(grad*mix_ref[:,cols].astype(f32),-1,keepdims=True)
        hi=delta.astype(bf16).astype(f32)
        tail=jnp.where(lane==0,hi,jnp.where(lane==1,delta-hi,0.0)).astype(bf16)
        low=grad.astype(bf16)
        both=jnp.concatenate([low,tail],axis=1)
        turned=jnp.zeros((head,rows),f32)
        for b in range(blocks):
            s=mm(k_refs[b][...],q,NT)
            p=jnp.exp2(s*scale+bias_ref[b])
            d=mm(vaug_ref[b],both,NT)
            ds=(p*d).astype(bf16)
            dk_ref[b]+=mm(ds,q)
            dv_ref[b]+=mm(p.astype(bf16),low)
            turned+=mm(k_turned[b],ds)
        g=turned.T*soft
        g=g*cos+pltpu.roll(g*sin,head//2,1)
        u=pre_ref[:,cols]
        r=lax.rsqrt(jnp.mean(u*u,-1,keepdims=True)+norm_eps)
        n=u*r
        dgain_ref[...]+=jnp.sum(g*n,0,keepdims=True)
        g=g*gain
        dpre_ref[:,cols]=(r*(g-n*jnp.mean(g*n,-1,keepdims=True))).astype(bf16)
    key_ref[...]=(dk_ref[...]*soft).astype(bf16)
    value_ref[...]=dv_ref[...].astype(bf16)

def attend_back(q, kvs, qseg, ksegs, grad, mix, inv, pre, gain, cos, sin, kv_heads, head, first=0, count=None, deps=()):
    rows,cols=q.shape; blocks=len(kvs); group=cols//kv_heads
    count=count or kv_heads
    scale=math.log2(math.e)/math.sqrt(head)
    wide=lambda: pl.BlockSpec((rows,group),lambda g:(0,first+g))
    part=lambda: pl.BlockSpec((rows,head),lambda g:(0,first+g))
    whole=lambda *shape: pl.BlockSpec(shape,lambda g:(0,)*len(shape))
    return pl.pallas_call(functools.partial(attend_back_kernel,scale,blocks,len(deps)),
        out_shape=(jax.ShapeDtypeStruct((rows,count*group),bf16),jax.ShapeDtypeStruct((1,head),f32),
                   jax.ShapeDtypeStruct((blocks,rows,count*head),bf16),jax.ShapeDtypeStruct((blocks,rows,count*head),bf16)),
        grid=(count,),
        in_specs=[wide()]+[part()]*blocks+[pl.BlockSpec((rows,head),lambda g:(0,kv_heads+first+g))]*blocks
          +[whole(1,rows),whole(rows,blocks),wide(),wide(),part(),wide(),whole(1,head),whole(rows,head),whole(rows,head)]+[ANY]*len(deps),
        out_specs=(pl.BlockSpec((rows,group),lambda g:(0,g)),whole(1,head),pl.BlockSpec((blocks,rows,head),lambda g:(0,0,g)),pl.BlockSpec((blocks,rows,head),lambda g:(0,0,g))),
        scratch_shapes=[pltpu.VMEM((blocks,rows,rows),f32),pltpu.VMEM((blocks,rows,2*head),bf16)]+[pltpu.VMEM((blocks,rows,head),f32)]*2,
        compiler_params=params(), name="attend_back",
        cost_estimate=cost(6+11*count),
    )(q,*kvs,*kvs,qseg[None],ksegs.T,grad,mix,inv,pre,gain[None],cos,sin,*deps)

def heads_back_kernel(count, grad_ref, pre_ref, gain_ref, cos_ref, sin_ref, *refs):
    dpre_ref,dgain_ref=refs[count:]
    head=gain_ref.shape[1]
    total=jnp.zeros((1,head),f32)
    for j in range(pre_ref.shape[1]//head):
        cols=slice(j*head,(j+1)*head)
        g=grad_ref[:,cols]
        g=g*cos_ref[...]+pltpu.roll(g*sin_ref[...],head//2,1)
        u=pre_ref[:,cols]
        r=lax.rsqrt(jnp.mean(u*u,-1,keepdims=True)+norm_eps)
        n=u*r
        total+=jnp.sum(g*n,0,keepdims=True)
        g=g*gain_ref[...]
        dpre_ref[:,cols]=(r*(g-n*jnp.mean(g*n,-1,keepdims=True))).astype(bf16)
    dgain_ref[...]=total

def heads_back(grad, pre, gain, cos, sin, deps=()):
    rows,cols=grad.shape; head=gain.shape[0]
    full=lambda *a: pl.BlockSpec(a,lambda i:(0,0))
    return pl.pallas_call(functools.partial(heads_back_kernel,len(deps)),
        out_shape=(jax.ShapeDtypeStruct((rows,cols),bf16),jax.ShapeDtypeStruct((1,head),f32)),
        grid=(1,),
        in_specs=[full(rows,cols)]*2+[full(1,head),full(rows,head),full(rows,head)]+[ANY]*len(deps),
        out_specs=(full(rows,cols),full(1,head)),
        compiler_params=params(), name="heads_back", cost_estimate=cost(3),
    )(grad,pre,gain[None],cos,sin,*deps)

def key_value_kernel(count, x_ref, in_gain_ref, wk_ref, wv_ref, gain_ref, cos_ref, sin_ref, *refs):
    norm_ref,pre_ref,kv_ref=refs[count:]
    head=gain_ref.shape[1]; width=wk_ref.shape[1]
    x=x_ref[...].astype(f32)
    norm=(x*lax.rsqrt(jnp.mean(x*x,-1,keepdims=True)+norm_eps)*in_gain_ref[...]).astype(bf16)
    norm_ref[...]=norm
    pre=mm(norm,wk_ref[...])
    pre_ref[...]=pre
    gain=gain_ref[...]; cos=cos_ref[...]; sin=sin_ref[...]
    for j in range(width//head):
        u=pre[:, j*head:(j+1)*head]
        n=u*lax.rsqrt(jnp.mean(u*u,-1,keepdims=True)+norm_eps)*gain
        kv_ref[:, j*head:(j+1)*head]=(n*cos+pltpu.roll(n,head//2,1)*sin).astype(bf16)
    kv_ref[:,width:]=mm(norm,wv_ref[...]).astype(bf16)

def key_value(x, in_gain, wk, wv, gain, cos, sin, deps=()):
    rows,depth=x.shape; width=wk.shape[1]; head=gain.shape[0]
    full=lambda a: pl.BlockSpec(a,lambda i:(0,0))
    return pl.pallas_call(functools.partial(key_value_kernel,len(deps)),
        out_shape=(jax.ShapeDtypeStruct((rows,depth),bf16),jax.ShapeDtypeStruct((rows,width),f32),jax.ShapeDtypeStruct((rows,2*width),bf16)),
        grid=(1,),
        in_specs=[full((rows,depth)),full((1,depth)),full((depth,width)),full((depth,width)),full((1,head)),full((rows,head)),full((rows,head))]+[ANY]*len(deps),
        out_specs=(full((rows,depth)),full((rows,width)),full((rows,2*width))),
        compiler_params=params(), name="key_value",
        cost_estimate=cost(5),
    )(x,in_gain[None],wk,wv,gain[None],cos,sin,*deps)

def out_kernel(count, mix_ref, w_ref, x_ref, gain_ref, plan_ref, *refs):
    middle_ref,sent_ref=refs[count:]
    i=pl.program_id(0); tile=w_ref.shape[1]
    rows=mix_ref.shape[0]
    for t in range(middle_ref.shape[1]//tile):
        @pl.when(i==t)
        def _():
            cols=slice(t*tile,(t+1)*tile)
            middle_ref[:,cols]=x_ref[:,cols].astype(f32)+mm(mix_ref[...],w_ref[...])
    @pl.when(i==pl.num_programs(0)-1)
    def _():
        v=middle_ref[...]
        sent_ref[:rows]=(v*lax.rsqrt(jnp.mean(v*v,-1,keepdims=True)+norm_eps)*gain_ref[...]).astype(bf16)
        sent_ref[rows:]=jnp.zeros((sent_ref.shape[0]-rows,sent_ref.shape[1]),bf16)
        sent_ref[rows:,:plan_ref.shape[1]]=plan_ref[...]

def project_out(mix, w, x, gain, plan, tile=512, deps=()):
    rows,depth=mix.shape; width=w.shape[1]; experts=plan.shape[0]
    full=lambda *a: pl.BlockSpec(a,lambda i:(0,0))
    return pl.pallas_call(functools.partial(out_kernel,len(deps)),
        out_shape=(jax.ShapeDtypeStruct((rows,width),f32),jax.ShapeDtypeStruct((rows+experts,width),bf16)),
        grid=(width//tile,),
        in_specs=[full(rows,depth),pl.BlockSpec((depth,tile),lambda i:(0,i)),full(rows,width),full(1,width),full(experts,rows)]+[ANY]*len(deps),
        out_specs=(full(rows,width),full(rows+experts,width)),
        compiler_params=params(), name="project_out", cost_estimate=cost(10),
    )(mix,w,x,gain[None],plan,*deps)

def turned_kernel(parts, count, *refs):
    w_ref=refs[parts]; out_ref=refs[parts+1+count]
    start=0; total=None
    for x_ref in refs[:parts]:
        stop=start+x_ref.shape[1]
        term=mm(x_ref[...],w_ref[:,start:stop],NT)
        total=term if total is None else total+term
        start=stop
    out_ref[...]=total.astype(out_ref.dtype)

def times_turned(xs, w, dtype, tile=512, deps=()):
    rows=xs[0].shape[0]; cols,depth=w.shape
    tile=min(tile,cols)
    return pl.pallas_call(functools.partial(turned_kernel,len(xs),len(deps)),
        out_shape=jax.ShapeDtypeStruct((rows,cols),dtype),
        grid=(cols//tile,),
        in_specs=[pl.BlockSpec(x.shape,lambda i:(0,0)) for x in xs]+[pl.BlockSpec((tile,depth),lambda i:(i,0))]+[ANY]*len(deps),
        out_specs=pl.BlockSpec((rows,tile),lambda i:(0,i)),
        compiler_params=params(), name="times_turned", cost_estimate=cost(11),
    )(*xs,w,*deps)

def hold(value, *deps):
    return pl.pallas_call(lambda *refs: None,
        out_shape=jax.ShapeDtypeStruct(value.shape,value.dtype),
        in_specs=[ANY]*(1+len(deps)), out_specs=ANY, input_output_aliases={0:0},
        name="hold", cost_estimate=cost(0.1),
    )(value,*deps)

TN=(((0,),(0,)),((),()))
UNCHOSEN=1024.0

def pack_kernel(count, gate_ref, up_ref, down_ref, *refs):
    out_ref=refs[count]
    ff=gate_ref.shape[1]
    out_ref[:,:ff]=gate_ref[...]
    out_ref[:,ff:2*ff]=up_ref[...]
    out_ref[:,2*ff:]=down_ref[...].T

def pack_weights(gate, up, down, which, deps=()):
    rows,ff=gate.shape[1:]
    return pl.pallas_call(functools.partial(pack_kernel,len(deps)),
        out_shape=jax.ShapeDtypeStruct((rows,3*ff),bf16),
        grid=(1,),
        in_specs=[pl.BlockSpec((pl.squeezed,rows,ff),lambda i:(which,0,0))]*2+[pl.BlockSpec((pl.squeezed,ff,rows),lambda i:(which,0,0))]+[ANY]*len(deps),
        out_specs=pl.BlockSpec((rows,3*ff),lambda i:(0,0)),
        compiler_params=params(), name="pack_weights",
        cost_estimate=cost(3),
    )(gate,up,down,*deps)

def expert_kernel(capacity, blocks, chained, pieces, count, *refs):
    mine_ref,place_ref=refs[:2]; refs=refs[2:]
    x_refs,c_refs,plan_refs=refs[:blocks],refs[blocks:2*blocks],refs[2*blocks:3*blocks]; refs=refs[3*blocks:]
    prev_out=prev_back=(None,)*blocks
    if chained:
        prev_out,prev_back=refs[:blocks],refs[blocks:2*blocks]; refs=refs[2*blocks:]
    router_ref=refs[0]; weight_refs=refs[1:1+pieces]; refs=refs[1+pieces+count:]
    rows_ref,pair_ref,hid_ref,dgate_ref,dup_ref=refs[:5]; refs=refs[5:]
    out_refs,back_refs=refs[:blocks],refs[blocks:2*blocks]
    kept_ref,sems=refs[2*blocks:]
    experts,tokens=plan_refs[0].shape
    ff=hid_ref.shape[1]
    copies=[[] for _ in range(3)]
    for i in range(3):
        for j,piece in enumerate(weight_refs):
            tall=piece.shape[0]
            spot=pl.ds(pl.multiple_of(place_ref[j],tall),tall)
            copies[i].append(pltpu.make_async_copy(piece.at[:,i*ff:(i+1)*ff],kept_ref.at[i,spot],sems.at[i,j]))
            copies[i][-1].start()
    def ready(i):
        for copy in copies[i]:
            copy.wait()
    hit=lax.broadcasted_iota(jnp.int32,(experts,tokens),0)==mine_ref[0]
    slot_of=lax.broadcasted_iota(jnp.int32,(capacity,tokens),0)
    picks=[];rows=[];cots=[];weights=[]
    for b in range(blocks):
        plan=plan_refs[b][...].astype(f32)
        logits=mm(router_ref[...],x_refs[b][...],NT)
        logits=jnp.where(plan<UNCHOSEN,logits,masked_score)
        e=jnp.exp(logits-jnp.max(logits,0,keepdims=True))
        gates=e/jnp.sum(e,0,keepdims=True)
        slot=jnp.sum(jnp.where(hit,plan,0.0),0,keepdims=True).astype(jnp.int32)
        gate=jnp.sum(jnp.where(hit,gates,0.0),0,keepdims=True)
        on=slot_of==slot
        weights.append(jnp.sum(jnp.where(on,gate,0.0),1,keepdims=True))
        picks.append(jnp.where(on,1.0,0.0).astype(bf16))
        rows.append(mm(picks[b],x_refs[b][...]).astype(bf16))
        cots.append(mm(picks[b],c_refs[b][...]))
    rows=jnp.concatenate(rows,0); cots=jnp.concatenate(cots,0); weights=jnp.concatenate(weights,0)
    rows_ref[...]=rows
    pair=(weights*cots).astype(bf16)
    pair_ref[...]=pair
    ready(0)
    gate_pre=mm(rows,kept_ref[0])
    ready(1)
    up_pre=mm(rows,kept_ref[1])
    sig=jax.nn.sigmoid(gate_pre)
    act=gate_pre*sig
    hidden=(act*up_pre).astype(bf16)
    hid_ref[...]=hidden
    ready(2)
    hidden_grad=mm(pair,kept_ref[2])
    dgate=(hidden_grad*up_pre*sig*(1.0+gate_pre*(1.0-sig))).astype(bf16)
    dup=(hidden_grad*act).astype(bf16)
    dgate_ref[...]=dgate; dup_ref[...]=dup
    back=(mm(dgate,kept_ref[0],NT)+mm(dup,kept_ref[1],NT)).astype(bf16)
    out=mm(hidden,kept_ref[2],NT)
    gate_grad=jnp.sum(out*cots,1,keepdims=True)
    out=(out*weights).astype(bf16)
    for b in range(blocks):
        part=slice(b*capacity,(b+1)*capacity)
        for prev,ref,vals in ((prev_back[b],back_refs[b],back),(prev_out[b],out_refs[b],out)):
            total=mm(picks[b],vals[part],TN)
            if chained:
                total+=prev[:tokens].astype(f32)
            ref[:tokens]=total.astype(bf16)
        grad=jnp.sum(jnp.where(picks[b]>0,gate_grad[part],0.0),0,keepdims=True)
        grad=jnp.where(hit,grad,0.0)
        high=grad.astype(bf16).astype(f32)
        back_refs[b][tokens:]=jnp.zeros((experts,back_refs[b].shape[1]),bf16)
        for i,digit in enumerate((high,grad-high)):
            spot=slice(i*tokens,(i+1)*tokens)
            if chained:
                digit+=prev_back[b][tokens:,spot].astype(f32)
            back_refs[b][tokens:,spot]=digit.astype(bf16)

def expert_chunk(mine, xs, cs, router, pieces, places, capacity, prev=None, deps=()):
    blocks=len(xs); tokens,width=cs[0].shape; ff=pieces[0].shape[1]//3; experts=router.shape[0]
    rows=blocks*capacity
    full=lambda *shape: pl.BlockSpec(shape,lambda i:(0,)*len(shape))
    once=lambda *shape: pl.BlockSpec(shape,lambda i:(0,)*len(shape),pipeline_mode=pl.Buffered(1))
    partial=[jax.ShapeDtypeStruct((tokens,width),bf16)]*blocks
    res=pl.pallas_call(functools.partial(expert_kernel,capacity,blocks,prev is not None,len(pieces),len(deps)),
        out_shape=[jax.ShapeDtypeStruct((rows,width),bf16)]*2+[jax.ShapeDtypeStruct((rows,ff),bf16)]*3
          +partial+[jax.ShapeDtypeStruct((tokens+experts,width),bf16)]*blocks,
        grid=(1,),
        in_specs=[pl.BlockSpec(memory_space=pltpu.SMEM)]*2+[once(tokens,width)]*(2*blocks)
          +[pl.BlockSpec((experts,tokens),lambda i:(tokens//experts,0),pipeline_mode=pl.Buffered(1))]*blocks
          +([once(tokens,width)]*blocks+[once(tokens+experts,width)]*blocks if prev else [])+[once(experts,width)]+[ANY]*(len(pieces)+len(deps)),
        out_specs=[once(rows,width)]*2+[once(rows,ff)]*3+[once(tokens,width)]*blocks+[once(tokens+experts,width)]*blocks,
        scratch_shapes=[pltpu.VMEM((3,width,ff),bf16),pltpu.SemaphoreType.DMA((3,len(pieces)))],
        compiler_params=params(), name="expert_chunk",
        cost_estimate=cost(4+4.7*blocks),
    )(mine,places,*xs,*cs,*xs,*(tuple(prev[0])+tuple(prev[1]) if prev else ()),router,*pieces,*deps)
    return res[:5],res[5:5+blocks],res[5+blocks:]

def expert_grads_kernel(chunks, count, *refs):
    join=lambda i: jnp.concatenate([r[...] for r in refs[i*chunks:(i+1)*chunks]],0)
    rows,pair,hid,dgate,dup=[join(i) for i in range(5)]
    out_ref=refs[5*chunks+count]
    ff=hid.shape[1]
    rows=rows.T; pair=pair.T
    out_ref[:,:ff]=mm(rows,dgate).astype(bf16)
    out_ref[:,ff:2*ff]=mm(rows,dup).astype(bf16)
    out_ref[:,2*ff:]=mm(pair,hid).astype(bf16)

def expert_grads(acts, tile=512, deps=()):
    chunks=len(acts); width=acts[0][0].shape[1]; ff=acts[0][2].shape[1]
    count=sum(a[0].shape[0] for a in acts)
    tall=[pl.BlockSpec((a[0].shape[0],tile),lambda i:(0,i)) for a in acts]
    flat=[pl.BlockSpec((a[0].shape[0],ff),lambda i:(0,0)) for a in acts]
    return pl.pallas_call(functools.partial(expert_grads_kernel,chunks,len(deps)),
        out_shape=jax.ShapeDtypeStruct((width,3*ff),bf16),
        grid=(width//tile,),
        in_specs=tall*2+flat*3+[ANY]*len(deps),
        out_specs=pl.BlockSpec((tile,3*ff),lambda i:(i,0)),
        compiler_params=params(), name="expert_grads",
        cost_estimate=cost(16),
    )(*[a[i] for i in range(5) for a in acts],*deps)


def pooled_kernel(rows, parts, count, *refs):
    core_ref=refs[0]; left=jnp.concatenate([refs[1][...],refs[2][...]],0)
    rights=refs[3:3+2*parts]; out_ref,turned_ref=refs[3+2*parts+count:]
    turned_ref[...]=left.T.reshape(turned_ref.shape)
    pairs=turned_ref.shape[0]//2
    kept=jnp.concatenate([turned_ref[2*i+core_ref[0]] for i in range(pairs)],0)
    start=0
    for p in range(parts):
        right=jnp.concatenate([rights[p][...],rights[parts+p][...]],0)
        out_ref[:,start:start+right.shape[1]]=mm(kept,right).astype(bf16)
        start+=right.shape[1]

def pooled_grad(core, left, left_other, rights, rights_other, rows, tile=512, deps=()):
    tokens,depth=left.shape; parts=len(rights); cols=sum(r.shape[1] for r in rights)
    tile=max(min(tile,depth),2*rows)
    full=[pl.BlockSpec(r.shape,lambda i:(0,0)) for r in rights]
    return pl.pallas_call(functools.partial(pooled_kernel,rows,parts,len(deps)),
        out_shape=jax.ShapeDtypeStruct((depth//2,cols),bf16),
        grid=(depth//tile,),
        in_specs=[pl.BlockSpec(memory_space=pltpu.SMEM)]+[pl.BlockSpec((tokens,tile),lambda i:(0,i))]*2+full*2+[ANY]*len(deps),
        out_specs=pl.BlockSpec((tile//2,cols),lambda i:(i,0)),
        scratch_shapes=[pltpu.VMEM((tile//rows,rows,2*tokens),bf16)],
        compiler_params=params(), name="pooled_grad", cost_estimate=cost(9*depth*cols/8e6),
    )(core,left,left_other,*rights,*rights_other,*deps)


def rows_back_kernel(count, mine_ref, other_ref, moving_ref, middle_ref, gain_ref, sent_ref, router_ref, cot_ref, *refs):
    grad_ref,branch_ref,router_grad_ref,gain_grad_ref=refs[count:]
    tokens=middle_ref.shape[0]
    total=mine_ref[...].astype(f32)+other_ref[...].astype(f32)+moving_ref[...].astype(f32)
    gate_grad=total[tokens:,:tokens]+total[tokens:,tokens:2*tokens]
    rows=sent_ref[:tokens]; router=router_ref[...]
    logits=mm(router,rows,NT)
    logits=jnp.where(sent_ref[tokens:,:tokens].astype(f32)<UNCHOSEN,logits,masked_score)
    e=jnp.exp(logits-jnp.max(logits,0,keepdims=True))
    gates=e/jnp.sum(e,0,keepdims=True)
    logit_grad=(gates*(gate_grad-jnp.sum(gates*gate_grad,0,keepdims=True))).astype(bf16)
    router_grad_ref[...]=mm(logit_grad,rows)
    grad=total[:tokens]+mm(logit_grad,router,TN)
    v=middle_ref[...]
    r=lax.rsqrt(jnp.mean(v*v,-1,keepdims=True)+norm_eps)
    n=v*r
    gain_grad_ref[...]=jnp.sum(grad*n,0,keepdims=True)
    g=grad*gain_ref[...]
    out=cot_ref[...].astype(f32)+r*(g-n*jnp.mean(g*n,-1,keepdims=True))
    grad_ref[...]=out
    branch_ref[...]=out.astype(bf16)

def rows_back(mine, other, moving, middle, gain, sent, router, cot, deps=()):
    tokens,width=middle.shape; experts=router.shape[0]
    full=lambda *a: pl.BlockSpec(a,lambda i:(0,0))
    tall=full(tokens+experts,width); flat=full(tokens,width)
    return pl.pallas_call(functools.partial(rows_back_kernel,len(deps)),
        out_shape=(jax.ShapeDtypeStruct((tokens,width),f32),jax.ShapeDtypeStruct((tokens,width),bf16),
                   jax.ShapeDtypeStruct((experts,width),f32),jax.ShapeDtypeStruct((1,width),f32)),
        grid=(1,),
        in_specs=[tall,tall,tall,flat,full(1,width),tall,full(experts,width),flat]+[ANY]*len(deps),
        out_specs=(flat,flat,full(experts,width),full(1,width)),
        compiler_params=params(), name="rows_back", cost_estimate=cost(6),
    )(mine,other,moving,middle,gain[None],sent,router,cot,*deps)


def unpack_kernel(count, extra, *refs):
    gate_ref,up_ref,down_ref=refs[count+extra:]
    ff=gate_ref.shape[2]
    for e in range(count):
        gate_ref[e]=refs[e][:,:ff].astype(f32)
        up_ref[e]=refs[e][:,ff:2*ff].astype(f32)
        down_ref[e]=refs[e][:,2*ff:].astype(f32).T

def unpack_grads(lows, deps=()):
    count=len(lows); rows,ff=lows[0].shape[0],lows[0].shape[1]//3
    full=lambda *a: pl.BlockSpec(a,lambda i:(0,)*len(a),pipeline_mode=pl.Buffered(1))
    return pl.pallas_call(functools.partial(unpack_kernel,count,len(deps)),
        out_shape=(jax.ShapeDtypeStruct((count,rows,ff),f32),)*2+(jax.ShapeDtypeStruct((count,ff,rows),f32),),
        grid=(1,),
        in_specs=[full(rows,3*ff)]*count+[ANY]*len(deps),
        out_specs=(full(count,rows,ff),)*2+(full(count,ff,rows),),
        compiler_params=params(), name="unpack_grads", cost_estimate=cost(7),
    )(*lows,*deps)

ALL=("dp","context","experts")


def by_chips(array, step):
    axes=("context","experts")
    length=lax.axis_size(axes)
    return lax.ppermute(array,axes,[(i,i+2*step) for i in range(length) if 0<=i+2*step<length])


def after(value, *others):
    return lax.optimization_barrier((value,)+others)[0]


def swap_cores(array):
    return lax.ppermute(array,"experts",[(i,i^1) for i in range(lax.axis_size("experts"))])


def chip_order():
    chips=lax.axis_size("experts")//2
    return list(range(0,chips,2))+list(range(1,chips,2))[::-1]


def next_chip(array):
    order=chip_order(); chips=len(order)
    return lax.ppermute(array,"experts",[(2*order[i]+c,2*order[(i+1)%chips]+c) for i in range(chips) for c in range(2)])


def gather_ring(array):
    lanes=[array]
    for _ in range(len(chip_order())-1):
        lanes.append(next_chip(lanes[-1]))
    return [(lane,swap_cores(lane)) for lane in lanes]


def ring_step(part, moving=None, holds=()):
    mine,other=part
    if moving is not None:
        other=hold(other,moving,*holds)
    total=mine.astype(f32)+swap_cores(other).astype(f32)
    return total if moving is None else total+moving.astype(f32)


def sum_everywhere(array):
    for axis in ALL:
        length=lax.axis_size(axis); step=1
        while step<length:
            array=array+lax.ppermute(array,axis,[(i,i^step) for i in range(length)])
            step*=2
    return array


def rms_scale(values, norm_gain):
    return values*lax.rsqrt(jnp.mean(values*values,axis=-1,keepdims=True)+norm_eps)*norm_gain


def rope_rows(positions, head_width):
    frequencies=jnp.power(1000000.0,-jnp.arange(0,head_width,2).astype(f32)/head_width)
    angles=positions.astype(f32)[:,None]*frequencies[None,:]
    cosine,sine=jnp.cos(angles),jnp.sin(angles)
    return jnp.concatenate([cosine,cosine],1),jnp.concatenate([-sine,sine],1)


def slot_plan(ids, order, experts):
    tokens,top=ids.shape
    count=tokens*top
    place=jnp.arange(count,dtype=jnp.int32)
    owner=(order[None,:]//top==jnp.arange(tokens,dtype=jnp.int32)[:,None]).astype(bf16)
    choice=order[:,None]%top==jnp.arange(top,dtype=jnp.int32)[None,:]
    digits=jnp.concatenate([jnp.where(choice,(place//64)[:,None],0),jnp.where(choice,(place%64)[:,None],0)],1).astype(bf16)
    found=mm(owner,digits)
    found=64.0*found[:,:top]+found[:,top:]
    chosen=ids.T[None]==jnp.arange(experts,dtype=jnp.int32)[:,None,None]
    spot=jnp.sum(jnp.where(chosen,found.T[None],0.0),1)
    picked=jnp.any(chosen,1)
    spot=jnp.where(picked,spot,float(count))
    earlier=jnp.sum((spot[:,:,None]<spot[:,None,:]).astype(f32),1)
    return jnp.where(picked,earlier,float(UNCHOSEN))


def chip_back(step):
    chips=lax.axis_size("experts")//2
    chip=lax.axis_index("experts")//2
    spot=jnp.where(chip%2==0,chip//2,chips-1-chip//2)
    spot=lax.rem(spot-step+chips,chips)
    return jnp.where(spot<(chips+1)//2,2*spot,2*(chips-1-spot)+1)


def ring_rows(parts, holds=()):
    chips=len(chip_order())
    moving=[]
    for step in list(range(1,chips))+[0]:
        total=lax.dynamic_index_in_dim(parts,chip_back(step),1,False).astype(f32)
        if moving:
            total=total+moving[-1].astype(f32)
        if step==0:
            return total,moving
        total=total.astype(bf16)
        if len(holds)>=len(moving)>0:
            total=hold(total,holds[len(moving)-1])
        moving.append(next_chip(total))


def shards(hidden_in, segments, expert_ids, placement_order, out_grad, attention_gain, query_weight, key_matrix, value_matrix,
           query_gain, key_gain, out_weight, feedforward_gain, router_weight, gate_weight, up_weight, down_weight):
    tok_rows,model_width=hidden_in.shape[1:]
    head_dim=query_gain.shape[0]
    kv_width=key_matrix.shape[1]
    kv_heads=kv_width//head_dim
    top_count=expert_ids.shape[2]
    local_experts=gate_weight.shape[0]
    all_experts=local_experts*lax.axis_size("experts")
    capacity=tok_rows*top_count//all_experts
    reach=WINDOW//tok_rows
    seq_axes=("context","experts")
    seq_place=lax.axis_index(seq_axes)
    devices=math.prod(lax.axis_size(a) for a in ALL)
    expert_place=lax.axis_index("experts")

    before=()
    packed=[pack_weights(gate_weight,up_weight,down_weight,0)]
    cot_lanes=[out_grad[0],next_chip(out_grad[0])]

    positions=seq_place*tok_rows+jnp.arange(tok_rows,dtype=jnp.int32)
    cos_rows,sin_rows=rope_rows(positions,head_dim)
    attention_input,key_pre,kv=key_value(hidden_in[0],attention_gain,key_matrix,value_matrix,key_gain,cos_rows,sin_rows,deps=(packed[0],))
    for expert in range(1,local_experts):
        packed.append(pack_weights(gate_weight,up_weight,down_weight,expert,deps=(kv,packed[-1])))
    weights=[lax.all_gather(p,("dp","context"),axis=0,tiled=True) for p in packed]
    pieces=[([w],jnp.zeros((1,),jnp.int32)) for w in weights]
    plan=slot_plan(expert_ids[0],placement_order[0,0],all_experts)

    lower=expert_place%2==0
    lane=[kv]
    query_pre,query_rows=project_heads(attention_input,query_weight,query_gain,cos_rows,sin_rows,deps=(packed[-1],))
    for step in range(reach//2):
        lane.append(by_chips(hold(lane[-1],query_rows) if step==1 else lane[-1],1))
    cot_lanes[1]=hold(cot_lanes[1],lane[-1])
    for _ in range(len(chip_order())-2):
        cot_lanes.append(next_chip(cot_lanes[-1]))
    cots=[(c,swap_cores(c)) for c in cot_lanes]
    kvs=[lane[0]]
    for near,far in zip(lane[:-1],lane[1:]):
        kvs+=[swap_cores(jnp.where(lower,near,far)),far]
    seg_row=segments[0]
    seg_padded=jnp.concatenate([jnp.full((reach*tok_rows,),-1,jnp.int32),seg_row],0)
    key_segs=lax.dynamic_slice_in_dim(seg_padded,seq_place*tok_rows,(reach+1)*tok_rows,0).reshape(reach+1,tok_rows)[::-1]
    query_segs=key_segs[0]
    attn_mix,inverse=attend(query_rows,kvs,query_segs,key_segs,kv_heads,head_dim)
    middle,sent=project_out(attn_mix,out_weight,hidden_in[0],feedforward_gain,plan.astype(bf16),deps=(cots[2][0],))
    sent=hold(sent,cots[3][0])
    router_rows=router_weight.T
    chips=len(cots)
    steps=list(range(chips))
    ffn_blocks=[(sent,swap_cores(sent))]
    acts=[[] for _ in range(local_experts)]
    out_parts=[{} for _ in range(local_experts)]; back_parts=[{} for _ in range(local_experts)]
    expert_full=[None]*local_experts
    before=(middle,)
    def run(expert, some, *deps):
        nonlocal before
        blocks=[(2*s+i) for s in some for i in range(2)]
        xs=[ffn_blocks[s][i] for s in some for i in range(2)]
        cs=[cots[s][i] for s in some for i in range(2)]
        known=([out_parts[expert-1][k] for k in blocks],[back_parts[expert-1][k] for k in blocks]) if expert else None
        which=(expert_place*local_experts+expert).astype(jnp.int32)[None]
        act,outs,backs=expert_chunk(which,xs,cs,router_rows,*pieces[expert][:2],capacity,known,deps=before+deps)
        acts[expert].append(act)
        out_parts[expert].update(zip(blocks,outs)); back_parts[expert].update(zip(blocks,backs))
        before=(act[4],)
    def grads(expert, *deps):
        nonlocal before
        expert_full[expert]=expert_grads(acts[expert],deps=before+deps)
        before=(expert_full[expert],)
    def part(parts, s):
        return parts[-1][2*s],parts[-1][2*s+1]
    coming=next_chip(sent)
    for s in steps:
        run(0,[s],)
        if s+1<chips:
            coming=hold(coming,*before)
            ffn_blocks.append((coming,swap_cores(coming)))
            if s+2<chips:
                coming=next_chip(coming)
    for expert in range(1,local_experts-1):
        grads(expert-1)
        run(expert,steps[:chips//2]); run(expert,steps[chips//2:])
    last=local_experts-1
    grads(last-1)
    run(last,steps[1:2])
    total=ring_step(part(back_parts,1)).astype(bf16)
    moving=next_chip(total)
    for s in steps[2:]:
        run(last,[s],total)
        if s==2:
            run(last,steps[:1])
        total=ring_step(part(back_parts,s),moving,before).astype(bf16)
        moving=next_chip(total)
    grads(last,total)
    moving=hold(moving,*before)
    mine,other=part(back_parts,0)
    total=hold(ring_step(part(out_parts,1)).astype(bf16),moving)
    out_moving=next_chip(total)
    middle_grad,branch_grad,router_grad,ffn_gain_grad=rows_back(mine,swap_cores(other),moving,middle,feedforward_gain,sent,router_rows,out_grad[0])
    router_grad=router_grad.T
    mix_grad=times_turned([branch_grad],out_weight,bf16,deps=before)
    out_moving=hold(out_moving,mix_grad)

    ff=gate_weight.shape[2]
    expert_low=[lax.psum_scatter(a,("dp","context"),scatter_dimension=0,tiled=True) for a in expert_full]
    core=expert_place%2
    core_ref=core.astype(jnp.int32)[None]
    out_part=pooled_grad(core_ref,attn_mix,swap_cores(attn_mix),[branch_grad],[swap_cores(branch_grad)],out_weight.shape[0]//devices,deps=(mix_grad,out_moving))
    out_low=lax.psum_scatter(out_part,("dp","context"),scatter_dimension=0,tiled=True)

    halves=2 if kv_heads%2==0 else 1
    count=kv_heads//halves
    query_parts,gain_parts,key_grads,value_grads=[],[],[],[]
    before=(out_part,expert_low[0])
    last_kernel=(out_part,)
    for half in range(halves):
        query_part,gain_part,key_parts,value_parts=attend_back(query_rows,kvs,query_segs,key_segs,mix_grad,attn_mix,inverse,query_pre,
            query_gain,cos_rows,sin_rows,kv_heads,head_dim,half*count,count,deps=before)
        query_parts.append(query_part); gain_parts.append(gain_part)
        key_grads.append(key_parts); value_grads.append(value_parts)
        before=(query_part,)
        if half+2<chips:
            total=hold(ring_step(part(out_parts,half+2),out_moving).astype(bf16),*last_kernel)
            out_moving=hold(next_chip(total),query_part)
            before+=(out_moving,)
        last_kernel=(query_part,)
    query_both=[swap_cores(q) for q in query_parts]
    input_other=swap_cores(attention_input)
    query_sum=pooled_grad(core_ref,attention_input,input_other,query_parts,query_both,model_width//devices,deps=before+(expert_low[-1],))
    query_low=lax.psum_scatter(query_sum,("dp","context"),scatter_dimension=0,tiled=True)

    window=[jnp.concatenate([k[d] for k in key_grads]+[v[d] for v in value_grads],1) for d in range(reach+1)]
    lanes=[w.astype(f32) for w in window[::2]]
    for d in range(1,reach,2):
        moved=swap_cores(window[d]).astype(f32)
        lanes[d//2]+=jnp.where(lower,moved,0.0)
        lanes[d//2+1]+=jnp.where(lower,0.0,moved)
    attn_in_part=times_turned(query_parts,query_weight,f32,deps=(query_sum,))
    carry=lanes[-1].astype(bf16)
    for own,kernel in zip(lanes[-2::-1],(query_sum,attn_in_part)):
        carry=hold(by_chips(carry,-1),kernel).astype(f32)+own
        carry=carry.astype(bf16) if own is not lanes[0] else carry
    query_gain_part=sum(gain_parts)
    value_pre_grad=carry[:,kv_width:].astype(bf16)

    key_pre_grad,key_gain_part=heads_back(carry[:,:kv_width],key_pre,key_gain,cos_rows,sin_rows,deps=(attn_in_part,))
    attn_in_grad=attn_in_part+mm(key_pre_grad,key_matrix,NT)+mm(value_pre_grad,value_matrix,NT)
    attn_unused,attn_pull=jax.vjp(rms_scale,hidden_in[0].astype(f32),attention_gain)
    x_norm_grad,attn_gain_grad=attn_pull(attn_in_grad)
    input_grad=middle_grad+x_norm_grad

    small=jnp.concatenate([g.reshape(devices,-1) for g in (router_grad,ffn_gain_grad,attn_gain_grad,query_gain_part,key_gain_part)],1)
    pairs=small.reshape(devices//2,2,-1)
    small=lax.dynamic_index_in_dim(pairs,core,1,False)+swap_cores(lax.dynamic_index_in_dim(pairs,1-core,1,False))
    kv_pre_grad=jnp.concatenate([key_pre_grad,value_pre_grad],1)
    kv_part=pooled_grad(core_ref,attention_input,input_other,[kv_pre_grad],[swap_cores(kv_pre_grad)],model_width//devices,
        deps=(attn_in_part,expert_low[-1],out_low)).reshape(devices//2,-1,2*kv_width)
    gate_weight_grad,up_weight_grad,down_weight_grad=unpack_grads(expert_low,deps=(kv_part,))
    extra=-(-small.shape[1]//(16*2*kv_width))*16
    small=jnp.pad(small.astype(bf16),((0,0),(0,extra*2*kv_width-small.shape[1]))).reshape(devices//2,extra,2*kv_width)
    out_weight_grad,out_sent=ring_rows(out_low.reshape(1,chips,-1,out_low.shape[1]))
    out_weight_grad=out_weight_grad.reshape(-1,out_low.shape[1])
    assert chips-2<=halves
    block_out=(middle+ring_step(part(out_parts,0),out_moving)).astype(bf16)
    kv_sum,_=ring_rows(jnp.concatenate([kv_part,small],1).reshape(-1,chips,kv_part.shape[1]+extra,2*kv_width))
    kv_sum=kv_sum.astype(bf16).reshape(-1,2*kv_width)
    query_weight_grad,_=ring_rows(hold(query_low,kv_sum,out_sent[-1],gate_weight_grad).reshape(1,chips,-1,query_low.shape[1]))
    query_weight_grad=query_weight_grad.reshape(-1,query_low.shape[1])
    kv_rows=lax.psum_scatter(hold(kv_sum,query_low),("dp","context"),scatter_dimension=0,tiled=True).astype(f32)
    rows=model_width//devices; few=head_dim//devices
    kv_weight_grad=kv_rows[:rows]
    small=kv_rows[rows:].reshape(-1)
    router_weight_grad=small[:rows*all_experts].reshape(rows,all_experts)
    rest=small[rows*all_experts:]

    return (block_out[None],input_grad[None],rest[rows:2*rows],query_weight_grad,kv_weight_grad[:,:kv_width],kv_weight_grad[:,kv_width:],
        rest[2*rows:2*rows+few],rest[2*rows+few:2*rows+2*few],out_weight_grad,rest[:rows],router_weight_grad,gate_weight_grad,up_weight_grad,
        down_weight_grad)


def solution(mesh):
    tokens=P("dp",("context","experts"),None)
    rows=P(ALL,None); flat=P(ALL)
    tall=P("experts",("dp","context"),None); wide=P("experts",None,("dp","context"))
    in_specs=(tokens,P("dp",None),tokens,tokens,tokens)+(P(),)*9+(tall,tall,wide)
    out_specs=(tokens,tokens,flat,rows,rows,rows,flat,flat,rows,flat,rows,tall,tall,wide)
    return jax.shard_map(shards,mesh=mesh,in_specs=in_specs,out_specs=out_specs,check_vma=False)
```

```python
import functools, math
import jax, jax.numpy as jnp
from jax import lax
import jax.experimental.pallas as pl
import jax.experimental.pallas.tpu as pltpu
from jax.sharding import PartitionSpec as P

f32=jnp.float32; bf16=jnp.bfloat16
WINDOW=1024
norm_eps=1e-6
masked_score=-1e30

def cost(us):
    return pl.CostEstimate(flops=int(us*1.15e9),bytes_accessed=1<<18,transcendentals=0)

VMEM_BYTES=60*1024*1024
NT=(((1,),(1,)),((),()))
NN=(((1,),(0,)),((),()))

def params(steps=1):
    return pltpu.CompilerParams(dimension_semantics=("arbitrary",)*steps, vmem_limit_bytes=VMEM_BYTES)

ANY=pl.BlockSpec(memory_space=pl.ANY)

def mm(a,b,dims=NN):
    return lax.dot_general(a,b,dims,preferred_element_type=f32)

def heads_kernel(count, x_ref, w_ref, gain_ref, cos_ref, sin_ref, *refs):
    pre_ref,out_ref=refs[count:]
    head=gain_ref.shape[1]
    pre=mm(x_ref[...], w_ref[...])
    pre_ref[...]=pre
    gain=gain_ref[...]; cos=cos_ref[...]; sin=sin_ref[...]
    for j in range(pre.shape[1]//head):
        u=pre[:, j*head:(j+1)*head]
        n=u*lax.rsqrt(jnp.mean(u*u,-1,keepdims=True)+norm_eps)*gain
        out_ref[:, j*head:(j+1)*head]=(n*cos+pltpu.roll(n,head//2,1)*sin).astype(bf16)

def project_heads(x, w, gain, cos, sin, tile=512, deps=()):
    rows,depth=x.shape; cols=w.shape[1]; head=gain.shape[0]
    tile=min(tile,cols)
    whole=lambda shape: pl.BlockSpec(shape, lambda i:(0,0))
    return pl.pallas_call(functools.partial(heads_kernel,len(deps)),
        out_shape=(jax.ShapeDtypeStruct((rows,cols),f32),jax.ShapeDtypeStruct((rows,cols),bf16)),
        grid=(cols//tile,),
        in_specs=[whole((rows,depth)),pl.BlockSpec((depth,tile),lambda i:(0,i)),whole((1,head)),whole((rows,head)),whole((rows,head))]+[ANY]*len(deps),
        out_specs=(pl.BlockSpec((rows,tile),lambda i:(0,i)),)*2,
        compiler_params=params(), name="project_heads",
        cost_estimate=cost(13),
    )(x,w,gain[None],cos,sin,*deps)

def attend_kernel(scale, blocks, count, *refs):
    q_ref=refs[0]; k_refs=refs[1:1+blocks]; v_refs=refs[1+blocks:1+2*blocks]
    qseg_ref,kseg_ref=refs[1+2*blocks:3+2*blocks]
    out_ref,inv_ref,bias_ref,vaug_ref=refs[3+2*blocks+count:]
    rows,head=k_refs[0].shape
    @pl.when(pl.program_id(0)==0)
    def _():
        vaug_ref[...]=jnp.ones_like(vaug_ref)
        lead=lax.broadcasted_iota(jnp.int32,(rows,rows),0)-lax.broadcasted_iota(jnp.int32,(rows,rows),1)
        for b in range(blocks):
            gap=lead+b*rows
            ok=(qseg_ref[...]==kseg_ref[b:b+1,:])&(gap>=0)&(gap<WINDOW)
            bias_ref[b]=jnp.where(ok,0.0,masked_score)
    for b in range(blocks):
        vaug_ref[b,:,:head]=v_refs[b][...]
    lane=lax.broadcasted_iota(jnp.int32,(rows,head),1)
    inv_all=jnp.zeros((rows,head),f32)
    for j in range(q_ref.shape[1]//head):
        q=q_ref[:, j*head:(j+1)*head]
        acc=jnp.zeros((rows,2*head),f32)
        for b in range(blocks):
            s=mm(q,k_refs[b][...],NT)
            p=jnp.exp2(s*scale+bias_ref[b]).astype(bf16)
            acc+=mm(p,vaug_ref[b])
        inv=1.0/acc[:,head:]
        out_ref[:, j*head:(j+1)*head]=(acc[:,:head]*inv).astype(bf16)
        inv_all=jnp.where(lane==j,inv,inv_all)
    inv_ref[...]=inv_all

def attend(q, kvs, qseg, ksegs, kv_heads, head, deps=()):
    rows,cols=q.shape; blocks=len(kvs); group=cols//kv_heads
    scale=math.log2(math.e)/math.sqrt(head)
    return pl.pallas_call(functools.partial(attend_kernel,scale,blocks,len(deps)),
        out_shape=(jax.ShapeDtypeStruct((rows,cols),bf16),jax.ShapeDtypeStruct((rows,kv_heads*head),f32)),
        grid=(kv_heads,),
        in_specs=[pl.BlockSpec((rows,group),lambda g:(0,g))]
          +[pl.BlockSpec((rows,head),lambda g:(0,g))]*blocks+[pl.BlockSpec((rows,head),lambda g:(0,kv_heads+g))]*blocks
          +[pl.BlockSpec((rows,1),lambda g:(0,0)),pl.BlockSpec((blocks,rows),lambda g:(0,0))]+[ANY]*len(deps),
        out_specs=(pl.BlockSpec((rows,group),lambda g:(0,g)),pl.BlockSpec((rows,head),lambda g:(0,g))),
        scratch_shapes=[pltpu.VMEM((blocks,rows,rows),f32),pltpu.VMEM((blocks,rows,2*head),bf16)],
        compiler_params=params(), name="attend",
        cost_estimate=cost(16),
    )(q,*kvs,*kvs,qseg[:,None],ksegs,*deps)

def attend_back_kernel(scale, blocks, count, *refs):
    q_ref=refs[0]; k_refs=refs[1:1+blocks]; v_refs=refs[1+blocks:1+2*blocks]
    qseg_ref,kseg_ref,grad_ref,mix_ref,inv_ref,pre_ref,gain_ref,cos_ref,sin_ref=refs[1+2*blocks:10+2*blocks]
    dpre_ref,dgain_ref,key_ref,value_ref,bias_ref,vaug_ref,dk_ref,dv_ref=refs[10+2*blocks+count:]
    rows,head=k_refs[0].shape
    soft=scale*math.log(2.0)
    @pl.when(pl.program_id(0)==0)
    def _():
        vaug_ref[...]=jnp.ones_like(vaug_ref)
        lead=lax.broadcasted_iota(jnp.int32,(rows,rows),1)-lax.broadcasted_iota(jnp.int32,(rows,rows),0)
        for b in range(blocks):
            gap=lead+b*rows
            ok=(kseg_ref[:,b:b+1]==qseg_ref[...])&(gap>=0)&(gap<WINDOW)
            bias_ref[b]=jnp.where(ok,0.0,masked_score)
        dgain_ref[...]=jnp.zeros_like(dgain_ref)
    k_turned=[]
    for b in range(blocks):
        vaug_ref[b,:,:head]=v_refs[b][...]
        k_turned.append(k_refs[b][...].T)
    lane=lax.broadcasted_iota(jnp.int32,(rows,head),1)
    gain=gain_ref[...]; cos=cos_ref[...]; sin=sin_ref[...]
    dk_ref[...]=jnp.zeros_like(dk_ref); dv_ref[...]=jnp.zeros_like(dv_ref)
    for j in range(q_ref.shape[1]//head):
        cols=slice(j*head,(j+1)*head)
        q=q_ref[:,cols]
        inv=inv_ref[:,j:j+1]
        grad=grad_ref[:,cols].astype(f32)*inv
        delta=-jnp.sum(grad*mix_ref[:,cols].astype(f32),-1,keepdims=True)
        hi=delta.astype(bf16).astype(f32)
        tail=jnp.where(lane==0,hi,jnp.where(lane==1,delta-hi,0.0)).astype(bf16)
        low=grad.astype(bf16)
        both=jnp.concatenate([low,tail],axis=1)
        turned=jnp.zeros((head,rows),f32)
        for b in range(blocks):
            s=mm(k_refs[b][...],q,NT)
            p=jnp.exp2(s*scale+bias_ref[b])
            d=mm(vaug_ref[b],both,NT)
            ds=(p*d).astype(bf16)
            dk_ref[b]+=mm(ds,q)
            dv_ref[b]+=mm(p.astype(bf16),low)
            turned+=mm(k_turned[b],ds)
        g=turned.T*soft
        g=g*cos+pltpu.roll(g*sin,head//2,1)
        u=pre_ref[:,cols]
        r=lax.rsqrt(jnp.mean(u*u,-1,keepdims=True)+norm_eps)
        n=u*r
        dgain_ref[...]+=jnp.sum(g*n,0,keepdims=True)
        g=g*gain
        dpre_ref[:,cols]=(r*(g-n*jnp.mean(g*n,-1,keepdims=True))).astype(bf16)
    key_ref[...]=(dk_ref[...]*soft).astype(bf16)
    value_ref[...]=dv_ref[...].astype(bf16)

def attend_back(q, kvs, qseg, ksegs, grad, mix, inv, pre, gain, cos, sin, kv_heads, head, first=0, count=None, deps=()):
    rows,cols=q.shape; blocks=len(kvs); group=cols//kv_heads
    count=count or kv_heads
    scale=math.log2(math.e)/math.sqrt(head)
    wide=lambda: pl.BlockSpec((rows,group),lambda g:(0,first+g))
    part=lambda: pl.BlockSpec((rows,head),lambda g:(0,first+g))
    whole=lambda *shape: pl.BlockSpec(shape,lambda g:(0,)*len(shape))
    return pl.pallas_call(functools.partial(attend_back_kernel,scale,blocks,len(deps)),
        out_shape=(jax.ShapeDtypeStruct((rows,count*group),bf16),jax.ShapeDtypeStruct((1,head),f32),
                   jax.ShapeDtypeStruct((blocks,rows,count*head),bf16),jax.ShapeDtypeStruct((blocks,rows,count*head),bf16)),
        grid=(count,),
        in_specs=[wide()]+[part()]*blocks+[pl.BlockSpec((rows,head),lambda g:(0,kv_heads+first+g))]*blocks
          +[whole(1,rows),whole(rows,blocks),wide(),wide(),part(),wide(),whole(1,head),whole(rows,head),whole(rows,head)]+[ANY]*len(deps),
        out_specs=(pl.BlockSpec((rows,group),lambda g:(0,g)),whole(1,head),pl.BlockSpec((blocks,rows,head),lambda g:(0,0,g)),pl.BlockSpec((blocks,rows,head),lambda g:(0,0,g))),
        scratch_shapes=[pltpu.VMEM((blocks,rows,rows),f32),pltpu.VMEM((blocks,rows,2*head),bf16)]+[pltpu.VMEM((blocks,rows,head),f32)]*2,
        compiler_params=params(), name="attend_back",
        cost_estimate=cost(6+11*count),
    )(q,*kvs,*kvs,qseg[None],ksegs.T,grad,mix,inv,pre,gain[None],cos,sin,*deps)

def heads_back_kernel(count, grad_ref, pre_ref, gain_ref, cos_ref, sin_ref, *refs):
    dpre_ref,dgain_ref=refs[count:]
    head=gain_ref.shape[1]
    total=jnp.zeros((1,head),f32)
    for j in range(pre_ref.shape[1]//head):
        cols=slice(j*head,(j+1)*head)
        g=grad_ref[:,cols]
        g=g*cos_ref[...]+pltpu.roll(g*sin_ref[...],head//2,1)
        u=pre_ref[:,cols]
        r=lax.rsqrt(jnp.mean(u*u,-1,keepdims=True)+norm_eps)
        n=u*r
        total+=jnp.sum(g*n,0,keepdims=True)
        g=g*gain_ref[...]
        dpre_ref[:,cols]=(r*(g-n*jnp.mean(g*n,-1,keepdims=True))).astype(bf16)
    dgain_ref[...]=total

def heads_back(grad, pre, gain, cos, sin, deps=()):
    rows,cols=grad.shape; head=gain.shape[0]
    full=lambda *a: pl.BlockSpec(a,lambda i:(0,0))
    return pl.pallas_call(functools.partial(heads_back_kernel,len(deps)),
        out_shape=(jax.ShapeDtypeStruct((rows,cols),bf16),jax.ShapeDtypeStruct((1,head),f32)),
        grid=(1,),
        in_specs=[full(rows,cols)]*2+[full(1,head),full(rows,head),full(rows,head)]+[ANY]*len(deps),
        out_specs=(full(rows,cols),full(1,head)),
        compiler_params=params(), name="heads_back", cost_estimate=cost(3),
    )(grad,pre,gain[None],cos,sin,*deps)

def key_value_kernel(count, x_ref, in_gain_ref, wk_ref, wv_ref, gain_ref, cos_ref, sin_ref, *refs):
    norm_ref,pre_ref,kv_ref=refs[count:]
    head=gain_ref.shape[1]; width=wk_ref.shape[1]
    x=x_ref[...].astype(f32)
    norm=(x*lax.rsqrt(jnp.mean(x*x,-1,keepdims=True)+norm_eps)*in_gain_ref[...]).astype(bf16)
    norm_ref[...]=norm
    pre=mm(norm,wk_ref[...])
    pre_ref[...]=pre
    gain=gain_ref[...]; cos=cos_ref[...]; sin=sin_ref[...]
    for j in range(width//head):
        u=pre[:, j*head:(j+1)*head]
        n=u*lax.rsqrt(jnp.mean(u*u,-1,keepdims=True)+norm_eps)*gain
        kv_ref[:, j*head:(j+1)*head]=(n*cos+pltpu.roll(n,head//2,1)*sin).astype(bf16)
    kv_ref[:,width:]=mm(norm,wv_ref[...]).astype(bf16)

def key_value(x, in_gain, wk, wv, gain, cos, sin, deps=()):
    rows,depth=x.shape; width=wk.shape[1]; head=gain.shape[0]
    full=lambda a: pl.BlockSpec(a,lambda i:(0,0))
    return pl.pallas_call(functools.partial(key_value_kernel,len(deps)),
        out_shape=(jax.ShapeDtypeStruct((rows,depth),bf16),jax.ShapeDtypeStruct((rows,width),f32),jax.ShapeDtypeStruct((rows,2*width),bf16)),
        grid=(1,),
        in_specs=[full((rows,depth)),full((1,depth)),full((depth,width)),full((depth,width)),full((1,head)),full((rows,head)),full((rows,head))]+[ANY]*len(deps),
        out_specs=(full((rows,depth)),full((rows,width)),full((rows,2*width))),
        compiler_params=params(), name="key_value",
        cost_estimate=cost(5),
    )(x,in_gain[None],wk,wv,gain[None],cos,sin,*deps)

def out_kernel(count, mix_ref, w_ref, x_ref, gain_ref, plan_ref, *refs):
    middle_ref,sent_ref=refs[count:]
    i=pl.program_id(0); tile=w_ref.shape[1]
    rows=mix_ref.shape[0]
    for t in range(middle_ref.shape[1]//tile):
        @pl.when(i==t)
        def _():
            cols=slice(t*tile,(t+1)*tile)
            middle_ref[:,cols]=x_ref[:,cols].astype(f32)+mm(mix_ref[...],w_ref[...])
    @pl.when(i==pl.num_programs(0)-1)
    def _():
        v=middle_ref[...]
        sent_ref[:rows]=(v*lax.rsqrt(jnp.mean(v*v,-1,keepdims=True)+norm_eps)*gain_ref[...]).astype(bf16)
        sent_ref[rows:]=jnp.zeros((sent_ref.shape[0]-rows,sent_ref.shape[1]),bf16)
        sent_ref[rows:,:plan_ref.shape[1]]=plan_ref[...]

def project_out(mix, w, x, gain, plan, tile=512, deps=()):
    rows,depth=mix.shape; width=w.shape[1]; experts=plan.shape[0]
    full=lambda *a: pl.BlockSpec(a,lambda i:(0,0))
    return pl.pallas_call(functools.partial(out_kernel,len(deps)),
        out_shape=(jax.ShapeDtypeStruct((rows,width),f32),jax.ShapeDtypeStruct((rows+experts,width),bf16)),
        grid=(width//tile,),
        in_specs=[full(rows,depth),pl.BlockSpec((depth,tile),lambda i:(0,i)),full(rows,width),full(1,width),full(experts,rows)]+[ANY]*len(deps),
        out_specs=(full(rows,width),full(rows+experts,width)),
        compiler_params=params(), name="project_out", cost_estimate=cost(10),
    )(mix,w,x,gain[None],plan,*deps)

def turned_kernel(parts, count, *refs):
    w_ref=refs[parts]; out_ref=refs[parts+1+count]
    start=0; total=None
    for x_ref in refs[:parts]:
        stop=start+x_ref.shape[1]
        term=mm(x_ref[...],w_ref[:,start:stop],NT)
        total=term if total is None else total+term
        start=stop
    out_ref[...]=total.astype(out_ref.dtype)

def times_turned(xs, w, dtype, tile=512, deps=()):
    rows=xs[0].shape[0]; cols,depth=w.shape
    tile=min(tile,cols)
    return pl.pallas_call(functools.partial(turned_kernel,len(xs),len(deps)),
        out_shape=jax.ShapeDtypeStruct((rows,cols),dtype),
        grid=(cols//tile,),
        in_specs=[pl.BlockSpec(x.shape,lambda i:(0,0)) for x in xs]+[pl.BlockSpec((tile,depth),lambda i:(i,0))]+[ANY]*len(deps),
        out_specs=pl.BlockSpec((rows,tile),lambda i:(0,i)),
        compiler_params=params(), name="times_turned", cost_estimate=cost(11),
    )(*xs,w,*deps)

def hold(value, *deps):
    return pl.pallas_call(lambda *refs: None,
        out_shape=jax.ShapeDtypeStruct(value.shape,value.dtype),
        in_specs=[ANY]*(1+len(deps)), out_specs=ANY, input_output_aliases={0:0},
        name="hold", cost_estimate=cost(0.1),
    )(value,*deps)

TN=(((0,),(0,)),((),()))
UNCHOSEN=1024.0

def pack_kernel(count, gate_ref, up_ref, down_ref, *refs):
    out_ref=refs[count]
    ff=gate_ref.shape[1]
    out_ref[:,:ff]=gate_ref[...]
    out_ref[:,ff:2*ff]=up_ref[...]
    out_ref[:,2*ff:]=down_ref[...].T

def pack_weights(gate, up, down, which, deps=()):
    rows,ff=gate.shape[1:]
    return pl.pallas_call(functools.partial(pack_kernel,len(deps)),
        out_shape=jax.ShapeDtypeStruct((rows,3*ff),bf16),
        grid=(1,),
        in_specs=[pl.BlockSpec((pl.squeezed,rows,ff),lambda i:(which,0,0))]*2+[pl.BlockSpec((pl.squeezed,ff,rows),lambda i:(which,0,0))]+[ANY]*len(deps),
        out_specs=pl.BlockSpec((rows,3*ff),lambda i:(0,0)),
        compiler_params=params(), name="pack_weights",
        cost_estimate=cost(3),
    )(gate,up,down,*deps)

def expert_kernel(capacity, blocks, chained, pieces, count, *refs):
    mine_ref,place_ref=refs[:2]; refs=refs[2:]
    x_refs,c_refs,plan_refs=refs[:blocks],refs[blocks:2*blocks],refs[2*blocks:3*blocks]; refs=refs[3*blocks:]
    prev_out=prev_back=(None,)*blocks
    if chained:
        prev_out,prev_back=refs[:blocks],refs[blocks:2*blocks]; refs=refs[2*blocks:]
    router_ref=refs[0]; weight_refs=refs[1:1+pieces]; refs=refs[1+pieces+count:]
    rows_ref,pair_ref,hid_ref,dgate_ref,dup_ref=refs[:5]; refs=refs[5:]
    out_refs,back_refs=refs[:blocks],refs[blocks:2*blocks]
    kept_ref,sems=refs[2*blocks:]
    experts,tokens=plan_refs[0].shape
    ff=hid_ref.shape[1]
    copies=[[] for _ in range(3)]
    for i in range(3):
        for j,piece in enumerate(weight_refs):
            tall=piece.shape[0]
            spot=pl.ds(pl.multiple_of(place_ref[j],tall),tall)
            copies[i].append(pltpu.make_async_copy(piece.at[:,i*ff:(i+1)*ff],kept_ref.at[i,spot],sems.at[i,j]))
            copies[i][-1].start()
    def ready(i):
        for copy in copies[i]:
            copy.wait()
    hit=lax.broadcasted_iota(jnp.int32,(experts,tokens),0)==mine_ref[0]
    slot_of=lax.broadcasted_iota(jnp.int32,(capacity,tokens),0)
    picks=[];rows=[];cots=[];weights=[]
    for b in range(blocks):
        plan=plan_refs[b][...].astype(f32)
        logits=mm(router_ref[...],x_refs[b][...],NT)
        logits=jnp.where(plan<UNCHOSEN,logits,masked_score)
        e=jnp.exp(logits-jnp.max(logits,0,keepdims=True))
        gates=e/jnp.sum(e,0,keepdims=True)
        slot=jnp.sum(jnp.where(hit,plan,0.0),0,keepdims=True).astype(jnp.int32)
        gate=jnp.sum(jnp.where(hit,gates,0.0),0,keepdims=True)
        on=slot_of==slot
        weights.append(jnp.sum(jnp.where(on,gate,0.0),1,keepdims=True))
        picks.append(jnp.where(on,1.0,0.0).astype(bf16))
        rows.append(mm(picks[b],x_refs[b][...]).astype(bf16))
        cots.append(mm(picks[b],c_refs[b][...]))
    rows=jnp.concatenate(rows,0); cots=jnp.concatenate(cots,0); weights=jnp.concatenate(weights,0)
    rows_ref[...]=rows
    pair=(weights*cots).astype(bf16)
    pair_ref[...]=pair
    ready(0)
    gate_pre=mm(rows,kept_ref[0])
    ready(1)
    up_pre=mm(rows,kept_ref[1])
    sig=jax.nn.sigmoid(gate_pre)
    act=gate_pre*sig
    hidden=(act*up_pre).astype(bf16)
    hid_ref[...]=hidden
    ready(2)
    hidden_grad=mm(pair,kept_ref[2])
    dgate=(hidden_grad*up_pre*sig*(1.0+gate_pre*(1.0-sig))).astype(bf16)
    dup=(hidden_grad*act).astype(bf16)
    dgate_ref[...]=dgate; dup_ref[...]=dup
    back=(mm(dgate,kept_ref[0],NT)+mm(dup,kept_ref[1],NT)).astype(bf16)
    out=mm(hidden,kept_ref[2],NT)
    gate_grad=jnp.sum(out*cots,1,keepdims=True)
    out=(out*weights).astype(bf16)
    for b in range(blocks):
        part=slice(b*capacity,(b+1)*capacity)
        for prev,ref,vals in ((prev_back[b],back_refs[b],back),(prev_out[b],out_refs[b],out)):
            total=mm(picks[b],vals[part],TN)
            if chained:
                total+=prev[:tokens].astype(f32)
            ref[:tokens]=total.astype(bf16)
        grad=jnp.sum(jnp.where(picks[b]>0,gate_grad[part],0.0),0,keepdims=True)
        grad=jnp.where(hit,grad,0.0)
        high=grad.astype(bf16).astype(f32)
        back_refs[b][tokens:]=jnp.zeros((experts,back_refs[b].shape[1]),bf16)
        for i,digit in enumerate((high,grad-high)):
            spot=slice(i*tokens,(i+1)*tokens)
            if chained:
                digit+=prev_back[b][tokens:,spot].astype(f32)
            back_refs[b][tokens:,spot]=digit.astype(bf16)

def expert_chunk(mine, xs, cs, router, pieces, places, capacity, prev=None, deps=()):
    blocks=len(xs); tokens,width=cs[0].shape; ff=pieces[0].shape[1]//3; experts=router.shape[0]
    rows=blocks*capacity
    full=lambda *shape: pl.BlockSpec(shape,lambda i:(0,)*len(shape))
    once=lambda *shape: pl.BlockSpec(shape,lambda i:(0,)*len(shape),pipeline_mode=pl.Buffered(1))
    partial=[jax.ShapeDtypeStruct((tokens,width),bf16)]*blocks
    res=pl.pallas_call(functools.partial(expert_kernel,capacity,blocks,prev is not None,len(pieces),len(deps)),
        out_shape=[jax.ShapeDtypeStruct((rows,width),bf16)]*2+[jax.ShapeDtypeStruct((rows,ff),bf16)]*3
          +partial+[jax.ShapeDtypeStruct((tokens+experts,width),bf16)]*blocks,
        grid=(1,),
        in_specs=[pl.BlockSpec(memory_space=pltpu.SMEM)]*2+[once(tokens,width)]*(2*blocks)
          +[pl.BlockSpec((experts,tokens),lambda i:(tokens//experts,0),pipeline_mode=pl.Buffered(1))]*blocks
          +([once(tokens,width)]*blocks+[once(tokens+experts,width)]*blocks if prev else [])+[once(experts,width)]+[ANY]*(len(pieces)+len(deps)),
        out_specs=[once(rows,width)]*2+[once(rows,ff)]*3+[once(tokens,width)]*blocks+[once(tokens+experts,width)]*blocks,
        scratch_shapes=[pltpu.VMEM((3,width,ff),bf16),pltpu.SemaphoreType.DMA((3,len(pieces)))],
        compiler_params=params(), name="expert_chunk",
        cost_estimate=cost(4+4.7*blocks),
    )(mine,places,*xs,*cs,*xs,*(tuple(prev[0])+tuple(prev[1]) if prev else ()),router,*pieces,*deps)
    return res[:5],res[5:5+blocks],res[5+blocks:]

def expert_grads_kernel(chunks, chained, count, *refs):
    join=lambda i: jnp.concatenate([r[...] for r in refs[i*chunks:(i+1)*chunks]],0)
    rows,pair,hid,dgate,dup=[join(i) for i in range(5)]
    out_ref=refs[5*chunks+chained+count]
    def put(spot, value):
        if chained:
            value+=refs[5*chunks][:,spot].astype(f32)
        out_ref[:,spot]=value.astype(bf16)
    ff=hid.shape[1]
    rows=rows.T; pair=pair.T
    put(slice(0,ff),mm(rows,dgate))
    put(slice(ff,2*ff),mm(rows,dup))
    put(slice(2*ff,3*ff),mm(pair,hid))

def expert_grads(acts, prev=None, tile=512, deps=()):
    chunks=len(acts); width=acts[0][0].shape[1]; ff=acts[0][2].shape[1]
    count=sum(a[0].shape[0] for a in acts)
    tall=[pl.BlockSpec((a[0].shape[0],tile),lambda i:(0,i)) for a in acts]
    flat=[pl.BlockSpec((a[0].shape[0],ff),lambda i:(0,0)) for a in acts]
    known=() if prev is None else (prev,)
    part=pl.BlockSpec((tile,3*ff),lambda i:(i,0))
    return pl.pallas_call(functools.partial(expert_grads_kernel,chunks,len(known),len(deps)),
        out_shape=jax.ShapeDtypeStruct((width,3*ff),bf16),
        grid=(width//tile,),
        in_specs=tall*2+flat*3+[part]*len(known)+[ANY]*len(deps),
        out_specs=pl.BlockSpec((tile,3*ff),lambda i:(i,0)),
        compiler_params=params(), name="expert_grads",
        cost_estimate=cost(16),
    )(*[a[i] for i in range(5) for a in acts],*known,*deps)


def pooled_kernel(rows, parts, count, *refs):
    core_ref=refs[0]; left=jnp.concatenate([refs[1][...],refs[2][...]],0)
    rights=refs[3:3+2*parts]; out_ref,turned_ref=refs[3+2*parts+count:]
    turned_ref[...]=left.T.reshape(turned_ref.shape)
    pairs=turned_ref.shape[0]//2
    kept=jnp.concatenate([turned_ref[2*i+core_ref[0]] for i in range(pairs)],0)
    start=0
    for p in range(parts):
        right=jnp.concatenate([rights[p][...],rights[parts+p][...]],0)
        out_ref[:,start:start+right.shape[1]]=mm(kept,right).astype(bf16)
        start+=right.shape[1]

def pooled_grad(core, left, left_other, rights, rights_other, rows, tile=512, deps=()):
    tokens,depth=left.shape; parts=len(rights); cols=sum(r.shape[1] for r in rights)
    tile=max(min(tile,depth),2*rows)
    full=[pl.BlockSpec(r.shape,lambda i:(0,0)) for r in rights]
    return pl.pallas_call(functools.partial(pooled_kernel,rows,parts,len(deps)),
        out_shape=jax.ShapeDtypeStruct((depth//2,cols),bf16),
        grid=(depth//tile,),
        in_specs=[pl.BlockSpec(memory_space=pltpu.SMEM)]+[pl.BlockSpec((tokens,tile),lambda i:(0,i))]*2+full*2+[ANY]*len(deps),
        out_specs=pl.BlockSpec((tile//2,cols),lambda i:(i,0)),
        scratch_shapes=[pltpu.VMEM((tile//rows,rows,2*tokens),bf16)],
        compiler_params=params(), name="pooled_grad", cost_estimate=cost(9*depth*cols/8e6),
    )(core,left,left_other,*rights,*rights_other,*deps)


def rows_back_kernel(count, mine_ref, other_ref, moving_ref, middle_ref, gain_ref, sent_ref, router_ref, cot_ref, *refs):
    grad_ref,branch_ref,router_grad_ref,gain_grad_ref=refs[count:]
    tokens=middle_ref.shape[0]
    total=mine_ref[...].astype(f32)+other_ref[...].astype(f32)+moving_ref[...].astype(f32)
    gate_grad=total[tokens:,:tokens]+total[tokens:,tokens:2*tokens]
    rows=sent_ref[:tokens]; router=router_ref[...]
    logits=mm(router,rows,NT)
    logits=jnp.where(sent_ref[tokens:,:tokens].astype(f32)<UNCHOSEN,logits,masked_score)
    e=jnp.exp(logits-jnp.max(logits,0,keepdims=True))
    gates=e/jnp.sum(e,0,keepdims=True)
    logit_grad=(gates*(gate_grad-jnp.sum(gates*gate_grad,0,keepdims=True))).astype(bf16)
    router_grad_ref[...]=mm(logit_grad,rows)
    grad=total[:tokens]+mm(logit_grad,router,TN)
    v=middle_ref[...]
    r=lax.rsqrt(jnp.mean(v*v,-1,keepdims=True)+norm_eps)
    n=v*r
    gain_grad_ref[...]=jnp.sum(grad*n,0,keepdims=True)
    g=grad*gain_ref[...]
    out=cot_ref[...].astype(f32)+r*(g-n*jnp.mean(g*n,-1,keepdims=True))
    grad_ref[...]=out
    branch_ref[...]=out.astype(bf16)

def rows_back(mine, other, moving, middle, gain, sent, router, cot, deps=()):
    tokens,width=middle.shape; experts=router.shape[0]
    full=lambda *a: pl.BlockSpec(a,lambda i:(0,0))
    tall=full(tokens+experts,width); flat=full(tokens,width)
    return pl.pallas_call(functools.partial(rows_back_kernel,len(deps)),
        out_shape=(jax.ShapeDtypeStruct((tokens,width),f32),jax.ShapeDtypeStruct((tokens,width),bf16),
                   jax.ShapeDtypeStruct((experts,width),f32),jax.ShapeDtypeStruct((1,width),f32)),
        grid=(1,),
        in_specs=[tall,tall,tall,flat,full(1,width),tall,full(experts,width),flat]+[ANY]*len(deps),
        out_specs=(flat,flat,full(experts,width),full(1,width)),
        compiler_params=params(), name="rows_back", cost_estimate=cost(6),
    )(mine,other,moving,middle,gain[None],sent,router,cot,*deps)


def unpack_kernel(count, extra, *refs):
    gate_ref,up_ref,down_ref=refs[count+extra:]
    ff=gate_ref.shape[2]
    for e in range(count):
        gate_ref[e]=refs[e][:,:ff].astype(f32)
        up_ref[e]=refs[e][:,ff:2*ff].astype(f32)
        down_ref[e]=refs[e][:,2*ff:].astype(f32).T

def unpack_grads(lows, deps=()):
    count=len(lows); rows,ff=lows[0].shape[0],lows[0].shape[1]//3
    full=lambda *a: pl.BlockSpec(a,lambda i:(0,)*len(a),pipeline_mode=pl.Buffered(1))
    return pl.pallas_call(functools.partial(unpack_kernel,count,len(deps)),
        out_shape=(jax.ShapeDtypeStruct((count,rows,ff),f32),)*2+(jax.ShapeDtypeStruct((count,ff,rows),f32),),
        grid=(1,),
        in_specs=[full(rows,3*ff)]*count+[ANY]*len(deps),
        out_specs=(full(count,rows,ff),)*2+(full(count,ff,rows),),
        compiler_params=params(), name="unpack_grads", cost_estimate=cost(7),
    )(*lows,*deps)

ALL=("dp","context","experts")


def by_chips(array, step):
    axes=("context","experts")
    length=lax.axis_size(axes)
    return lax.ppermute(array,axes,[(i,i+2*step) for i in range(length) if 0<=i+2*step<length])


def after(value, *others):
    return lax.optimization_barrier((value,)+others)[0]


def swap_cores(array):
    return lax.ppermute(array,"experts",[(i,i^1) for i in range(lax.axis_size("experts"))])


def chip_order():
    chips=lax.axis_size("experts")//2
    return list(range(0,chips,2))+list(range(1,chips,2))[::-1]


def next_chip(array):
    order=chip_order(); chips=len(order)
    return lax.ppermute(array,"experts",[(2*order[i]+c,2*order[(i+1)%chips]+c) for i in range(chips) for c in range(2)])


def gather_ring(array):
    lanes=[array]
    for _ in range(len(chip_order())-1):
        lanes.append(next_chip(lanes[-1]))
    return [(lane,swap_cores(lane)) for lane in lanes]


def ring_step(part, moving=None, holds=()):
    mine,other=part
    if moving is not None:
        other=hold(other,moving,*holds)
    total=mine.astype(f32)+swap_cores(other).astype(f32)
    return total if moving is None else total+moving.astype(f32)


def sum_everywhere(array):
    for axis in ALL:
        length=lax.axis_size(axis); step=1
        while step<length:
            array=array+lax.ppermute(array,axis,[(i,i^step) for i in range(length)])
            step*=2
    return array


def rms_scale(values, norm_gain):
    return values*lax.rsqrt(jnp.mean(values*values,axis=-1,keepdims=True)+norm_eps)*norm_gain


def rope_rows(positions, head_width):
    frequencies=jnp.power(1000000.0,-jnp.arange(0,head_width,2).astype(f32)/head_width)
    angles=positions.astype(f32)[:,None]*frequencies[None,:]
    cosine,sine=jnp.cos(angles),jnp.sin(angles)
    return jnp.concatenate([cosine,cosine],1),jnp.concatenate([-sine,sine],1)


def slot_plan(ids, order, experts):
    tokens,top=ids.shape
    count=tokens*top
    place=jnp.arange(count,dtype=jnp.int32)
    owner=(order[None,:]//top==jnp.arange(tokens,dtype=jnp.int32)[:,None]).astype(bf16)
    choice=order[:,None]%top==jnp.arange(top,dtype=jnp.int32)[None,:]
    digits=jnp.concatenate([jnp.where(choice,(place//64)[:,None],0),jnp.where(choice,(place%64)[:,None],0)],1).astype(bf16)
    found=mm(owner,digits)
    found=64.0*found[:,:top]+found[:,top:]
    chosen=ids.T[None]==jnp.arange(experts,dtype=jnp.int32)[:,None,None]
    spot=jnp.sum(jnp.where(chosen,found.T[None],0.0),1)
    picked=jnp.any(chosen,1)
    spot=jnp.where(picked,spot,float(count))
    earlier=jnp.sum((spot[:,:,None]<spot[:,None,:]).astype(f32),1)
    return jnp.where(picked,earlier,float(UNCHOSEN))


def chip_back(step):
    chips=lax.axis_size("experts")//2
    chip=lax.axis_index("experts")//2
    spot=jnp.where(chip%2==0,chip//2,chips-1-chip//2)
    spot=lax.rem(spot-step+chips,chips)
    return jnp.where(spot<(chips+1)//2,2*spot,2*(chips-1-spot)+1)


def ring_rows(parts, holds=()):
    chips=len(chip_order())
    moving=[]
    for step in list(range(1,chips))+[0]:
        total=lax.dynamic_index_in_dim(parts,chip_back(step),1,False).astype(f32)
        if moving:
            total=total+moving[-1].astype(f32)
        if step==0:
            return total,moving
        total=total.astype(bf16)
        if len(holds)>=len(moving)>0:
            total=hold(total,holds[len(moving)-1])
        moving.append(next_chip(total))


def shards(hidden_in, segments, expert_ids, placement_order, out_grad, attention_gain, query_weight, key_matrix, value_matrix,
           query_gain, key_gain, out_weight, feedforward_gain, router_weight, gate_weight, up_weight, down_weight):
    tok_rows,model_width=hidden_in.shape[1:]
    head_dim=query_gain.shape[0]
    kv_width=key_matrix.shape[1]
    kv_heads=kv_width//head_dim
    top_count=expert_ids.shape[2]
    local_experts=gate_weight.shape[0]
    all_experts=local_experts*lax.axis_size("experts")
    capacity=tok_rows*top_count//all_experts
    reach=WINDOW//tok_rows
    seq_axes=("context","experts")
    seq_place=lax.axis_index(seq_axes)
    devices=math.prod(lax.axis_size(a) for a in ALL)
    expert_place=lax.axis_index("experts")

    before=()
    packed=[pack_weights(gate_weight,up_weight,down_weight,0)]
    cot_lanes=[out_grad[0],next_chip(out_grad[0])]

    positions=seq_place*tok_rows+jnp.arange(tok_rows,dtype=jnp.int32)
    cos_rows,sin_rows=rope_rows(positions,head_dim)
    attention_input,key_pre,kv=key_value(hidden_in[0],attention_gain,key_matrix,value_matrix,key_gain,cos_rows,sin_rows,deps=(packed[0],))
    for expert in range(1,local_experts):
        packed.append(pack_weights(gate_weight,up_weight,down_weight,expert,deps=(kv,packed[-1])))
    weights=[lax.all_gather(p,("dp","context"),axis=0,tiled=True) for p in packed]
    pieces=[([w],jnp.zeros((1,),jnp.int32)) for w in weights]
    plan=slot_plan(expert_ids[0],placement_order[0,0],all_experts)

    lower=expert_place%2==0
    lane=[kv]
    query_pre,query_rows=project_heads(attention_input,query_weight,query_gain,cos_rows,sin_rows,deps=(packed[-1],))
    for step in range(reach//2):
        lane.append(by_chips(hold(lane[-1],query_rows) if step==1 else lane[-1],1))
    cot_lanes[1]=hold(cot_lanes[1],lane[-1])
    for _ in range(len(chip_order())-2):
        cot_lanes.append(next_chip(cot_lanes[-1]))
    cots=[(c,swap_cores(c)) for c in cot_lanes]
    kvs=[lane[0]]
    for near,far in zip(lane[:-1],lane[1:]):
        kvs+=[swap_cores(jnp.where(lower,near,far)),far]
    seg_row=segments[0]
    seg_padded=jnp.concatenate([jnp.full((reach*tok_rows,),-1,jnp.int32),seg_row],0)
    key_segs=lax.dynamic_slice_in_dim(seg_padded,seq_place*tok_rows,(reach+1)*tok_rows,0).reshape(reach+1,tok_rows)[::-1]
    query_segs=key_segs[0]
    attn_mix,inverse=attend(query_rows,kvs,query_segs,key_segs,kv_heads,head_dim)
    middle,sent=project_out(attn_mix,out_weight,hidden_in[0],feedforward_gain,plan.astype(bf16),deps=(cots[2][0],))
    sent=hold(sent,cots[3][0])
    router_rows=router_weight.T
    chips=len(cots)
    steps=list(range(chips))
    ffn_blocks=[(sent,swap_cores(sent))]
    acts=[[] for _ in range(local_experts)]
    out_parts=[{} for _ in range(local_experts)]; back_parts=[{} for _ in range(local_experts)]
    expert_full=[None]*local_experts
    summed=[0]*local_experts
    before=(middle,)
    def run(expert, some, *deps):
        nonlocal before
        blocks=[(2*s+i) for s in some for i in range(2)]
        xs=[ffn_blocks[s][i] for s in some for i in range(2)]
        cs=[cots[s][i] for s in some for i in range(2)]
        known=([out_parts[expert-1][k] for k in blocks],[back_parts[expert-1][k] for k in blocks]) if expert else None
        which=(expert_place*local_experts+expert).astype(jnp.int32)[None]
        act,outs,backs=expert_chunk(which,xs,cs,router_rows,*pieces[expert][:2],capacity,known,deps=before+deps)
        acts[expert].append(act)
        out_parts[expert].update(zip(blocks,outs)); back_parts[expert].update(zip(blocks,backs))
        before=(act[4],)
    def grads(expert, *deps):
        nonlocal before
        expert_full[expert]=expert_grads(acts[expert][summed[expert]:],expert_full[expert],deps=before+deps)
        summed[expert]=len(acts[expert])
        before=(expert_full[expert],)
    def part(parts, s):
        return parts[-1][2*s],parts[-1][2*s+1]
    coming=next_chip(sent)
    for s in steps:
        run(0,[s],)
        if s+1<chips:
            coming=hold(coming,*before)
            ffn_blocks.append((coming,swap_cores(coming)))
            if s+2<chips:
                coming=next_chip(coming)
    for expert in range(1,local_experts-1):
        grads(expert-1)
        run(expert,steps[:chips//2]); run(expert,steps[chips//2:])
    last=local_experts-1
    grads(last-1)
    run(last,steps[1:2])
    total=ring_step(part(back_parts,1)).astype(bf16)
    moving=next_chip(total)
    for s in steps[2:]:
        run(last,[s],total)
        if s==2:
            run(last,steps[:1])
            total=ring_step(part(back_parts,s),moving,before).astype(bf16)
            moving=next_chip(total)
            grads(last,total)
            continue
        total=ring_step(part(back_parts,s),moving,before).astype(bf16)
        moving=next_chip(total)
    grads(last,total)
    moving=hold(moving,*before)
    mine,other=part(back_parts,0)
    total=hold(ring_step(part(out_parts,1)).astype(bf16),moving)
    out_moving=next_chip(total)
    middle_grad,branch_grad,router_grad,ffn_gain_grad=rows_back(mine,swap_cores(other),moving,middle,feedforward_gain,sent,router_rows,out_grad[0])
    router_grad=router_grad.T
    mix_grad=times_turned([branch_grad],out_weight,bf16,deps=before)
    out_moving=hold(out_moving,mix_grad)

    ff=gate_weight.shape[2]
    expert_low=[lax.psum_scatter(a,("dp","context"),scatter_dimension=0,tiled=True) for a in expert_full]
    core=expert_place%2
    core_ref=core.astype(jnp.int32)[None]
    out_part=pooled_grad(core_ref,attn_mix,swap_cores(attn_mix),[branch_grad],[swap_cores(branch_grad)],out_weight.shape[0]//devices,deps=(mix_grad,out_moving))
    out_low=lax.psum_scatter(out_part,("dp","context"),scatter_dimension=0,tiled=True)

    halves=2 if kv_heads%2==0 else 1
    count=kv_heads//halves
    query_parts,gain_parts,key_grads,value_grads=[],[],[],[]
    before=(out_part,expert_low[0])
    last_kernel=(out_part,)
    for half in range(halves):
        query_part,gain_part,key_parts,value_parts=attend_back(query_rows,kvs,query_segs,key_segs,mix_grad,attn_mix,inverse,query_pre,
            query_gain,cos_rows,sin_rows,kv_heads,head_dim,half*count,count,deps=before)
        query_parts.append(query_part); gain_parts.append(gain_part)
        key_grads.append(key_parts); value_grads.append(value_parts)
        before=(query_part,)
        if half+2<chips:
            total=hold(ring_step(part(out_parts,half+2),out_moving).astype(bf16),*last_kernel)
            out_moving=hold(next_chip(total),query_part)
            before+=(out_moving,)
        last_kernel=(query_part,)
    query_both=[swap_cores(q) for q in query_parts]
    input_other=swap_cores(attention_input)
    query_sum=pooled_grad(core_ref,attention_input,input_other,query_parts,query_both,model_width//devices,deps=before+(expert_low[-1],))
    query_low=lax.psum_scatter(query_sum,("dp","context"),scatter_dimension=0,tiled=True)

    window=[jnp.concatenate([k[d] for k in key_grads]+[v[d] for v in value_grads],1) for d in range(reach+1)]
    lanes=[w.astype(f32) for w in window[::2]]
    for d in range(1,reach,2):
        moved=swap_cores(window[d]).astype(f32)
        lanes[d//2]+=jnp.where(lower,moved,0.0)
        lanes[d//2+1]+=jnp.where(lower,0.0,moved)
    attn_in_part=times_turned(query_parts,query_weight,f32,deps=(query_sum,))
    carry=lanes[-1].astype(bf16)
    for own,kernel in zip(lanes[-2::-1],(query_sum,attn_in_part)):
        carry=hold(by_chips(carry,-1),kernel).astype(f32)+own
        carry=carry.astype(bf16) if own is not lanes[0] else carry
    query_gain_part=sum(gain_parts)
    value_pre_grad=carry[:,kv_width:].astype(bf16)

    key_pre_grad,key_gain_part=heads_back(carry[:,:kv_width],key_pre,key_gain,cos_rows,sin_rows,deps=(attn_in_part,))
    attn_in_grad=attn_in_part+mm(key_pre_grad,key_matrix,NT)+mm(value_pre_grad,value_matrix,NT)
    attn_unused,attn_pull=jax.vjp(rms_scale,hidden_in[0].astype(f32),attention_gain)
    x_norm_grad,attn_gain_grad=attn_pull(attn_in_grad)
    input_grad=middle_grad+x_norm_grad

    small=jnp.concatenate([g.reshape(devices,-1) for g in (router_grad,ffn_gain_grad,attn_gain_grad,query_gain_part,key_gain_part)],1)
    pairs=small.reshape(devices//2,2,-1)
    small=lax.dynamic_index_in_dim(pairs,core,1,False)+swap_cores(lax.dynamic_index_in_dim(pairs,1-core,1,False))
    kv_pre_grad=jnp.concatenate([key_pre_grad,value_pre_grad],1)
    kv_part=pooled_grad(core_ref,attention_input,input_other,[kv_pre_grad],[swap_cores(kv_pre_grad)],model_width//devices,
        deps=(attn_in_part,expert_low[-1],out_low)).reshape(devices//2,-1,2*kv_width)
    gate_weight_grad,up_weight_grad,down_weight_grad=unpack_grads(expert_low,deps=(kv_part,))
    extra=-(-small.shape[1]//(16*2*kv_width))*16
    small=jnp.pad(small.astype(bf16),((0,0),(0,extra*2*kv_width-small.shape[1]))).reshape(devices//2,extra,2*kv_width)
    out_weight_grad,out_sent=ring_rows(out_low.reshape(1,chips,-1,out_low.shape[1]))
    out_weight_grad=out_weight_grad.reshape(-1,out_low.shape[1])
    assert chips-2<=halves
    block_out=(middle+ring_step(part(out_parts,0),out_moving)).astype(bf16)
    kv_sum,_=ring_rows(jnp.concatenate([kv_part,small],1).reshape(-1,chips,kv_part.shape[1]+extra,2*kv_width))
    kv_sum=kv_sum.astype(bf16).reshape(-1,2*kv_width)
    query_weight_grad,_=ring_rows(hold(query_low,kv_sum,out_sent[-1],gate_weight_grad).reshape(1,chips,-1,query_low.shape[1]))
    query_weight_grad=query_weight_grad.reshape(-1,query_low.shape[1])
    kv_rows=lax.psum_scatter(hold(kv_sum,query_low),("dp","context"),scatter_dimension=0,tiled=True).astype(f32)
    rows=model_width//devices; few=head_dim//devices
    kv_weight_grad=kv_rows[:rows]
    small=kv_rows[rows:].reshape(-1)
    router_weight_grad=small[:rows*all_experts].reshape(rows,all_experts)
    rest=small[rows*all_experts:]

    return (block_out[None],input_grad[None],rest[rows:2*rows],query_weight_grad,kv_weight_grad[:,:kv_width],kv_weight_grad[:,kv_width:],
        rest[2*rows:2*rows+few],rest[2*rows+few:2*rows+2*few],out_weight_grad,rest[:rows],router_weight_grad,gate_weight_grad,up_weight_grad,
        down_weight_grad)


def solution(mesh):
    tokens=P("dp",("context","experts"),None)
    rows=P(ALL,None); flat=P(ALL)
    tall=P("experts",("dp","context"),None); wide=P("experts",None,("dp","context"))
    in_specs=(tokens,P("dp",None),tokens,tokens,tokens)+(P(),)*9+(tall,tall,wide)
    out_specs=(tokens,tokens,flat,rows,rows,rows,flat,flat,rows,flat,rows,tall,tall,wide)
    return jax.shard_map(shards,mesh=mesh,in_specs=in_specs,out_specs=out_specs,check_vma=False)
```
